128 devices in a mesh: ctx: 32 (over y, z_hi, x), wt: 4 (over z_lo, core).
Axes of the slice: x: 4, y: 4, z: 4 (z_hi: 2, z_lo: 2; z = z_hi * 2 + z_lo), core: 2. Of those that a mesh axis runs over, the one named last changes fastest.
Arguments:
- stream: bfloat16 [8192, 2048], P('ctx'), may hold values from -6 to 6
- layer_input: bfloat16 [8192, 256], P('ctx', 'wt'), may hold values from -6 to 6
- out_grad: bfloat16 [8192, 2048], P('ctx'), may hold values from -6 to 6
- doc_lengths: int32 [8], replicated, may hold values from 1 to 4096, 8192 in all
- stretch_slots: int32 [64], replicated, may hold values from 0 to 63, each once
- gain_input: float32 [2048], replicated, may hold values from 0.5 to 1.5
- gain_query: float32 [256], replicated, may hold values from 0.6 to 1.4
- gain_key: float32 [256], replicated, may hold values from 0.6 to 1.4
- w_query: bfloat16 [2048, 2048], P(None, 'wt'), may hold values from -0.125 to 0.125
- w_key: bfloat16 [2048, 512], P(None, 'wt'), may hold values from -0.125 to 0.125
- w_value: bfloat16 [2048, 512], P(None, 'wt'), may hold values from -0.125 to 0.125
- w_attn_out: bfloat16 [2048, 2048], P('wt'), may hold values from -0.5 to 0.5
- gain_attn: float32 [2048], replicated, may hold values from 0.5 to 1.5
- laurel_left: bfloat16 [2048, 64], P(None, 'wt'), may hold values from -0.125 to 0.125
- laurel_right: bfloat16 [64, 2048], P('wt'), may hold values from -0.75 to 0.75
- gain_laurel: float32 [2048], replicated, may hold values from 0.5 to 1.5
- gain_pre_ff: float32 [2048], replicated, may hold values from 0.5 to 1.5
- w_gate: bfloat16 [2048, 8192], P(None, 'wt'), may hold values from -0.125 to 0.125
- w_up: bfloat16 [2048, 8192], P(None, 'wt'), may hold values from -0.125 to 0.125
- w_down: bfloat16 [8192, 2048], P('wt'), may hold values from -0.0625 to 0.0625
- gain_post_ff: float32 [2048], replicated, may hold values from 0.5 to 1.5
- join_gate: bfloat16 [2048, 256], P(None, 'wt'), may hold values from -0.125 to 0.125
- join_proj: bfloat16 [256, 2048], P('wt'), may hold values from -0.375 to 0.375
- gain_join: float32 [2048], replicated, may hold values from 0.5 to 1.5
Outputs:
- layer_out: float32 [8192, 2048], P('ctx')
- stream_grad: float32 [8192, 2048], P('ctx')
- layer_input_grad: float32 [8192, 256], P('ctx', 'wt')
- grad_gain_input: float32 [2048], P('ctx')
- grad_gain_query: float32 [256], P('ctx')
- grad_gain_key: float32 [256], P('ctx')
- grad_w_query: float32 [2048, 2048], P('ctx', 'wt')
- grad_w_key: float32 [2048, 512], P('ctx', 'wt')
- grad_w_value: float32 [2048, 512], P('ctx', 'wt')
- grad_w_attn_out: float32 [2048, 2048], P('wt', 'ctx')
- grad_gain_attn: float32 [2048], P('ctx')
- grad_laurel_left: float32 [2048, 64], P('ctx', 'wt')
- grad_laurel_right: float32 [64, 2048], P('wt', 'ctx')
- grad_gain_laurel: float32 [2048], P('ctx')
- grad_gain_pre_ff: float32 [2048], P('ctx')
- grad_w_gate: float32 [2048, 8192], P('ctx', 'wt')
- grad_w_up: float32 [2048, 8192], P('ctx', 'wt')
- grad_w_down: float32 [8192, 2048], P('wt', 'ctx')
- grad_gain_post_ff: float32 [2048], P('ctx')
- grad_join_gate: float32 [2048, 256], P('ctx', 'wt')
- grad_join_proj: float32 [256, 2048], P('wt', 'ctx')
- grad_gain_join: float32 [2048], P('ctx')
The draws below stay inside these ranges and needn't reach their ends.
Inputs may be any that keep to these rules, and one draw needn't show every extreme that they name: doc_lengths sum to 8192; the longest document has exactly 4096 tokens; documents may span several stretches. stretch_slots names every stretch of the stream once.
All inputs are finite; a program needn't handle non-finite values.
Results may differ from the reference program's by a relative error of at most 0.035.
Values may be sent and summed in bfloat16 or wider, within the bound.
No kernel may reach another device: no remote copies, remote signals or barrier semaphores. Data moves between devices by JAX's collectives and lax.ppermute only.
A program may use at most 192 MiB of HBM per device.

```python
import math
import jax
import jax.numpy as jnp
import numpy as np
from jax import lax

D = 2048
HEADS = 8
KV_HEADS = 2
HEAD_DIM = 256
FF = 8192
PLE_DIM = 256
LAUREL = 64
STRETCH = 128
DOCS = 8
TOKENS = 8192
DOC_MOST = 4096
N_CTX = 32


def block_levels(stream_key, shape, split, least, high):
    gain, own = 1.0, jax.random.fold_in(stream_key, 6)
    for axis_at, blocks in split:
        steps = jnp.exp(jax.random.uniform(jax.random.fold_in(own, axis_at), (blocks,), jnp.float32, least / len(split), high / len(split)))
        gain = gain * jnp.repeat(steps, shape[axis_at] // blocks).reshape([-1 if axis == axis_at else 1 for axis in range(len(shape))])
    return gain


def split_up(count, total, limit, skew):
    loads = [(1 << 20) // math.isqrt(rank ** skew) + 1 for rank in range(2, count + 1)]
    rest, holding = total - limit - (count - 1), [1] * (count - 1)
    while rest > 0:
        candidates = [i for i in range(count - 1) if holding[i] < limit]
        pool, left = sum([loads[i] for i in candidates]), rest
        for i in candidates:
            more = min(limit - holding[i], max(1, left * loads[i] // pool), rest)
            holding[i] = holding[i] + more
            rest = rest - more
    return np.array([limit] + holding)


def uneven_parts(key, number_of, total, bound, lean):
    if number_of == 2:
        one = jax.random.randint(key, (), max(1, total - bound), min(bound, total - 1) + 1)
        return jnp.stack([one, total - one])
    tallies = jnp.asarray(split_up(number_of, total, bound, lean), jnp.int32)
    twos = (number_of - 1) // 2
    source_of, receiver = tallies[1:1 + 2 * twos:2], tallies[2:2 + 2 * twos:2]
    slack = jnp.minimum(source_of - 1, bound - receiver)
    shifted = jax.random.randint(jax.random.fold_in(key, 1), (twos,), 0, 1 << 20) % (slack + 1)
    tallies = tallies.at[1:1 + 2 * twos:2].set(source_of - shifted).at[2:2 + 2 * twos:2].set(receiver + shifted)
    return tallies[jax.random.permutation(jax.random.fold_in(key, 2), number_of)]


def noise(own_key, dims, deviation, bound, shards=(), held_as=jnp.bfloat16):
    array = jax.random.normal(own_key, dims, jnp.float32) * deviation
    if len(shards) > 0:
        array = block_levels(own_key, dims, shards, -0.22, 0.18) * array
    return jnp.clip(array, min=-bound, max=bound).astype(held_as)


def setup_inputs(seed: int = 0) -> dict:
    key_of = jax.random.split(jax.random.key(seed), 25)
    stream = noise(key_of[0], (TOKENS, D), 1.0, 6.0, ((0, 32),))
    layer_input = noise(key_of[1], (TOKENS, PLE_DIM), 1.0, 6.0, ((0, 32), (1, 4)))
    out_grad = noise(key_of[2], (TOKENS, D), 1.0, 6.0, ((0, 32),))
    doc_lengths = uneven_parts(key_of[3], DOCS, TOKENS, DOC_MOST, 2).astype(jnp.int32)
    stretch_slots = jax.random.permutation(key_of[4], 2 * N_CTX).astype(jnp.int32)
    gain_input = jnp.clip(1.0 + 0.1 * jax.random.normal(key_of[5], (D,), jnp.float32), 0.5, 1.5)
    gain_query = jnp.clip(jax.random.uniform(key_of[6], (HEAD_DIM,), jnp.float32, 0.6, 1.4), 0.6, 1.4)
    gain_key = jnp.clip(jax.random.uniform(key_of[7], (HEAD_DIM,), jnp.float32, 0.6, 1.4), 0.6, 1.4)
    w_query = noise(key_of[8], (D, HEADS * HEAD_DIM), D ** -0.5, 0.125, ((1, 4),))
    w_key = noise(key_of[9], (D, KV_HEADS * HEAD_DIM), D ** -0.5, 0.125, ((1, 4),))
    w_value = noise(key_of[10], (D, KV_HEADS * HEAD_DIM), D ** -0.5, 0.125, ((1, 4),))
    w_attn_out = noise(key_of[11], (HEADS * HEAD_DIM, D), (HEADS * HEAD_DIM // 16) ** -0.5, 0.5, ((0, 4),))
    gain_attn = jnp.clip(1.0 + 0.1 * jax.random.normal(key_of[12], (D,), jnp.float32), 0.5, 1.5)
    laurel_left = noise(key_of[13], (D, LAUREL), D ** -0.5, 0.125, ((1, 4),))
    laurel_right = noise(key_of[14], (LAUREL, D), LAUREL ** -0.5, 0.75, ((0, 4),))
    gain_laurel = jnp.clip(jax.random.uniform(key_of[15], (D,), jnp.float32, 0.5, 1.5), 0.5, 1.5)
    gain_pre_ff = jnp.clip(1.0 + 0.1 * jax.random.normal(key_of[16], (D,), jnp.float32), 0.5, 1.5)
    w_gate = noise(key_of[17], (D, FF), D ** -0.5, 0.125, ((1, 4),))
    w_up = noise(key_of[18], (D, FF), D ** -0.5, 0.125, ((1, 4),))
    w_down = noise(key_of[19], (FF, D), FF ** -0.5, 0.0625, ((0, 4),))
    gain_post_ff = jnp.clip(1.0 + 0.1 * jax.random.normal(key_of[20], (D,), jnp.float32), 0.5, 1.5)
    join_gate = noise(key_of[21], (D, PLE_DIM), D ** -0.5, 0.125, ((1, 4),))
    join_proj = noise(key_of[22], (PLE_DIM, D), PLE_DIM ** -0.5, 0.375, ((0, 4),))
    gain_join = jnp.clip(jax.random.uniform(key_of[23], (D,), jnp.float32, 0.5, 1.5), 0.5, 1.5)
    return {"stream": stream, "layer_input": layer_input, "out_grad": out_grad, "doc_lengths": doc_lengths, "stretch_slots": stretch_slots, "gain_input": gain_input, "gain_query": gain_query, "gain_key": gain_key, "w_query": w_query, "w_key": w_key, "w_value": w_value, "w_attn_out": w_attn_out, "gain_attn": gain_attn, "laurel_left": laurel_left, "laurel_right": laurel_right, "gain_laurel": gain_laurel, "gain_pre_ff": gain_pre_ff, "w_gate": w_gate, "w_up": w_up, "w_down": w_down, "gain_post_ff": gain_post_ff, "join_gate": join_gate, "join_proj": join_proj, "gain_join": gain_join}


epsilon = 1e-06
rope_base = 1000000.0
root_half = 0.7071067811865476
neg_big = -1e+30
highest = lax.Precision.HIGHEST

@jax.custom_vjp
def low(v):
    return lax.optimization_barrier(v.astype(jnp.bfloat16)).astype(jnp.float32)

@jax.custom_vjp
def low_back(v):
    return v

def low_keep(v):
    return (low(v), None)

def low_pass(kept, grad):
    return (grad,)

def back_keep(v):
    return (v, None)

def back_low(kept, grad):
    return (low(grad),)
low.defvjp(low_keep, low_pass)
low_back.defvjp(back_keep, back_low)

def matmul(left_side, right_side):
    return jnp.dot(left_side, right_side, precision=highest, preferred_element_type=jnp.float32)

def norm_gain(values, scales):
    return values * lax.rsqrt(lax.optimization_barrier(jnp.mean(values * values, axis=-1, keepdims=True)) + epsilon) * scales

def norm_plain(values):
    return values * lax.rsqrt(lax.optimization_barrier(jnp.mean(values * values, axis=-1, keepdims=True)) + epsilon)

def frequencies(head_dim):
    half_dim = head_dim // 2
    return 1.0 / rope_base ** (jnp.arange(half_dim, dtype=jnp.float32) * (2.0 / head_dim))

def rotate(values, cosine, sine_term):
    half_dim = values.shape[-1] // 2
    front_half = values[..., :half_dim]
    back_half = values[..., half_dim:]
    return jnp.concatenate([front_half * cosine - back_half * sine_term, back_half * cosine + front_half * sine_term], axis=-1)

def attend(queries, keys, values, segments):
    block_len = math.gcd(TOKENS, 512)
    span_len = min(TOKENS, DOC_MOST + block_len)
    group_len = HEADS // KV_HEADS
    score_scale = HEAD_DIM ** (-0.5)

    def one_block(block_no):
        query_start = (block_no * block_len).astype(jnp.int32)
        key_start = jnp.clip(query_start + block_len - span_len, 0, TOKENS - span_len).astype(jnp.int32)
        query_blk = lax.dynamic_slice_in_dim(queries, query_start, block_len, 0).reshape(block_len, KV_HEADS, group_len, HEAD_DIM)
        key_blk = lax.dynamic_slice_in_dim(keys, key_start, span_len, 0)
        value_blk = lax.dynamic_slice_in_dim(values, key_start, span_len, 0)
        query_pos = query_start + jnp.arange(block_len, dtype=jnp.int32)
        key_pos = key_start + jnp.arange(span_len, dtype=jnp.int32)
        query_seg = lax.dynamic_slice_in_dim(segments, query_start, block_len, 0)
        key_seg = lax.dynamic_slice_in_dim(segments, key_start, span_len, 0)
        allowed = (key_pos[None, :] <= query_pos[:, None]) & (key_seg[None, :] == query_seg[:, None])
        scores = jnp.einsum('qgxd,kgd->gxqk', query_blk, key_blk, precision=highest) * score_scale
        scores = jnp.where(allowed[None, None], low_back(scores), neg_big)
        attn_probs = low(jax.nn.softmax(scores, axis=-1))
        weighted = jnp.einsum('gxqk,kgd->qgxd', attn_probs, value_blk, precision=highest)
        return weighted.reshape(block_len, HEADS, HEAD_DIM)
    blocks = lax.map(jax.checkpoint(one_block), jnp.arange(TOKENS // block_len, dtype=jnp.int32))
    return blocks.reshape(TOKENS, HEADS, HEAD_DIM)

def reference(stream, layer_input, out_grad, doc_lengths, stretch_slots, gain_input, gain_query, gain_key, w_query, w_key, w_value, w_attn_out, gain_attn, laurel_left, laurel_right, gain_laurel, gain_pre_ff, w_gate, w_up, w_down, gain_post_ff, join_gate, join_proj, gain_join):
    row_ids = jnp.arange(TOKENS, dtype=jnp.int32)
    slot_ids = row_ids // STRETCH
    offsets = row_ids % STRETCH
    positions = (stretch_slots[slot_ids] * STRETCH + offsets).astype(jnp.int32)
    slot_of = jnp.zeros((2 * N_CTX,), jnp.int32).at[stretch_slots].set(jnp.arange(2 * N_CTX, dtype=jnp.int32))
    order = (slot_of[slot_ids] * STRETCH + offsets).astype(jnp.int32)
    doc_ends = jnp.cumsum(doc_lengths).astype(jnp.int32)
    stream_segments = lax.optimization_barrier(jnp.sum((doc_ends[None, :] <= row_ids[:, None]).astype(jnp.int32), axis=1)).astype(jnp.int32)
    angles = positions.astype(jnp.float32)[:, None] * frequencies(HEAD_DIM)[None, :]
    cosine = jnp.cos(angles)
    sine_term = jnp.sin(angles)

    def forward(stream_f, input_f, gain_input, gain_query, gain_key, w_query, w_key, w_value, w_attn_out, gain_attn, laurel_left, laurel_right, gain_laurel, gain_pre_ff, w_gate, w_up, w_down, gain_post_ff, join_gate, join_proj, gain_join):
        normed = norm_gain(stream_f, gain_input)
        normed_b = low(normed)
        query_raw = low_back(matmul(normed_b, w_query)).reshape(TOKENS, HEADS, HEAD_DIM)
        key_raw = low_back(matmul(normed_b, w_key)).reshape(TOKENS, KV_HEADS, HEAD_DIM)
        value_raw = low_back(matmul(normed_b, w_value)).reshape(TOKENS, KV_HEADS, HEAD_DIM)
        query_rot = low(rotate(norm_gain(query_raw, gain_query), cosine[:, None, :], sine_term[:, None, :]))
        key_rot = low(rotate(norm_gain(key_raw, gain_key), cosine[:, None, :], sine_term[:, None, :]))
        value_norm = low(norm_plain(value_raw))
        heads_out = attend(jnp.take(query_rot, order, axis=0), jnp.take(key_rot, order, axis=0), jnp.take(value_norm, order, axis=0), stream_segments)
        heads_out = jnp.take(heads_out, positions, axis=0)
        attn_b = low(low_back(heads_out)).reshape(TOKENS, HEADS * HEAD_DIM)
        attn_sum = low_back(matmul(attn_b, w_attn_out))
        laurel_mid = matmul(normed_b, laurel_left)
        laurel_sum = matmul(laurel_mid, laurel_right)
        residual = (stream_f + norm_gain(attn_sum, gain_attn) + normed + norm_gain(laurel_sum, gain_laurel)) * root_half
        pre_ff = low(norm_gain(residual, gain_pre_ff))
        gate_pre = low_back(matmul(pre_ff, w_gate))
        up_pre = low_back(matmul(pre_ff, w_up))
        activated = low(jax.nn.gelu(gate_pre, approximate=True) * up_pre)
        ff_sum = low_back(matmul(activated, w_down))
        after_ff = residual + norm_gain(ff_sum, gain_post_ff)
        join_pre = matmul(after_ff, join_gate)
        joined = jax.nn.gelu(join_pre, approximate=True) * input_f
        join_sum = matmul(joined, join_proj)
        return after_ff + norm_gain(join_sum, gain_join)
    floats = (stream.astype(jnp.float32), layer_input.astype(jnp.float32), gain_input, gain_query, gain_key, w_query.astype(jnp.float32), w_key.astype(jnp.float32), w_value.astype(jnp.float32), w_attn_out.astype(jnp.float32), gain_attn, laurel_left.astype(jnp.float32), laurel_right.astype(jnp.float32), gain_laurel, gain_pre_ff, w_gate.astype(jnp.float32), w_up.astype(jnp.float32), w_down.astype(jnp.float32), gain_post_ff, join_gate.astype(jnp.float32), join_proj.astype(jnp.float32), gain_join)
    result, backward = jax.vjp(forward, *floats)
    grads = backward(out_grad.astype(jnp.float32))
    return (result, grads[0], grads[1], grads[2], grads[3], grads[4], grads[5], grads[6], grads[7], grads[8], grads[9], grads[10], grads[11], grads[12], grads[13], grads[14], grads[15], grads[16], grads[17], grads[18], grads[19], grads[20])
```

```python
import jax
import jax.numpy as jnp
from jax import lax
from jax.experimental import pallas as pl
from jax.experimental.pallas import tpu as pltpu
from jax.sharding import PartitionSpec as P

EPS = 1e-06
ROPE_BASE = 1000000.0
ROOT_HALF = 0.7071067811865476
GELU_A = 0.7978845608028654
GELU_B = 0.044715
STRETCH = 128
HEAD = 256
SLOTS = 64
PAD_SLOTS = 72
CHUNK = 4
BF = jnp.bfloat16
F32 = jnp.float32


def hop(value, axis, mask):
    return lax.ppermute(value, axis, [(i, i ^ mask) for i in range(lax.axis_size(axis))])


def pick(value, index, axis):
    return lax.dynamic_index_in_dim(value, index, axis, keepdims=False)


def gather_wt(own):
    near = hop(own, "wt", 2)
    core = hop(own, "wt", 1)
    far = hop(near, "wt", 1)
    return own, near, core, far


def scatter_wt(part):
    half = part.shape[0] // 2
    quarter = half // 2
    kept = part[:half] + hop(part[half:].astype(BF), "wt", 1).astype(F32)
    return kept[:quarter] + hop(kept[quarter:].astype(BF), "wt", 2).astype(F32)


def scatter_axis(value, me, axis, unit, size):
    total = pick(value, me, axis).astype(F32)
    for k in range(1, size):
        total = total + hop(pick(value, me ^ k, axis).astype(BF), "ctx", k * unit).astype(F32)
    return total


def swap_halves(value):
    half = value.shape[0] // 2
    return jnp.concatenate([value[half:], value[:half]], axis=0)


def dot(left, right):
    return jnp.dot(left, right, preferred_element_type=F32)


def dot_rows(left, right):
    return lax.dot_general(left, right, (((0,), (0,)), ((), ())), preferred_element_type=F32)


def dot_cols(left, right):
    return lax.dot_general(left, right, (((1,), (1,)), ((), ())), preferred_element_type=F32)


def fine(left, right):
    return jnp.dot(
        left.astype(F32), right.astype(F32), precision=lax.Precision.HIGH, preferred_element_type=F32
    )


def fine_cols(left, right):
    return lax.dot_general(
        left.astype(F32),
        right.astype(F32),
        (((1,), (1,)), ((), ())),
        precision=lax.Precision.HIGH,
        preferred_element_type=F32,
    )


def rms(values):
    return lax.rsqrt(jnp.mean(values * values, axis=-1, keepdims=True) + EPS)


def norm_back(grad, normal, scale, gain):
    inner = grad * gain
    back = scale * (inner - normal * jnp.mean(inner * normal, axis=-1, keepdims=True))
    return back, jnp.sum(grad * normal, axis=0)


def rotate(values, cosine, sine):
    half = values.shape[-1] // 2
    front, rear = values[..., :half], values[..., half:]
    return jnp.concatenate([front * cosine - rear * sine, rear * cosine + front * sine], axis=-1)


def gelu_parts(value):
    square = value * value
    bend = jnp.tanh(GELU_A * value * (1.0 + GELU_B * square))
    half = 0.5 * (1.0 + bend)
    slope = half + 0.5 * value * (1.0 - bend * bend) * GELU_A * (1.0 + 3.0 * GELU_B * square)
    return value * half, slope


AT_V = PAD_SLOTS
AT_HI = 2 * PAD_SLOTS
AT_LO = AT_HI + 2
AT_Z = AT_LO + 2
AT_ENDS = AT_Z + 1


def load_pieces(pieces, held, sem):
    copies = [
        pltpu.make_async_copy(piece, held.at[pl.ds(8 * i, 8)], sem.at[i])
        for i, piece in enumerate(pieces)
    ]
    for copy in copies:
        copy.start()
    for copy in copies:
        copy.wait()


def query_places(meta, tile, shape, along):
    row = lax.broadcasted_iota(jnp.int32, shape, along) & (STRETCH - 1)
    row = (row + 64 * meta[AT_Z]) & (STRETCH - 1)
    place = meta[AT_HI + tile] * STRETCH + row
    start = jnp.zeros(shape, jnp.int32)
    for j in range(8):
        end = meta[AT_ENDS + j]
        start = jnp.maximum(start, jnp.where(place >= end, end, 0))
    return place, start


def key_places(meta, first, shape, along):
    at = lax.broadcasted_iota(jnp.int32, shape, along)
    row = ((at & (STRETCH - 1)) + 64 * meta[AT_Z]) & (STRETCH - 1)
    return first * STRETCH + (at - (at & (STRETCH - 1))) + row


def tile_of(ref, tile):
    rows = pl.ds(tile * STRETCH, STRETCH)
    return jnp.concatenate([ref[rows, :HEAD], ref[rows, HEAD:]], axis=0)


def stretches(meta, held, at, first):
    return jnp.concatenate([held[meta[at + first + u]] for u in range(CHUNK)], axis=0)


def turns_of(meta, tile):
    return (meta[AT_HI + tile] - meta[AT_LO + tile] + CHUNK) // CHUNK


def forward_kernel(meta, q_ref, *refs):
    pieces, (low_ref, full_ref, lse_ref), (held, acc, total, sem) = refs[:16], refs[16:19], refs[19:]
    load_pieces(pieces, held, sem)
    for tile in range(2):
        query = tile_of(q_ref, tile)
        place, start = query_places(meta, tile, (2 * STRETCH, 1), 0)
        acc[...] = jnp.zeros_like(acc)
        total[...] = jnp.zeros_like(total)

        def turn(i, carry):
            first = meta[AT_LO + tile] + CHUNK * i
            keys = stretches(meta, held, 0, first)
            values = stretches(meta, held, AT_V, first)
            scores = dot_cols(query, keys)
            key_at = key_places(meta, first, (1, CHUNK * STRETCH), 1)
            allowed = (key_at <= place) & (key_at >= start)
            weights = jnp.where(allowed, jnp.exp(scores), 0.0)
            part = weights[:, :STRETCH]
            for u in range(1, CHUNK):
                part = part + weights[:, u * STRETCH : (u + 1) * STRETCH]
            total[...] += part
            acc[...] += dot(weights.astype(BF), values)
            return carry

        lax.fori_loop(0, turns_of(meta, tile), turn, 0)
        row_total = jnp.sum(total[...], axis=1, keepdims=True)
        result = acc[...] / row_total
        rows = pl.ds(tile * STRETCH, STRETCH)
        for head in range(2):
            block = result[head * STRETCH : (head + 1) * STRETCH]
            low_ref[rows, head * HEAD : (head + 1) * HEAD] = block.astype(BF)
            full_ref[rows, head * HEAD : (head + 1) * HEAD] = block
        logs = jnp.broadcast_to(jnp.log(row_total), (2 * STRETCH, STRETCH))
        lse_ref[tile] = jnp.transpose(logs)[:8]


def backward_kernel(meta, q_ref, g_ref, full_ref, lse_ref, *refs):
    pieces, dq_ref, outs = refs[:16], refs[16], refs[17:33]
    held, grads, acc, sem = refs[33:]
    grads[...] = jnp.zeros_like(grads)
    load_pieces(pieces, held, sem)
    for tile in range(2):
        query = tile_of(q_ref, tile)
        grad = tile_of(g_ref, tile)
        full = tile_of(full_ref, tile)
        place, start = query_places(meta, tile, (1, 2 * STRETCH), 1)
        lse = lse_ref[tile][:1]
        delta = jnp.sum(grad.astype(F32) * full, axis=1, keepdims=True)
        delta = jnp.transpose(jnp.broadcast_to(delta, (2 * STRETCH, STRETCH)))[:1]
        acc[...] = jnp.zeros_like(acc)

        def turn(i, carry):
            first = meta[AT_LO + tile] + CHUNK * i
            keys = stretches(meta, held, 0, first)
            values = stretches(meta, held, AT_V, first)
            key_at = key_places(meta, first, (CHUNK * STRETCH, 1), 0)
            allowed = (key_at <= place) & (key_at >= start)
            weights = jnp.where(allowed, jnp.exp(dot_cols(keys, query) - lse), 0.0)
            slopes = (weights * (dot_cols(values, grad) - delta)).astype(BF)
            key_term = dot(slopes, query)
            value_term = dot(weights.astype(BF), grad)
            acc[...] += dot_rows(slopes, keys)
            for u in range(CHUNK):
                part = slice(u * STRETCH, (u + 1) * STRETCH)
                for at, term in ((meta[first + u], key_term), (meta[AT_V + first + u], value_term)):
                    grads[at] = (grads[at].astype(F32) + term[part]).astype(BF)
            return carry

        lax.fori_loop(0, turns_of(meta, tile), turn, 0)
        rows = pl.ds(tile * STRETCH, STRETCH)
        for head in range(2):
            block = acc[head * STRETCH : (head + 1) * STRETCH]
            dq_ref[rows, head * HEAD : (head + 1) * HEAD] = block * (HEAD**-0.5)
    copies = [
        pltpu.make_async_copy(grads.at[pl.ds(8 * i, 8)], out, sem.at[i])
        for i, out in enumerate(outs)
    ]
    for copy in copies:
        copy.start()
    for copy in copies:
        copy.wait()


def in_vmem():
    return pl.BlockSpec(memory_space=pltpu.VMEM)


def anywhere():
    return pl.BlockSpec(memory_space=pl.ANY)


def attend_forward(meta, query, pieces):
    rows = query.shape[0]
    return pl.pallas_call(
        forward_kernel,
        out_shape=(
            jax.ShapeDtypeStruct((rows, 2 * HEAD), BF),
            jax.ShapeDtypeStruct((rows, 2 * HEAD), F32),
            jax.ShapeDtypeStruct((2, 8, 2 * STRETCH), F32),
        ),
        in_specs=[pl.BlockSpec(memory_space=pltpu.SMEM), in_vmem()] + [anywhere()] * 16,
        out_specs=(in_vmem(), in_vmem(), in_vmem()),
        scratch_shapes=[
            pltpu.VMEM((2 * SLOTS, STRETCH, HEAD), BF),
            pltpu.VMEM((2 * STRETCH, HEAD), F32),
            pltpu.VMEM((2 * STRETCH, STRETCH), F32),
            pltpu.SemaphoreType.DMA((16,)),
        ],
        compiler_params=pltpu.CompilerParams(vmem_limit_bytes=24 * 1024 * 1024),
        cost_estimate=pl.CostEstimate(
            flops=3 * 10**9, bytes_accessed=10**7, transcendentals=2 * 10**6
        ),
        name="attend_forward",
    )(meta, query, *pieces)


def attend_backward(meta, query, grad, full, lse, pieces):
    rows = query.shape[0]
    piece = jax.ShapeDtypeStruct((8, STRETCH, HEAD), BF)
    outs = pl.pallas_call(
        backward_kernel,
        out_shape=(jax.ShapeDtypeStruct((rows, 2 * HEAD), F32),) + (piece,) * 16,
        in_specs=[pl.BlockSpec(memory_space=pltpu.SMEM)] + [in_vmem()] * 4 + [anywhere()] * 16,
        out_specs=(in_vmem(),) + (anywhere(),) * 16,
        scratch_shapes=[
            pltpu.VMEM((2 * SLOTS, STRETCH, HEAD), BF),
            pltpu.VMEM((2 * SLOTS, STRETCH, HEAD), BF),
            pltpu.VMEM((2 * STRETCH, HEAD), F32),
            pltpu.SemaphoreType.DMA((16,)),
        ],
        compiler_params=pltpu.CompilerParams(vmem_limit_bytes=36 * 1024 * 1024),
        cost_estimate=pl.CostEstimate(
            flops=10**10, bytes_accessed=2 * 10**7, transcendentals=2 * 10**6
        ),
        name="attend_backward",
    )(meta, query, grad, full, lse, *pieces)
    return outs[0], outs[1:]


def local(
    stream,
    layer_input,
    out_grad,
    doc_lengths,
    stretch_slots,
    gain_input,
    gain_query,
    gain_key,
    w_query,
    w_key,
    w_value,
    w_attn_out,
    gain_attn,
    laurel_left,
    laurel_right,
    gain_laurel,
    gain_pre_ff,
    w_gate,
    w_up,
    w_down,
    gain_post_ff,
    join_gate,
    join_proj,
    gain_join,
):
    wt = lax.axis_index("wt")
    core, zlo = wt & 1, wt >> 1
    ctx = lax.axis_index("ctx")
    at_x, at_z, at_y = ctx & 3, (ctx >> 2) & 1, ctx >> 3
    first_core = core == 0
    half = HEAD // 2

    def starts(k):
        return ((core ^ (k & 1)) * 2 + (zlo ^ (k >> 1))) * 64

    def natural(blocks):
        stacked = jnp.stack(blocks)
        return jnp.concatenate(
            [pick(stacked, wt ^ ((b & 1) * 2 + (b >> 1)), 0) for b in range(4)], axis=0
        )

    stream_f = jnp.concatenate(
        [lax.dynamic_slice_in_dim(stream, starts(k), 64, 0) for k in (0, 2, 1, 3)], axis=0
    ).astype(F32)
    grad_top = lax.dynamic_slice_in_dim(out_grad, starts(0), 64, 0).astype(F32)

    pack = jnp.concatenate([laurel_left.T, laurel_right, join_gate.T, join_proj], axis=0)
    packs = [pack] + [hop(pack, "wt", k) for k in (1, 2, 3)]
    left_t = jnp.concatenate([p[:16] for p in packs], axis=0)
    right_w = jnp.concatenate([p[16:32] for p in packs], axis=0)
    gate_t = jnp.concatenate([p[32:96] for p in packs], axis=0)
    proj_w = jnp.concatenate([p[96:160] for p in packs], axis=0)
    inputs = [lax.dynamic_slice_in_dim(layer_input, starts(k), 64, 0) for k in range(4)]
    input_f = jnp.concatenate(
        [inputs[0]] + [hop(inputs[k], "wt", k) for k in (1, 2, 3)], axis=1
    ).astype(F32)

    doc_ends = jnp.cumsum(doc_lengths)
    tiles = [lax.dynamic_index_in_dim(stretch_slots, 2 * ctx + (core ^ t), 0) for t in range(2)]
    hi = jnp.concatenate(tiles)
    lo = jnp.max(
        jnp.where(doc_ends[None, :] <= hi[:, None] * STRETCH, doc_ends[None, :], 0), axis=1
    )
    lo = lo // STRETCH
    row = (jnp.arange(STRETCH, dtype=jnp.int32) + 64 * zlo) & (STRETCH - 1)
    positions = (hi[:, None] * STRETCH + row[None, :]).reshape(-1)
    names = jnp.arange(SLOTS, dtype=jnp.int32)
    slot_of = jnp.sum(jnp.where(stretch_slots[None, :] == names[:, None], names[None, :], 0), axis=1)
    relative = (slot_of >> 1) ^ ctx
    rel_x, rel_z, rel_y = relative & 3, (relative >> 2) & 1, relative >> 3
    places = (
        rel_y * 8 + rel_x * 2 + rel_z,
        SLOTS // 2 + rel_x * 8 + rel_y * 2 + rel_z,
    )
    second = (slot_of & 1) == 1
    key_at = core * SLOTS + jnp.where(second, places[1], places[0])
    value_at = (1 - core) * SLOTS + jnp.where(second, places[0], places[1])
    blank = jnp.zeros((PAD_SLOTS - SLOTS,), jnp.int32)
    meta = jnp.concatenate([key_at, blank, value_at, blank, hi, lo, zlo[None], doc_ends]).astype(
        jnp.int32
    )
    exponents = jnp.arange(half, dtype=F32) * (2.0 / HEAD)
    angles = positions.astype(F32)[:, None] * (1.0 / ROPE_BASE**exponents)[None, :]
    cosine, sine = jnp.cos(angles), jnp.sin(angles)

    scale_in = rms(stream_f)
    normal_in = stream_f * scale_in
    normed = normal_in * gain_input
    normed_b = normed.astype(BF)
    key_half = dot(normed_b, w_key)
    value_half = dot(normed_b, w_value)
    arrived = swap_halves(hop(jnp.where(first_core, value_half, key_half), "wt", 1))
    kind = jnp.concatenate(
        [jnp.where(first_core, key_half, arrived), jnp.where(first_core, arrived, value_half)],
        axis=1,
    )
    kind_gain = jnp.where(first_core, gain_key, 1.0)
    kind_cos = jnp.where(first_core, cosine, 1.0)
    kind_sin = jnp.where(first_core, sine, 0.0)
    kind_scale = rms(kind)
    kind_normal = kind * kind_scale
    kind_b = rotate(kind_normal * kind_gain, kind_cos, kind_sin).astype(BF)

    across = hop(kind_b, "ctx", 4)
    pieces = []
    for h, (one, two) in enumerate(((1, 8), (8, 1))):
        rows = slice(h * STRETCH, (h + 1) * STRETCH)
        block = jnp.concatenate([kind_b[rows], across[rows]], axis=0)
        block = jnp.concatenate([block] + [hop(block, "ctx", k * one) for k in (1, 2, 3)], axis=0)
        pieces += [block] + [hop(block, "ctx", k * two) for k in (1, 2, 3)]
    pieces += [hop(piece, "wt", 1) for piece in pieces]
    pieces = [piece.reshape(8, STRETCH, HEAD) for piece in pieces]

    query_raw = dot(normed_b, w_query).reshape(2 * STRETCH, 2, HEAD)
    query_scale = rms(query_raw)
    query_normal = query_raw * query_scale
    query_rot = rotate(query_normal * gain_query, cosine[:, None, :], sine[:, None, :])
    query_b = (query_rot.astype(BF) * (HEAD**-0.5)).astype(BF).reshape(2 * STRETCH, 2 * HEAD)

    attn_b, attn_full, lse = attend_forward(meta, query_b, pieces)

    attn_sum = scatter_wt(dot(attn_b, w_attn_out))
    stream_own, normed_own, normed_own_b = stream_f[:64], normed[:64], normed_b[:64]
    normal_own = normal_in[:64]
    laurel_mid = fine_cols(normed_own_b, left_t)
    laurel_sum = fine(laurel_mid, right_w)
    attn_scale, laurel_scale = rms(attn_sum), rms(laurel_sum)
    attn_normal, laurel_normal = attn_sum * attn_scale, laurel_sum * laurel_scale
    residual = (
        stream_own + attn_normal * gain_attn + normed_own + laurel_normal * gain_laurel
    ) * ROOT_HALF
    pre_scale = rms(residual)
    pre_normal = residual * pre_scale
    pre_all = jnp.concatenate(gather_wt((pre_normal * gain_pre_ff).astype(BF)), axis=0)

    gate_pre = dot(pre_all, w_gate)
    up_pre = dot(pre_all, w_up)
    act_b = (gelu_parts(gate_pre)[0] * up_pre).astype(BF)
    ff_sum = scatter_wt(dot(act_b, w_down))
    pre_group = jnp.concatenate([pre_all] + [hop(pre_all, "ctx", k) for k in (1, 2, 3)], axis=0)
    act_group = jnp.concatenate([act_b] + [hop(act_b, "ctx", 8 * k) for k in (1, 2, 3)], axis=0)
    ff_scale = rms(ff_sum)
    ff_normal = ff_sum * ff_scale
    after_ff = residual + ff_normal * gain_post_ff

    join_pre = fine_cols(after_ff, gate_t)
    join_gelu, join_slope = gelu_parts(join_pre)
    joined = join_gelu * input_f
    join_sum = fine(joined, proj_w)
    join_scale = rms(join_sum)
    join_normal = join_sum * join_scale
    layer_out = after_ff + join_normal * gain_join

    grad_join_sum, gain_join_part = norm_back(grad_top, join_normal, join_scale, gain_join)
    grad_joined = fine_cols(grad_join_sum, proj_w)
    grad_join_pre = grad_joined * input_f * join_slope
    grad_input = grad_joined * join_gelu
    grad_after = grad_top + fine(grad_join_pre, gate_t)

    grad_ff, gain_post_part = norm_back(grad_after, ff_normal, ff_scale, gain_post_ff)
    grad_ff_all = jnp.concatenate(gather_wt(grad_ff.astype(BF)), axis=0)
    grad_act = dot_cols(grad_ff_all, w_down)
    gate_gelu, gate_slope = gelu_parts(gate_pre)
    grad_gate_b = (grad_act * up_pre * gate_slope).astype(BF)
    grad_up_b = (grad_act * gate_gelu).astype(BF)
    grad_pre = scatter_wt(dot_cols(grad_gate_b, w_gate) + dot_cols(grad_up_b, w_up))

    grad_resid, gain_pre_part = norm_back(grad_pre, pre_normal, pre_scale, gain_pre_ff)
    branch = (grad_after + grad_resid) * ROOT_HALF
    grad_attn, gain_attn_part = norm_back(branch, attn_normal, attn_scale, gain_attn)
    grad_attn_all = jnp.concatenate(gather_wt(grad_attn.astype(BF)), axis=0)
    grad_heads = dot_cols(grad_attn_all, w_attn_out).astype(BF)
    grad_laurel, gain_laurel_part = norm_back(branch, laurel_normal, laurel_scale, gain_laurel)
    grad_mid = fine_cols(grad_laurel, right_w)

    grad_query_rot, grad_pieces = attend_backward(
        meta, query_b, grad_heads, attn_full, lse, pieces
    )
    kind_rows = []
    for h, (one, two) in enumerate(((1, 8), (8, 1))):
        own = [
            grad_pieces[4 * h + j].astype(F32)
            + hop(grad_pieces[8 + 4 * h + j], "wt", 1).astype(F32)
            for j in range(4)
        ]
        total = own[0]
        for k in (1, 2, 3):
            total = total + hop(own[k].astype(BF), "ctx", k * two).astype(F32)
        total = total.reshape(4, 2, STRETCH, HEAD)
        sums = total[0]
        for k in (1, 2, 3):
            sums = sums + hop(total[k].astype(BF), "ctx", k * one).astype(F32)
        kind_rows.append(sums[0] + hop(sums[1].astype(BF), "ctx", 4).astype(F32))
    grad_kind_rot = jnp.concatenate(kind_rows, axis=0)
    grad_kind_normed = rotate(grad_kind_rot, kind_cos, -kind_sin)
    grad_kind, gain_kind_part = norm_back(grad_kind_normed, kind_normal, kind_scale, kind_gain)
    gain_key_part = jnp.where(first_core, gain_kind_part, 0.0)
    away = jnp.where(first_core, grad_kind[:, half:], grad_kind[:, :half]).astype(BF)
    home = jnp.where(first_core, grad_kind[:, :half], grad_kind[:, half:]).astype(BF)
    away = swap_halves(hop(away, "wt", 1))
    grad_key_b = jnp.where(first_core, home, away)
    grad_value_b = jnp.where(first_core, away, home)

    grad_query_normed = rotate(
        grad_query_rot.reshape(2 * STRETCH, 2, HEAD), cosine[:, None, :], -sine[:, None, :]
    )
    grad_query, gain_query_part = norm_back(
        grad_query_normed, query_normal, query_scale, gain_query
    )
    gain_query_part = jnp.sum(gain_query_part, axis=0)
    grad_query_b = grad_query.astype(BF).reshape(2 * STRETCH, 2 * HEAD)

    normed_part = (
        dot_cols(grad_query_b, w_query)
        + dot_cols(grad_key_b, w_key)
        + dot_cols(grad_value_b, w_value)
    )
    own_part = branch + fine(grad_mid, left_t)
    gain_input_part = jnp.sum(own_part * normal_own, axis=0) + jnp.sum(
        normed_part * normal_in, axis=0
    )
    grad_normed = own_part + scatter_wt(normed_part)
    grad_stream_extra, _ = norm_back(grad_normed, normal_own, scale_in[:64], gain_input)
    stream_grad = branch + grad_stream_extra

    def spread(own):
        first, near, core_rows, far = gather_wt(own.astype(BF))
        return natural([first, core_rows, near, far]).astype(F32)

    layer_out_all = spread(layer_out)
    stream_grad_all = spread(stream_grad)
    parts = [grad_input[:, 64 * k : 64 * (k + 1)] for k in range(4)]
    grad_input_all = natural([parts[0]] + [hop(parts[k], "wt", k) for k in (1, 2, 3)])

    def scatter_ctx(grad, order):
        value = grad.astype(BF).reshape(4, 2, 4, 64, -1)
        if order == "x":
            value = scatter_axis(value, at_x, 2, 1, 4).astype(BF)
            value = scatter_axis(value, at_y, 0, 8, 4).astype(BF)
        else:
            value = scatter_axis(value, at_y, 0, 8, 4).astype(BF)
            value = scatter_axis(value, at_x, 1, 1, 4).astype(BF)
        return scatter_axis(value, at_z, 0, 4, 2)

    quarter = 512
    ff_group = [
        lax.dynamic_slice_in_dim(grad_ff_all, (at_y ^ k) * quarter, quarter, 1) for k in range(4)
    ]
    ff_group = jnp.concatenate(
        [ff_group[0]] + [hop(ff_group[k], "ctx", 8 * k) for k in (1, 2, 3)], axis=0
    )
    down = dot_rows(ff_group, act_group).astype(BF).reshape(2, 4, 64, -1)
    down = scatter_axis(down, at_x, 1, 1, 4).astype(BF)
    grad_w_down = scatter_axis(down, at_z, 0, 4, 2).T

    wide = []
    for grad in (grad_gate_b, grad_up_b):
        cuts = [
            lax.dynamic_slice_in_dim(grad, (at_x ^ k) * quarter, quarter, 1) for k in range(4)
        ]
        cuts = jnp.concatenate([cuts[0]] + [hop(cuts[k], "ctx", k) for k in (1, 2, 3)], axis=0)
        value = dot_rows(pre_group, cuts).astype(BF).reshape(4, 2, 4, 64, quarter)
        value = scatter_axis(value, at_y, 0, 8, 4).astype(BF)
        value = scatter_axis(value, at_z, 0, 4, 2).astype(BF)
        got = [pick(value, at_x, 0)]
        got += [hop(pick(value, at_x ^ k, 0), "ctx", k) for k in (1, 2, 3)]
        stacked = jnp.stack(got)
        wide.append(
            jnp.concatenate([pick(stacked, at_x ^ q, 0) for q in range(4)], axis=1).astype(F32)
        )
    grad_w_gate, grad_w_up = wide

    grad_w_attn_out = scatter_ctx(dot_rows(grad_attn_all, attn_b), "y").T
    grad_w_query = scatter_ctx(dot_rows(normed_b, grad_query_b), "x")
    pair = jnp.concatenate([grad_key_b, grad_value_b], axis=1)
    grad_pair = scatter_ctx(dot_rows(normed_b, pair), "y")
    grad_w_key, grad_w_value = grad_pair[:, :half], grad_pair[:, half:]

    low = [
        dot_rows(grad_mid.astype(BF), normed_own_b),
        dot_rows(laurel_mid.astype(BF), grad_laurel.astype(BF)),
        dot_rows(grad_join_pre.astype(BF), after_ff.astype(BF)),
        dot_rows(joined.astype(BF), grad_join_sum.astype(BF)),
    ]
    gains = jnp.stack(
        [gain_attn_part, gain_laurel_part, gain_pre_part, gain_post_part, gain_join_part]
        + [jnp.zeros_like(gain_attn_part)] * 3
    )

    def small_block(k):
        return [value[value.shape[0] // 4 * k :][: value.shape[0] // 4] for value in low] + [gains]

    small = jnp.concatenate(
        small_block(0) + small_block(2) + small_block(1) + small_block(3), axis=0
    )
    small = scatter_ctx(scatter_wt(small).T, "x")
    grad_left, grad_right = small[:, :16], small[:, 16:32].T
    grad_gate, grad_proj = small[:, 32:96], small[:, 96:160].T

    late = jnp.concatenate(
        [
            gain_input_part.reshape(32, 64),
            gain_query_part.reshape(32, 8),
            gain_key_part.reshape(32, 8),
            jnp.zeros((32, 48), F32),
        ],
        axis=1,
    ).reshape(4, 2, 4, 128)
    for axis, me, unit, size in ((2, at_x, 1, 4), (0, at_y, 8, 4), (0, at_z, 4, 2)):
        total = pick(late, me, axis)
        for k in range(1, size):
            total = total + hop(pick(late, me ^ k, axis), "ctx", k * unit)
        late = total
    late = late + hop(late, "wt", 1)
    late = late + hop(late, "wt", 2)

    return (
        layer_out_all,
        stream_grad_all,
        grad_input_all,
        late[:64],
        late[64:72],
        late[72:80],
        grad_w_query,
        grad_w_key,
        grad_w_value,
        grad_w_attn_out,
        small[:, 160],
        grad_left,
        grad_right,
        small[:, 161],
        small[:, 162],
        grad_w_gate,
        grad_w_up,
        grad_w_down,
        small[:, 163],
        grad_gate,
        grad_proj,
        small[:, 164],
    )


def solution(mesh):
    rows, cols, tops = P("ctx", "wt"), P("wt", "ctx"), P("ctx")
    down, across = P(None, "wt"), P("wt", None)
    return jax.shard_map(
        local,
        mesh=mesh,
        in_specs=(
            P("ctx", None),
            P("ctx", "wt"),
            P("ctx", None),
            P(),
            P(),
            P(),
            P(),
            P(),
            down,
            down,
            down,
            across,
            P(),
            down,
            across,
            P(),
            P(),
            down,
            down,
            across,
            P(),
            down,
            across,
            P(),
        ),
        out_specs=(
            P("ctx", None),
            P("ctx", None),
            rows,
            tops,
            tops,
            tops,
            rows,
            rows,
            rows,
            cols,
            tops,
            rows,
            cols,
            tops,
            tops,
            rows,
            rows,
            cols,
            tops,
            rows,
            cols,
            tops,
        ),
        check_vma=False,
    )
```

```python
import jax
import jax.numpy as jnp
from jax import lax
from jax.experimental import pallas as pl
from jax.experimental.pallas import tpu as pltpu
from jax.sharding import PartitionSpec as P

EPS = 1e-06
ROPE_BASE = 1000000.0
ROOT_HALF = 0.7071067811865476
GELU_A = 0.7978845608028654
GELU_B = 0.044715
STRETCH = 128
HEAD = 256
SLOTS = 64
PAD_SLOTS = 72
CHUNK = 4
D = 2048
VMEM_GRANT = 60 * 1024 * 1024
BF = jnp.bfloat16
F32 = jnp.float32


def hop(value, axis, mask):
    return lax.ppermute(value, axis, [(i, i ^ mask) for i in range(lax.axis_size(axis))])


def pick(value, index, axis):
    return lax.dynamic_index_in_dim(value, index, axis, keepdims=False)


def ctx_of(y, z, x):
    return (y * 2 + z) * 4 + x


GROUP_X = [[ctx_of(y, z, x) for x in range(4)] for y in range(4) for z in range(2)]
GROUP_Y = [[ctx_of(y, z, x) for y in range(4)] for z in range(2) for x in range(4)]
GROUP_Z = [[ctx_of(y, z, x) for z in range(2)] for y in range(4) for x in range(4)]


def gather_group(value, groups):
    return lax.all_gather(value, "ctx", axis=0, axis_index_groups=groups)


def scatter_group(value, groups):
    return lax.psum_scatter(
        value, "ctx", scatter_dimension=0, axis_index_groups=groups, tiled=True
    )


def gate_kernel(*refs):
    pass


def hold(values, event):
    return pl.pallas_call(
        gate_kernel,
        out_shape=tuple(jax.ShapeDtypeStruct(value.shape, value.dtype) for value in values),
        in_specs=[pl.BlockSpec(memory_space=pl.ANY)] * (len(values) + 1),
        out_specs=(pl.BlockSpec(memory_space=pl.ANY),) * len(values),
        input_output_aliases={i: i for i in range(len(values))},
        name="gate",
    )(*values, event)


def ring_gather(block, near, other):
    one = hop(block, "ctx", near)
    two = hop(block, "ctx", other)
    half = block.shape[0] // 2
    return [
        block,
        one,
        two,
        hop(one[:half], "ctx", other),
        hop(two[half:], "ctx", near),
    ]


def gather_wt(own):
    near = hop(own, "wt", 2)
    core = hop(own, "wt", 1)
    far = hop(near, "wt", 1)
    return own, near, core, far


def scatter_wt(kept, sent):
    kept = kept + hop(sent, "wt", 1).astype(F32)
    quarter = kept.shape[0] // 2
    return kept[:quarter], hop(kept[quarter:].astype(BF), "wt", 2)


def fold(kept, sent, mask):
    return (kept.astype(F32) + hop(sent, "ctx", mask).astype(F32)).astype(BF)


def swap_halves(value):
    half = value.shape[0] // 2
    return jnp.concatenate([value[half:], value[:half]], axis=0)


def dot(left, right):
    return jnp.dot(left, right, preferred_element_type=F32)


def dot_rows(left, right):
    return lax.dot_general(left, right, (((0,), (0,)), ((), ())), preferred_element_type=F32)


def dot_cols(left, right):
    return lax.dot_general(left, right, (((1,), (1,)), ((), ())), preferred_element_type=F32)


def halves_of(value):
    high = value.astype(BF)
    return high, (value - high.astype(F32)).astype(BF)


def fine(left, right):
    high, low = halves_of(left)
    return dot(high, right) + dot(low, right)


def fine_cols(left, right):
    high, low = halves_of(left)
    return dot_cols(high, right) + dot_cols(low, right)


def rms(values):
    return lax.rsqrt(jnp.mean(values * values, axis=-1, keepdims=True) + EPS)


def norm_back(grad, normal, scale, gain):
    inner = grad * gain
    back = scale * (inner - normal * jnp.mean(inner * normal, axis=-1, keepdims=True))
    return back, jnp.sum(grad * normal, axis=0, keepdims=grad.ndim == 2)


def rotate(values, cosine, sine):
    half = values.shape[-1] // 2
    front, rear = values[..., :half], values[..., half:]
    return jnp.concatenate([front * cosine - rear * sine, rear * cosine + front * sine], axis=-1)


def gelu_parts(value):
    square = value * value
    bend = jnp.tanh(GELU_A * value * (1.0 + GELU_B * square))
    half = 0.5 * (1.0 + bend)
    slope = half + 0.5 * value * (1.0 - bend * bend) * GELU_A * (1.0 + 3.0 * GELU_B * square)
    return value * half, slope


AT_V = PAD_SLOTS
AT_HI = 2 * PAD_SLOTS
AT_LO = AT_HI + 2
AT_Z = AT_LO + 2
AT_ENDS = AT_Z + 1


def piece_copies(pieces, held, sem):
    copies, at = [], 0
    for i, piece in enumerate(pieces):
        count = piece.shape[0]
        place = held.at[pl.ds(at, count)]
        copies.append(pltpu.make_async_copy(piece, place, sem.at[i]))
        at += count
    return copies


def load_pieces(pieces, held, sem):
    copies = piece_copies(pieces, held, sem)
    for copy in copies:
        copy.start()
    for copy in copies:
        copy.wait()


def query_places(meta, tile, shape, along):
    row = lax.broadcasted_iota(jnp.int32, shape, along) & (STRETCH - 1)
    row = (row + 64 * meta[AT_Z]) & (STRETCH - 1)
    place = meta[AT_HI + tile] * STRETCH + row
    start = jnp.zeros(shape, jnp.int32)
    for j in range(8):
        end = meta[AT_ENDS + j]
        start = jnp.maximum(start, jnp.where(place >= end, end, 0))
    return place, start


def key_places(meta, first, shape, along):
    at = lax.broadcasted_iota(jnp.int32, shape, along)
    row = ((at & (STRETCH - 1)) + 64 * meta[AT_Z]) & (STRETCH - 1)
    return first * STRETCH + (at - (at & (STRETCH - 1))) + row


def tile_of(ref, tile):
    rows = pl.ds(tile * STRETCH, STRETCH)
    return jnp.concatenate([ref[rows, :HEAD], ref[rows, HEAD:]], axis=0)


def stretches(meta, held, at, first):
    return jnp.concatenate([held[meta[at + first + u]] for u in range(CHUNK)], axis=0)


def turns_of(meta, tile):
    return (meta[AT_HI + tile] - meta[AT_LO + tile] + CHUNK) // CHUNK


def forward_kernel(meta, q_ref, w_ref, *refs):
    pieces, (low_ref, full_ref, lse_ref, kept_ref, sent_ref) = refs[:20], refs[20:25]
    held, acc, total, sem = refs[25:]
    load_pieces(pieces, held, sem)
    for tile in range(2):
        query = tile_of(q_ref, tile)
        place, start = query_places(meta, tile, (2 * STRETCH, 1), 0)
        acc[...] = jnp.zeros_like(acc)
        total[...] = jnp.zeros_like(total)

        def turn(i, carry):
            first = meta[AT_LO + tile] + CHUNK * i
            keys = stretches(meta, held, 0, first)
            values = stretches(meta, held, AT_V, first)
            scores = dot_cols(query, keys)
            key_at = key_places(meta, first, (1, CHUNK * STRETCH), 1)
            allowed = (key_at <= place) & (key_at >= start)
            weights = jnp.where(allowed, jnp.exp(scores), 0.0)
            part = weights[:, :STRETCH]
            for u in range(1, CHUNK):
                part = part + weights[:, u * STRETCH : (u + 1) * STRETCH]
            total[...] += part
            acc[...] += dot(weights.astype(BF), values)
            return carry

        lax.fori_loop(0, turns_of(meta, tile), turn, 0)
        row_total = jnp.sum(total[...], axis=1, keepdims=True)
        result = acc[...] / row_total
        rows = pl.ds(tile * STRETCH, STRETCH)
        for head in range(2):
            block = result[head * STRETCH : (head + 1) * STRETCH]
            low_ref[rows, head * HEAD : (head + 1) * HEAD] = block.astype(BF)
            full_ref[rows, head * HEAD : (head + 1) * HEAD] = block
        logs = jnp.broadcast_to(jnp.log(row_total), (2 * STRETCH, STRETCH))
        lse_ref[tile] = jnp.transpose(logs)[:8]
    kept_ref[...] = dot(low_ref[:STRETCH], w_ref[...])
    sent_ref[...] = dot(low_ref[STRETCH:], w_ref[...]).astype(BF)


def backward_kernel(meta, q_ref, full_ref, lse_ref, w_ref, *refs):
    parts, pieces, dq_ref, outs = refs[:4], refs[4:24], refs[-10], refs[-9:-5]
    held, grads, acc, g_ref, sem = refs[-5:]
    copies = piece_copies(pieces, held, sem)
    for copy in copies:
        copy.start()
    for i, part in enumerate(parts):
        g_ref[64 * i : 64 * (i + 1)] = dot_cols(part[...], w_ref[...]).astype(BF)
    grads[...] = jnp.zeros_like(grads)
    for copy in copies:
        copy.wait()
    for tile in range(2):
        query = tile_of(q_ref, tile)
        grad = tile_of(g_ref, tile)
        full = tile_of(full_ref, tile)
        place, start = query_places(meta, tile, (1, 2 * STRETCH), 1)
        lse = lse_ref[tile][:1]
        delta = jnp.sum(grad.astype(F32) * full, axis=1, keepdims=True)
        delta = jnp.transpose(jnp.broadcast_to(delta, (2 * STRETCH, STRETCH)))[:1]
        acc[...] = jnp.zeros_like(acc)

        def turn(i, carry):
            first = meta[AT_LO + tile] + CHUNK * i
            keys = stretches(meta, held, 0, first)
            values = stretches(meta, held, AT_V, first)
            key_at = key_places(meta, first, (CHUNK * STRETCH, 1), 0)
            allowed = (key_at <= place) & (key_at >= start)
            weights = jnp.where(allowed, jnp.exp(dot_cols(keys, query) - lse), 0.0)
            slopes = (weights * (dot_cols(values, grad) - delta)).astype(BF)
            key_term = dot(slopes, query)
            value_term = dot(weights.astype(BF), grad)
            acc[...] += dot_rows(slopes, keys)
            for u in range(CHUNK):
                part = slice(u * STRETCH, (u + 1) * STRETCH)
                for at, term in ((meta[first + u], key_term), (meta[AT_V + first + u], value_term)):
                    grads[at] = (grads[at].astype(F32) + term[part]).astype(BF)
            return carry

        lax.fori_loop(0, turns_of(meta, tile), turn, 0)
        rows = pl.ds(tile * STRETCH, STRETCH)
        for head in range(2):
            block = acc[head * STRETCH : (head + 1) * STRETCH]
            dq_ref[rows, head * HEAD : (head + 1) * HEAD] = block * (HEAD**-0.5)
    copies = []
    for side in range(2):
        for h in range(2):
            at = 64 * side + 32 * h
            for out, first, count, begin in ((0, 24, 8, 8 * h), (1, 0, 24, 24 * h)):
                copies.append(
                    pltpu.make_async_copy(
                        grads.at[pl.ds(at + first, count)],
                        outs[2 * side + out].at[pl.ds(begin, count)],
                        sem.at[len(copies)],
                    )
                )
    for copy in copies:
        copy.start()
    for copy in copies:
        copy.wait()


def in_vmem():
    return pl.BlockSpec(memory_space=pltpu.VMEM)


def anywhere():
    return pl.BlockSpec(memory_space=pl.ANY)


def attend_forward(meta, query, w_attn_out, pieces):
    rows, width = query.shape[0], w_attn_out.shape[1]
    return pl.pallas_call(
        forward_kernel,
        out_shape=(
            jax.ShapeDtypeStruct((rows, 2 * HEAD), BF),
            jax.ShapeDtypeStruct((rows, 2 * HEAD), F32),
            jax.ShapeDtypeStruct((2, 8, 2 * STRETCH), F32),
            jax.ShapeDtypeStruct((STRETCH, width), F32),
            jax.ShapeDtypeStruct((STRETCH, width), BF),
        ),
        in_specs=[pl.BlockSpec(memory_space=pltpu.SMEM), in_vmem(), in_vmem()] + [anywhere()] * 20,
        out_specs=(in_vmem(),) * 5,
        scratch_shapes=[
            pltpu.VMEM((2 * SLOTS, STRETCH, HEAD), BF),
            pltpu.VMEM((2 * STRETCH, HEAD), F32),
            pltpu.VMEM((2 * STRETCH, STRETCH), F32),
            pltpu.SemaphoreType.DMA((20,)),
        ],
        compiler_params=pltpu.CompilerParams(vmem_limit_bytes=VMEM_GRANT),
        cost_estimate=pl.CostEstimate(
            flops=3 * 10**9, bytes_accessed=10**7, transcendentals=2 * 10**6
        ),
        name="attend_forward",
    )(meta, query, w_attn_out, *pieces)


def attend_backward(meta, query, full, lse, w_attn_out, parts, pieces, *events):
    rows = query.shape[0]
    outs = pl.pallas_call(
        backward_kernel,
        out_shape=(jax.ShapeDtypeStruct((rows, 2 * HEAD), F32),)
        + tuple(jax.ShapeDtypeStruct((count, STRETCH, HEAD), BF) for count in (16, 48, 16, 48)),
        in_specs=[pl.BlockSpec(memory_space=pltpu.SMEM)] + [in_vmem()] * 8
        + [anywhere()] * (20 + len(events)),
        out_specs=(in_vmem(),) + (anywhere(),) * 4,
        scratch_shapes=[
            pltpu.VMEM((2 * SLOTS, STRETCH, HEAD), BF),
            pltpu.VMEM((2 * SLOTS, STRETCH, HEAD), BF),
            pltpu.VMEM((2 * STRETCH, HEAD), F32),
            pltpu.VMEM((rows, 2 * HEAD), BF),
            pltpu.SemaphoreType.DMA((20,)),
        ],
        compiler_params=pltpu.CompilerParams(vmem_limit_bytes=VMEM_GRANT),
        cost_estimate=pl.CostEstimate(
            flops=10**10, bytes_accessed=2 * 10**7, transcendentals=2 * 10**6
        ),
        name="attend_backward",
    )(meta, query, full, lse, w_attn_out, *parts, *pieces, *events)
    return outs[0], outs[1:]


UNITS = 512


def ff_forward_kernel(*refs):
    parts, attn, w_gate, w_up, w_down = refs[:4], refs[4], refs[5], refs[6], refs[7]
    gate_out, up_out, pre_out, act_out, kept, sent = refs[8:14]
    now, acc = refs[14:]
    turn = pl.program_id(0)

    @pl.when(turn == 0)
    def first():
        for i, part in enumerate(parts):
            pre_out[64 * i : 64 * (i + 1)] = part[...]
        act_out[:, pl.num_programs(0) * UNITS :] = attn[...]
        acc[...] = jnp.zeros_like(acc)

    gate = dot(pre_out[...], w_gate[...])
    up = dot(pre_out[...], w_up[...])
    gate_out[...] = gate
    up_out[...] = up
    now[...] = (gelu_parts(gate)[0] * up).astype(BF)
    act_out[:, pl.ds(pl.multiple_of(turn * UNITS, UNITS), UNITS)] = now[...]
    acc[...] += dot(now[...], w_down[...])

    @pl.when(turn == pl.num_programs(0) - 1)
    def last():
        kept[...] = acc[:STRETCH]
        sent[...] = acc[STRETCH:].astype(BF)


def ff_forward(parts, attn, w_gate, w_up, w_down):
    width, units = w_gate.shape
    rows, heads = attn.shape
    whole = lambda shape: pl.BlockSpec(shape, lambda i: (0, 0))
    tall, flat = pl.BlockSpec((width, UNITS), lambda i: (0, i)), pl.BlockSpec((UNITS, width), lambda i: (i, 0))
    strip = pl.BlockSpec((rows, UNITS), lambda i: (0, i))
    return pl.pallas_call(
        ff_forward_kernel,
        grid=(units // UNITS,),
        out_shape=(
            jax.ShapeDtypeStruct((rows, units), F32),
            jax.ShapeDtypeStruct((rows, units), F32),
            jax.ShapeDtypeStruct((rows, width), BF),
            jax.ShapeDtypeStruct((rows, units + heads), BF),
            jax.ShapeDtypeStruct((rows // 2, width), F32),
            jax.ShapeDtypeStruct((rows // 2, width), BF),
        ),
        in_specs=[whole((rows // 4, width))] * 4 + [whole((rows, heads)), tall, tall, flat],
        out_specs=(
            strip,
            strip,
            whole((rows, width)),
            whole((rows, units + heads)),
            whole((rows // 2, width)),
            whole((rows // 2, width)),
        ),
        scratch_shapes=[pltpu.VMEM((rows, UNITS), BF), pltpu.VMEM((rows, width), F32)],
        compiler_params=pltpu.CompilerParams(vmem_limit_bytes=VMEM_GRANT),
        cost_estimate=pl.CostEstimate(
            flops=6 * rows * width * units, bytes_accessed=3 * 10**7, transcendentals=rows * units
        ),
        name="ff_forward",
    )(*parts, attn, w_gate, w_up, w_down)


def ff_backward_kernel(me, *refs):
    parts, (gate_ref, up_ref, w_gate, w_up, w_down) = refs[:4], refs[4:9]
    cuts, (all_out, kept, sent), acc = refs[10:14], refs[14:17], refs[17]
    block = pl.program_id(0)

    @pl.when(block == 0)
    def first():
        for i, part in enumerate(parts):
            all_out[64 * i : 64 * (i + 1)] = part[...]
        acc[...] = jnp.zeros_like(acc)

    grad_act = dot_cols(all_out[...], w_down[...])
    value, slope = gelu_parts(gate_ref[...])
    gate_grad = (grad_act * up_ref[...] * slope).astype(BF)
    up_grad = (grad_act * value).astype(BF)
    for k in range(4):


        @pl.when(block == k)
        def store():
            cuts[k][:, :UNITS] = gate_grad
            cuts[k][:, UNITS:] = up_grad

    acc[...] += dot_cols(gate_grad, w_gate[...]) + dot_cols(up_grad, w_up[...])

    @pl.when(block == 3)
    def last():
        kept[...] = acc[:STRETCH]
        sent[...] = acc[STRETCH:].astype(BF)


def ff_backward(me, parts, gate_pre, up_pre, w_gate, w_up, w_down, event):
    width, units = w_gate.shape
    rows = gate_pre.shape[0]
    whole = lambda shape: pl.BlockSpec(shape, lambda k, me: (0, 0))
    tall = pl.BlockSpec((width, UNITS), lambda k, me: (0, k ^ me[0]))
    flat = pl.BlockSpec((UNITS, width), lambda k, me: (k ^ me[0], 0))
    strip = pl.BlockSpec((rows, UNITS), lambda k, me: (0, k ^ me[0]))
    outs = pl.pallas_call(
        ff_backward_kernel,
        grid_spec=pltpu.PrefetchScalarGridSpec(
            num_scalar_prefetch=1,
            grid=(4,),
            in_specs=[whole((rows // 4, width))] * 4 + [strip, strip, tall, tall, flat, anywhere()],
            out_specs=(whole((rows, 2 * UNITS)),) * 4
            + (whole((rows, width)), whole((rows // 2, width)), whole((rows // 2, width))),
            scratch_shapes=[pltpu.VMEM((rows, width), F32)],
        ),
        out_shape=(jax.ShapeDtypeStruct((rows, 2 * UNITS), BF),) * 4
        + (
            jax.ShapeDtypeStruct((rows, width), BF),
            jax.ShapeDtypeStruct((rows // 2, width), F32),
            jax.ShapeDtypeStruct((rows // 2, width), BF),
        ),
        compiler_params=pltpu.CompilerParams(vmem_limit_bytes=VMEM_GRANT),
        cost_estimate=pl.CostEstimate(
            flops=6 * rows * width * units, bytes_accessed=3 * 10**7, transcendentals=rows * units
        ),
        name="ff_backward",
    )(me[None], *parts, gate_pre, up_pre, w_gate, w_up, w_down, event)
    return outs[:4], outs[4], outs[5:]


def relative_rows(spots, stream):
    return jnp.concatenate(
        [stream[pl.ds(pl.multiple_of(spots[i], 64), 64)] for i in range(4)], axis=0
    )


def swapped(value):
    return jnp.concatenate([value[STRETCH:], value[:STRETCH]], axis=0)


def input_kernel(spots, stream, w_key, w_value, g_in, normed_out, mine, theirs):
    rows = relative_rows(spots, stream).astype(F32)
    normed_out[...] = (rows * rms(rows) * g_in[...]).astype(BF)
    key, value = dot(normed_out[...], w_key[...]), dot(normed_out[...], w_value[...])
    first = spots[4] == 0
    mine[...] = jnp.where(first, key, value)
    theirs[...] = swapped(jnp.where(first, value, key))


def kind_kernel(spots, mine, came, cosine, sine, gain, low_out, full_out):
    first = spots[4] == 0
    kind = jnp.concatenate(
        [jnp.where(first, mine[...], came[...]), jnp.where(first, came[...], mine[...])], axis=1
    )
    full_out[...] = kind
    turn = (jnp.where(first, cosine[...], 1.0), jnp.where(first, sine[...], 0.0))
    scaled = kind * rms(kind) * jnp.where(first, gain[...], 1.0)
    low_out[...] = rotate(scaled, *turn).astype(BF)


def lay_kernel(*refs):
    for h in range(2):
        for i in range(4):
            refs[8 + h][256 * i : 256 * (i + 1)] = refs[4 * h + i][...]


def kind_back_kernel(spots, sums_a, sums_b, came, kind_ref, cosine, sine, gain, home, away, gains):
    first = spots[4] == 0
    turn = (jnp.where(first, cosine[...], 1.0), jnp.where(first, -sine[...], 0.0))
    grad = jnp.concatenate([sums_a[...] + came[0].astype(F32), sums_b[...] + came[1].astype(F32)], axis=0)
    kind = kind_ref[...]
    scale = rms(kind)
    grad, gain_part = norm_back(
        rotate(grad, *turn), kind * scale, scale, jnp.where(first, gain[...], 1.0)
    )
    gains[...] = jnp.where(first, gain_part, 0.0)
    half = HEAD // 2
    home[...] = jnp.where(first, grad[:, :half], grad[:, half:]).astype(BF)
    away[...] = swapped(jnp.where(first, grad[:, half:], grad[:, :half])).astype(BF)


def query_kernel(normed, w_query, cosine, sine, gain, event, low_out, raw_out):
    for head in range(2):
        at = slice(head * HEAD, (head + 1) * HEAD)
        raw = dot(normed[...], w_query[:, at])
        raw_out[:, at] = raw
        turned = rotate(raw * rms(raw) * gain[...], cosine[...], sine[...]).astype(BF)
        low_out[:, at] = (turned.astype(F32) * HEAD**-0.5).astype(BF)


def query_back_kernel(grad_ref, raw_ref, cosine, sine, gain, event, low_out, gains):
    gains[...] = jnp.zeros_like(gains)
    for head in range(2):
        at = slice(head * HEAD, (head + 1) * HEAD)
        raw = raw_ref[:, at]
        scale = rms(raw)
        grad, part = norm_back(
            rotate(grad_ref[:, at], cosine[...], -sine[...]), raw * scale, scale, gain[...]
        )
        low_out[:, at] = grad.astype(BF)
        gains[...] += part


def normed_back_kernel(spots, home, came, query, w_query, w_key, w_value, stream, *outs):
    kept, sent, gain_out, cuts = outs[0], outs[1], outs[2], outs[3:]
    first = spots[4] == 0
    key = jnp.where(first, home[...].astype(F32), came[...].astype(F32)).astype(BF)
    value = jnp.where(first, came[...].astype(F32), home[...].astype(F32)).astype(BF)
    part = dot_cols(query[...], w_query[...])
    part = part + dot_cols(key, w_key[...]) + dot_cols(value, w_value[...])
    kept[...] = part[:STRETCH]
    sent[...] = part[STRETCH:].astype(BF)
    rows = relative_rows(spots, stream).astype(F32)
    gain_out[...] = jnp.sum(part * (rows * rms(rows)), axis=0, keepdims=True)
    for k, cut in enumerate(cuts):
        at = spots[5] ^ k
        cut[:, :128] = query[:, pl.ds(pl.multiple_of(at * 128, 128), 128)]
        side = jnp.where(at >= 2, value.astype(F32), key.astype(F32))
        side = jnp.where((at & 1) == 1, side[:, 64:], side[:, :64])
        cut[:, 128:] = side.astype(BF)


def far_kernel(own, came, *refs):
    for i, out in enumerate(refs[-4:]):
        at = slice(4 * i, 4 * i + 4)
        out[...] = (own[at].astype(F32) + came[at].astype(F32)).astype(BF)


def near_kernel(own, came, *refs):
    passed, (base_a, base_b), sends = refs[:4], refs[4:6], refs[6:]

    def summed(first, count):
        at = slice(first, first + count)
        return own[at].astype(F32) + came[at].astype(F32)

    for h, base in enumerate((base_a, base_b)):
        near, other = sends[2 * h], sends[2 * h + 1]
        base[...] = summed(24 * h, 8)
        near[:4] = summed(24 * h + 8, 4).astype(BF)
        near[4:] = (summed(24 * h + 12, 4) + passed[2 * h + 1][...].astype(F32)).astype(BF)
        other[:4] = (summed(24 * h + 16, 4) + passed[2 * h][...].astype(F32)).astype(BF)
        other[4:] = summed(24 * h + 20, 4).astype(BF)


def inner_kernel(base_a, base_b, *refs):
    came, kept, sends = refs[:4], refs[4:6], refs[6:]
    for h, base in enumerate((base_a, base_b)):
        total = base[...] + came[2 * h][...].astype(F32) + came[2 * h + 1][...].astype(F32)
        kept[h][...] = total[:2]
        for k in (1, 2, 3):
            sends[3 * h + k - 1][...] = total[2 * k : 2 * k + 2].astype(BF)


def last_kernel(kept_a, kept_b, *refs):
    came, kept, send = refs[:6], refs[6:8], refs[8]
    for h, base in enumerate((kept_a, kept_b)):
        total = base[...]
        for k in range(3):
            total = total + came[3 * h + k][...].astype(F32)
        kept[h][...] = total[0]
        send[h] = total[1].astype(BF)


def mid_kernel(kept, came, stream, left, right, g_in, g_attn, g_laurel, g_pre, *outs):
    pre_out, resid_out, attn_out, laurel_out, low_out = outs
    rows = stream[...].astype(F32)
    normed = rows * rms(rows) * g_in[...]
    attn = kept[...] + came[...].astype(F32)
    low = dot_cols(normed.astype(BF), left[...])
    laurel = fine(low, right[...])
    resid = (
        rows + attn * rms(attn) * g_attn[...] + normed + laurel * rms(laurel) * g_laurel[...]
    ) * ROOT_HALF
    pre_out[...] = (resid * rms(resid) * g_pre[...]).astype(BF)
    resid_out[...] = resid
    attn_out[...] = attn
    laurel_out[...] = laurel
    low_out[...] = low


def join_kernel(kept, came, resid, top, inputs, gate_t, proj, g_post, g_join, event, *outs):
    ff_out, after_out, results, gains, mine, theirs = outs
    ff = kept[...] + came[...].astype(F32)
    ff_scale = rms(ff)
    ff_normal = ff * ff_scale
    after = resid[...] + ff_normal * g_post[...]
    value, slope = gelu_parts(fine_cols(after, gate_t[...]))
    channels = inputs[...].astype(F32)
    joined = value * channels
    join = fine(joined, proj[...])
    join_scale = rms(join)
    join_normal = join * join_scale
    results[:, :D] = (after + join_normal * g_join[...]).astype(BF)
    grad = top[...].astype(F32)
    grad_join, gain_join = norm_back(grad, join_normal, join_scale, g_join[...])
    grad_joined = fine_cols(grad_join, proj[...])
    grad_pre = grad_joined * channels * slope
    results[:, D:] = (grad_joined * value).astype(BF)
    grad_after = grad + fine(grad_pre, gate_t[...])
    after_out[...] = grad_after
    grad_ff, gain_post = norm_back(grad_after, ff_normal, ff_scale, g_post[...])
    ff_out[...] = grad_ff.astype(BF)
    gains[...] = jnp.zeros_like(gains)
    gains[0:1] = gain_post
    gains[1:2] = gain_join
    low_gate = dot_rows(grad_pre.astype(BF), after.astype(BF)).astype(BF)
    low_proj = dot_rows(joined.astype(BF), grad_join.astype(BF)).astype(BF)
    for k, (out, i) in enumerate(((mine, 0), (theirs, 0), (mine, 1), (theirs, 1))):
        out[i, :64] = low_gate[64 * k : 64 * (k + 1)]
        out[i, 64:] = low_proj[64 * k : 64 * (k + 1)]


def resid_kernel(
    kept,
    came,
    resid,
    after,
    attn,
    laurel,
    low,
    stream,
    left,
    right,
    g_in,
    g_attn,
    g_laurel,
    g_pre,
    gates_mine,
    gates_sent,
    *refs,
):
    attn_out, branch_out, own_out, gains, mine, theirs = refs[-6:]
    mine[:, 32:] = gates_mine[...]
    theirs[:, 32:] = gates_sent[...]
    scale = rms(resid[...])
    grad = kept[...] + came[...].astype(F32)
    grad_resid, gain_pre = norm_back(grad, resid[...] * scale, scale, g_pre[...])
    branch = (after[...] + grad_resid) * ROOT_HALF
    branch_out[...] = branch
    scale = rms(attn[...])
    grad_attn, gain_attn = norm_back(branch, attn[...] * scale, scale, g_attn[...])
    attn_out[...] = grad_attn.astype(BF)
    scale = rms(laurel[...])
    grad_laurel, gain_laurel = norm_back(branch, laurel[...] * scale, scale, g_laurel[...])
    grad_low = fine_cols(grad_laurel, right[...])
    own = branch + fine(grad_low, left[...])
    own_out[...] = own
    rows = stream[...].astype(F32)
    normal = rows * rms(rows)
    gains[...] = jnp.zeros_like(gains)
    gains[0:1] = gain_attn
    gains[1:2] = gain_laurel
    gains[2:3] = gain_pre
    gains[3:4] = jnp.sum(own * normal, axis=0, keepdims=True)
    low_left = dot_rows(grad_low.astype(BF), (normal * g_in[...]).astype(BF)).astype(BF)
    low_right = dot_rows(low[...].astype(BF), grad_laurel.astype(BF)).astype(BF)
    for k, (out, i) in enumerate(((mine, 0), (theirs, 0), (mine, 1), (theirs, 1))):
        out[i, :16] = low_left[16 * k : 16 * (k + 1)]
        out[i, 16:32] = low_right[16 * k : 16 * (k + 1)]


def final_kernel(kept, came, own, branch, stream, g_in, out):
    rows = stream[...].astype(F32)
    scale = rms(rows)
    grad = own[...] + kept[...] + came[...].astype(F32)
    extra, _ = norm_back(grad, rows * scale, scale, g_in[...])
    out[...] = (branch[...] + extra).astype(BF)


def in_one(kernel, shapes, args, name, event=(), spots=()):
    return pl.pallas_call(
        kernel,
        out_shape=tuple(jax.ShapeDtypeStruct(shape, kind) for shape, kind in shapes),
        in_specs=[pl.BlockSpec(memory_space=pltpu.SMEM)] * len(spots)
        + [in_vmem()] * len(args)
        + [anywhere()] * len(event),
        out_specs=(in_vmem(),) * len(shapes),
        compiler_params=pltpu.CompilerParams(vmem_limit_bytes=VMEM_GRANT),
        cost_estimate=pl.CostEstimate(flops=10**9, bytes_accessed=5 * 10**6, transcendentals=10**5),
        name=name,
    )(*spots, *args, *event)


def pack_kernel(left, right, gate_w, proj, inputs, event, out):
    unit = (
        lax.broadcasted_iota(jnp.int32, (64, 64), 0) == lax.broadcasted_iota(jnp.int32, (64, 64), 1)
    ).astype(BF)
    out[:16] = dot_cols(unit[:16, :16], left[...]).astype(BF)
    out[16:32] = right[...]
    out[32:96] = dot_cols(unit, gate_w[...]).astype(BF)
    out[96:160] = proj[...]
    turned = dot_cols(unit, inputs[...]).astype(BF)
    out[160:] = jnp.zeros_like(out[160:])
    for i in range(4):
        out[160:, 256 * i : 256 * (i + 1)] = turned[16 * i : 16 * (i + 1)]


Y_FIRST = (0, 3, 1, 2)
Y_OTHER = (0, 1, 3, 2)


def group_sum(me, group, cuts, at, size):
    total = None
    for k, cut in enumerate(cuts):
        term = dot_rows(group[me ^ k, :, pl.ds(pl.multiple_of(at, size), size)], cut)
        total = term if total is None else total + term
    return total


def wide_kernel(where, group, *refs):
    cuts, (gate_kept, gate_sent, up_kept, up_sent) = refs[:4], refs[-4:]
    x, y, z = where[0], where[1], where[2]
    half = cuts[0].shape[1] // 2
    for i, far_y in enumerate(Y_FIRST):
        j = Y_OTHER.index(far_y)
        for far_z in range(2):
            at = ((y ^ far_y) * 2 + (z ^ far_z)) * 256
            total = group_sum(x, group, [cut[...] for cut in cuts], at, 256).astype(BF)
            (gate_kept, gate_sent)[far_z][i] = total[:, :half]
            (up_kept, up_sent)[far_z][j] = total[:, half:]


def wide_product(where, group, cuts, event):
    shapes = [(4, 256, cuts[0].shape[1] // 2)] * 4
    return pl.pallas_call(
        wide_kernel,
        out_shape=tuple(jax.ShapeDtypeStruct(shape, BF) for shape in shapes),
        in_specs=[pl.BlockSpec(memory_space=pltpu.SMEM)] + [in_vmem()] * 5 + [anywhere()],
        out_specs=(in_vmem(),) * 4,
        compiler_params=pltpu.CompilerParams(vmem_limit_bytes=VMEM_GRANT),
        cost_estimate=pl.CostEstimate(flops=5 * 10**9, bytes_accessed=10**7, transcendentals=0),
        name="wide_product",
    )(where, group, *cuts, event)


def turn_kernel(where, small, event, kept, sent):
    y, z = where[1], where[2]
    low = small.shape[0]
    unit = (
        lax.broadcasted_iota(jnp.int32, (low, low), 0)
        == lax.broadcasted_iota(jnp.int32, (low, low), 1)
    ).astype(BF)
    for i, far_y in enumerate(Y_FIRST):
        for far_z in range(2):
            at = ((y ^ far_y) * 2 + (z ^ far_z)) * 256
            at = pl.ds(pl.multiple_of(at, 256), 256)
            (kept, sent)[far_z][i] = dot_rows(small[:, at], unit).astype(BF)


def token_kernel(where, group, gains, *refs):
    cuts, (kept, sent) = refs[:4], refs[4:]
    x, y, z = where[0], where[1], where[2]
    unit = (
        lax.broadcasted_iota(jnp.int32, (16, 64), 0) == lax.broadcasted_iota(jnp.int32, (16, 64), 1)
    ).astype(BF)
    for i, far_y in enumerate(Y_FIRST):
        for far_z in range(2):
            at = ((y ^ far_y) * 2 + (z ^ far_z)) * 256
            total = group_sum(x, group, [cut[...] for cut in cuts], at, 256)
            more = dot_rows(gains[:, pl.ds(pl.multiple_of(at, 256), 256)], unit)
            total = jnp.concatenate([total, more], axis=1).astype(BF)
            (kept, sent)[i // 2][i % 2, far_z] = total


def token_product(where, group, gains, cuts):
    shape = (2, 2, 256, cuts[0].shape[1] + 64)
    return pl.pallas_call(
        token_kernel,
        out_shape=(jax.ShapeDtypeStruct(shape, BF),) * 2,
        in_specs=[pl.BlockSpec(memory_space=pltpu.SMEM)] + [in_vmem()] * 6,
        out_specs=(in_vmem(),) * 2,
        compiler_params=pltpu.CompilerParams(vmem_limit_bytes=VMEM_GRANT),
        cost_estimate=pl.CostEstimate(flops=10**9, bytes_accessed=6 * 10**6, transcendentals=0),
        name="token_product",
    )(where, group, gains, *cuts)


def cut_kernel(where, ff_ref, *refs):
    parts, cuts = refs[:4], refs[5:]
    for k, cut in enumerate(cuts):
        at = pl.ds(pl.multiple_of((where[1] ^ k) * 512, 512), 512)
        cut[:, :512] = ff_ref[:, at]
        for i, part in enumerate(parts):
            cut[64 * i : 64 * (i + 1), 512:] = part[:, at]


def width_cuts(where, grad_ff, parts, event):
    rows = grad_ff.shape[0]
    return pl.pallas_call(
        cut_kernel,
        out_shape=(jax.ShapeDtypeStruct((rows, 1024), BF),) * 4,
        in_specs=[pl.BlockSpec(memory_space=pltpu.SMEM)] + [in_vmem()] * 5 + [anywhere()],
        out_specs=(in_vmem(),) * 4,
        compiler_params=pltpu.CompilerParams(vmem_limit_bytes=VMEM_GRANT),
        cost_estimate=pl.CostEstimate(flops=0, bytes_accessed=6 * 10**6, transcendentals=0),
        name="width_cuts",
    )(where, grad_ff, *parts, event)


def down_kernel(where, group, *refs):
    cuts, kept, sent, total = refs[:4], refs[5], refs[6], refs[7]
    x, y, z = where[0], where[1], where[2]
    units = group.shape[2]
    for first in range(0, units, 512):
        side = 0 if first < units - 512 else 512
        value = None
        for k, cut in enumerate(cuts):
            term = dot_rows(cut[:, side : side + 512], group[y ^ k, :, first : first + 512])
            value = term if value is None else value + term
        total[...] = value
        for i, far_x in enumerate(Y_FIRST):
            for far_z in range(2):
                at = pl.multiple_of(((z ^ far_z) * 4 + (x ^ far_x)) * 64, 64)
                rows = total[pl.ds(at, 64)].astype(BF)
                (kept, sent)[far_z][i, :, first : first + 512] = rows


def down_product(where, group, cuts, event):
    shape = (4, 64, group.shape[2])
    return pl.pallas_call(
        down_kernel,
        out_shape=(jax.ShapeDtypeStruct(shape, BF),) * 2,
        in_specs=[pl.BlockSpec(memory_space=pltpu.SMEM)] + [in_vmem()] * 5 + [anywhere()],
        out_specs=(in_vmem(),) * 2,
        scratch_shapes=[pltpu.VMEM((512, 512), F32)],
        compiler_params=pltpu.CompilerParams(vmem_limit_bytes=VMEM_GRANT),
        cost_estimate=pl.CostEstimate(flops=3 * 10**9, bytes_accessed=10**7, transcendentals=0),
        name="down_product",
    )(where, group, *cuts, event)


def local(
    stream,
    layer_input,
    out_grad,
    doc_lengths,
    stretch_slots,
    gain_input,
    gain_query,
    gain_key,
    w_query,
    w_key,
    w_value,
    w_attn_out,
    gain_attn,
    laurel_left,
    laurel_right,
    gain_laurel,
    gain_pre_ff,
    w_gate,
    w_up,
    w_down,
    gain_post_ff,
    join_gate,
    join_proj,
    gain_join,
):
    wt = lax.axis_index("wt")
    core, zlo = wt & 1, wt >> 1
    ctx = lax.axis_index("ctx")
    at_x, at_z, at_y = ctx & 3, (ctx >> 2) & 1, ctx >> 3
    first_core = core == 0
    half = HEAD // 2

    def starts(k):
        return ((core ^ (k & 1)) * 2 + (zlo ^ (k >> 1))) * 64

    def natural(blocks):
        stacked = jnp.stack(blocks)
        return jnp.concatenate(
            [pick(stacked, wt ^ ((b & 1) * 2 + (b >> 1)), 0) for b in range(4)], axis=0
        )

    stream_own = lax.dynamic_slice_in_dim(stream, starts(0), 64, 0)
    grad_top = lax.dynamic_slice_in_dim(out_grad, starts(0), 64, 0)
    where = jnp.stack([at_x, at_y, at_z])
    spots = (jnp.stack([starts(0), starts(2), starts(1), starts(3), core, at_x]),)
    g_in, g_attn, g_laurel, g_pre, g_post, g_join = (
        gain[None, :]
        for gain in (gain_input, gain_attn, gain_laurel, gain_pre_ff, gain_post_ff, gain_join)
    )

    doc_ends = jnp.cumsum(doc_lengths)
    tiles = [lax.dynamic_index_in_dim(stretch_slots, 2 * ctx + (core ^ t), 0) for t in range(2)]
    hi = jnp.concatenate(tiles)
    lo = jnp.max(
        jnp.where(doc_ends[None, :] <= hi[:, None] * STRETCH, doc_ends[None, :], 0), axis=1
    )
    lo = lo // STRETCH
    row = (jnp.arange(STRETCH, dtype=jnp.int32) + 64 * zlo) & (STRETCH - 1)
    positions = (hi[:, None] * STRETCH + row[None, :]).reshape(-1)
    names = jnp.arange(SLOTS, dtype=jnp.int32)
    slot_of = jnp.sum(jnp.where(stretch_slots[None, :] == names[:, None], names[None, :], 0), axis=1)
    relative = (slot_of >> 1) ^ ctx
    rel_x, rel_z, rel_y = relative & 3, (relative >> 2) & 1, relative >> 3
    places = (
        (rel_y ^ (rel_y >> 1)) * 8 + rel_x * 2 + rel_z,
        SLOTS // 2 + (rel_x ^ (rel_x >> 1)) * 8 + rel_y * 2 + rel_z,
    )
    second = (slot_of & 1) == 1
    key_at = core * SLOTS + jnp.where(second, places[1], places[0])
    value_at = (1 - core) * SLOTS + jnp.where(second, places[0], places[1])
    blank = jnp.zeros((PAD_SLOTS - SLOTS,), jnp.int32)
    meta = jnp.concatenate([key_at, blank, value_at, blank, hi, lo, zlo[None], doc_ends]).astype(
        jnp.int32
    )
    exponents = jnp.arange(half, dtype=F32) * (2.0 / HEAD)
    angles = positions.astype(F32)[:, None] * (1.0 / ROPE_BASE**exponents)[None, :]
    cosine, sine = jnp.cos(angles), jnp.sin(angles)

    half_rows, heads_b = ((2 * STRETCH, half), F32), ((2 * STRETCH, 2 * HEAD), BF)
    normed_b, mine, theirs = in_one(
        input_kernel,
        (((2 * STRETCH, D), BF), half_rows, half_rows),
        (stream, w_key, w_value, g_in),
        "input",
        spots=spots,
    )
    kind_b, kind = in_one(
        kind_kernel,
        (((2 * STRETCH, HEAD), BF), ((2 * STRETCH, HEAD), F32)),
        (mine, hop(theirs, "wt", 1), cosine, sine, gain_key[None, :]),
        "kind",
        spots=spots,
    )

    across = hop(kind_b, "ctx", 4)
    groups = []
    for h, one in enumerate((1, 8)):
        rows = slice(h * STRETCH, (h + 1) * STRETCH)
        block = jnp.concatenate([kind_b[rows], across[rows]], axis=0)
        groups.append([block] + [hop(block, "ctx", k * one) for k in (1, 2, 3)])
    quads = in_one(lay_kernel, (((1024, HEAD), BF),) * 2, (*groups[0], *groups[1]), "lay")
    pieces = ring_gather(quads[0], 8, 24) + ring_gather(quads[1], 1, 3)
    pieces += [hop(piece, "wt", 1) for piece in pieces]
    pieces = [piece.reshape(-1, STRETCH, HEAD) for piece in pieces]

    (pack,) = in_one(
        pack_kernel,
        (((176, D), BF),),
        (laurel_left, laurel_right, join_gate, join_proj, layer_input),
        "pack",
        (quads[0],),
    )
    packs = lax.all_gather(pack, "wt", axis=0)

    query_b, query_raw = in_one(
        query_kernel,
        (heads_b, ((2 * STRETCH, 2 * HEAD), F32)),
        (normed_b, w_query, cosine, sine, gain_query[None, :]),
        "query",
        (pieces[0],),
    )

    attn_b, attn_full, lse, kept, sent = attend_forward(meta, query_b, w_attn_out, pieces)

    kept, came = scatter_wt(kept, sent)

    def from_packs(first, last):
        return jnp.concatenate([pick(packs, wt ^ k, 0)[first:last] for k in range(4)], axis=0)

    left_t, right_w = from_packs(0, 16), from_packs(16, 32)
    gate_t, proj_w = from_packs(32, 96), from_packs(96, 160)
    inputs = packs[:, 160:, :1024].reshape(4, 16, 4, 256).transpose(0, 2, 1, 3)
    inputs = lax.dynamic_slice_in_dim(inputs.reshape(4, 64, 256), starts(0), 64, 2)
    inputs = jnp.concatenate([pick(inputs, wt ^ k, 0) for k in range(4)], axis=0).T
    normed_group = gather_group(normed_b, GROUP_X)
    wide_f, wide_b = ((64, D), F32), ((64, D), BF)
    pre_b, resid, attn_sum, laurel_sum, laurel_mid = in_one(
        mid_kernel,
        (wide_b, wide_f, wide_f, wide_f, ((64, 64), F32)),
        (kept, came, stream_own, left_t, right_w, g_in, g_attn, g_laurel, g_pre),
        "mid",
    )

    gate_pre, up_pre, pre_all, act_attn, kept, sent = ff_forward(
        gather_wt(pre_b), attn_b, w_gate, w_up, w_down
    )
    kept, came = scatter_wt(kept, sent)
    pre_group = gather_group(pre_all, GROUP_X)
    act_group = gather_group(act_attn, GROUP_Y)

    grad_ff, grad_after, results, gains_join, gates_mine, gates_sent = in_one(
        join_kernel,
        (
            wide_b,
            wide_f,
            ((64, D + 256), BF),
            ((8, D), F32),
            ((2, 128, D), BF),
            ((2, 128, D), BF),
        ),
        (kept, came, resid, grad_top, inputs, gate_t, proj_w, g_post, g_join),
        "join",
        (normed_group,),
    )

    grad_ff_parts = gather_wt(grad_ff)
    wide_cuts, grad_ff_all, (kept, sent) = ff_backward(
        at_x, grad_ff_parts, gate_pre, up_pre, w_gate, w_up, w_down, resid
    )
    kept, came = scatter_wt(kept, sent)
    wide_cuts = [wide_cuts[0]] + [hop(wide_cuts[k], "ctx", k) for k in (1, 2, 3)]

    def spread(parts):
        first, near, core_rows, far = parts
        return natural([first, core_rows, near, far]).astype(F32)

    results = lax.all_gather(results, "wt", axis=0)
    layer_out_all = jnp.concatenate([results[i, :, :D] for i in (0, 2, 1, 3)]).astype(F32)
    grad_input_all = jnp.concatenate(
        [
            lax.dynamic_slice_in_dim(results[i], D + 64 * (wt ^ i), 64, 1)
            for i in (0, 2, 1, 3)
        ]
    ).astype(F32)

    grad_attn, branch, own_part, gains_resid, small_mine, small_sent = in_one(
        resid_kernel,
        (wide_b, wide_f, wide_f, ((8, D), F32), ((2, 160, D), BF), ((2, 160, D), BF)),
        (
            kept,
            came,
            resid,
            grad_after,
            attn_sum,
            laurel_sum,
            laurel_mid,
            stream_own,
            left_t,
            right_w,
            g_in,
            g_attn,
            g_laurel,
            g_pre,
            gates_mine,
            gates_sent,
        ),
        "resid",
        (pre_group, *wide_cuts[1:]),
    )
    grad_attn_parts = gather_wt(grad_attn)
    down_cuts = width_cuts(where, grad_ff_all, grad_attn_parts, grad_attn)
    down_cuts = [down_cuts[0]] + [hop(down_cuts[k], "ctx", 8 * k) for k in (1, 2, 3)]
    small = small_mine.astype(F32) + hop(small_sent, "wt", 1).astype(F32)
    small_far = small[1].astype(BF)
    small = (small[0] + hop(small_far, "wt", 2).astype(F32)).astype(BF)

    grad_query_rot, grad_pieces = attend_backward(
        meta, query_b, attn_full, lse, w_attn_out, grad_attn_parts, pieces, down_cuts[0], small_far
    )
    def blocks(count, kind):
        return ((count, STRETCH, HEAD), kind)

    def hops(values, masks):
        return [hop(value, "ctx", mask) for value, mask in zip(values, masks)]

    own_far, own_rest, sent_far, sent_rest = grad_pieces
    came_rest = hop(sent_rest, "wt", 1)
    far = in_one(
        far_kernel,
        (blocks(4, BF),) * 4,
        (own_far, hop(sent_far, "wt", 1)),
        "far",
        (*down_cuts[1:], came_rest),
    )
    bases = in_one(
        near_kernel,
        (blocks(8, F32),) * 2 + (blocks(8, BF),) * 4,
        (own_rest, came_rest, *hops(far, (8, 24, 1, 3))),
        "near",
    )
    inner = in_one(
        inner_kernel,
        (blocks(2, F32),) * 2 + (blocks(2, BF),) * 6,
        (*bases[:2], *hops(bases[2:], (8, 24, 1, 3))),
        "inner",
    )
    last = in_one(
        last_kernel,
        (((STRETCH, HEAD), F32),) * 2 + (blocks(2, BF),),
        (*inner[:2], *hops(inner[2:], (1, 2, 3, 8, 16, 24))),
        "last",
    )
    across = hop(last[2], "ctx", 4)
    home, away, gain_key_part = in_one(
        kind_back_kernel,
        (((2 * STRETCH, half), BF), ((2 * STRETCH, half), BF), ((1, HEAD), F32)),
        (*last[:2], across, kind, cosine, sine, gain_key[None, :]),
        "kind_back",
        spots=spots,
    )
    grad_query_b, gain_query_part = in_one(
        query_back_kernel,
        (heads_b, ((1, HEAD), F32)),
        (grad_query_rot, query_raw, cosine, sine, gain_query[None, :]),
        "query_back",
        (far[0],),
    )

    outs = in_one(
        normed_back_kernel,
        (((STRETCH, D), F32), ((STRETCH, D), BF), ((1, D), F32))
        + (((2 * STRETCH, 192), BF),) * 4,
        (home, hop(away, "wt", 1), grad_query_b, w_query, w_key, w_value, stream),
        "normed_back",
        spots=spots,
    )
    kept, sent, gain_input_part, token_cuts = outs[0], outs[1], outs[2], outs[3:]
    kept, came = scatter_wt(kept, sent)
    (stream_grad,) = in_one(
        final_kernel, (wide_b,), (kept, came, own_part, branch, stream_own, g_in), "final"
    )

    stream_grad_all = spread(gather_wt(stream_grad))
    gate_kept, gate_sent, up_kept, up_sent = wide_product(
        where, pre_group, wide_cuts, grad_attn
    )
    gate = fold(gate_kept, gate_sent, 4)
    (up_sent,) = hold((up_sent,), gate)
    up = fold(up_kept, up_sent, 4)
    kept, sent = in_one(
        turn_kernel, (((4, 256, 160), BF),) * 2, (small,), "turn", (far[0],), spots=(where,)
    )
    (sent,) = hold((sent,), up)
    small = fold(kept, sent, 4)
    z_event = small
    gate, up, small = hold((gate, up, small), last[2])
    gate = jnp.concatenate([gate, small], axis=2)
    gate = fold(gate[:2], gate[2:], 8)
    gate = fold(gate[0], gate[1], 24)
    up = fold(up[:2], up[2:], 24)
    up = fold(up[0], up[1], 8)

    def exchange_x(value):
        value = value.reshape(4, 64, -1)
        stacked = jnp.stack(
            [pick(value, at_x, 0)] + [hop(pick(value, at_x ^ k, 0), "ctx", k) for k in (1, 2, 3)]
        )
        return [pick(stacked, at_x ^ q, 0) for q in range(4)]

    down_kept, down_sent = down_product(where, act_group, down_cuts, bases[2])
    (down_sent,) = hold((down_sent,), z_event)
    down = fold(down_kept, down_sent, 4)
    down = fold(down[:2], down[2:], 1)
    down = (down[0].astype(F32) + hop(down[1], "ctx", 3).astype(F32)).T
    grad_w_down, grad_w_attn_out = down[:2048], down[2048:]

    heads = jnp.concatenate(
        [gain_query_part.reshape(32, 8), gain_key_part.reshape(32, 8), jnp.zeros((32, 48), F32)],
        axis=1,
    ).reshape(1, -1)
    line = jnp.arange(8)[:, None]
    late_gains = jnp.where(line == 0, heads, 0.0) + jnp.where(
        line == 1, gain_input_part, 0.0
    )
    late_gains = jnp.concatenate(
        [late_gains + jnp.roll(gains_join, 2, axis=0), gains_resid], axis=0
    )

    token_cuts = [token_cuts[0]] + [hop(token_cuts[k], "ctx", k) for k in (1, 2, 3)]
    tokens = fold(*token_product(where, normed_group, late_gains.astype(BF), token_cuts), 8)
    tokens = fold(tokens[0], tokens[1], 24)
    tokens = fold(tokens[0], tokens[1], 4)
    shares = exchange_x(jnp.concatenate([gate, up, tokens], axis=1))
    small = sum([share[:, 512:672].astype(F32) for share in shares])
    grad_left, grad_right = small[:, :16], small[:, 16:32].T
    grad_gate, grad_proj = small[:, 32:96], small[:, 96:160].T

    def columns(first, last):
        return jnp.concatenate([share[:, first:last] for share in shares], axis=1).astype(F32)

    grad_w_gate, grad_w_up, grad_w_query = columns(0, 512), columns(672, 1184), columns(1184, 1312)
    grad_pair = columns(1312, 1376)
    grad_w_key, grad_w_value = grad_pair[:, :half], grad_pair[:, half:]
    gains = sum([share[:, 1376:1392].astype(F32) for share in shares])
    gains = gains + hop(gains, "wt", 1)
    gains = gains + hop(gains, "wt", 2)

    return (
        layer_out_all,
        stream_grad_all,
        grad_input_all,
        gains[:, 1] + gains[:, 11],
        gains[:8, 0],
        gains[8:16, 0],
        grad_w_query,
        grad_w_key,
        grad_w_value,
        grad_w_attn_out,
        gains[:, 8],
        grad_left,
        grad_right,
        gains[:, 9],
        gains[:, 10],
        grad_w_gate,
        grad_w_up,
        grad_w_down,
        gains[:, 2],
        grad_gate,
        grad_proj,
        gains[:, 3],
    )


def solution(mesh):
    rows, cols, tops = P("ctx", "wt"), P("wt", "ctx"), P("ctx")
    down, across = P(None, "wt"), P("wt", None)
    return jax.shard_map(
        local,
        mesh=mesh,
        in_specs=(
            P("ctx", None),
            P("ctx", "wt"),
            P("ctx", None),
            P(),
            P(),
            P(),
            P(),
            P(),
            down,
            down,
            down,
            across,
            P(),
            down,
            across,
            P(),
            P(),
            down,
            down,
            across,
            P(),
            down,
            across,
            P(),
        ),
        out_specs=(
            P("ctx", None),
            P("ctx", None),
            rows,
            tops,
            tops,
            tops,
            rows,
            rows,
            rows,
            cols,
            tops,
            rows,
            cols,
            tops,
            tops,
            rows,
            rows,
            cols,
            tops,
            rows,
            cols,
            tops,
        ),
        check_vma=False,
    )
```

```python
import jax
import jax.numpy as jnp
from jax import lax
from jax.experimental import pallas as pl
from jax.experimental.pallas import tpu as pltpu
from jax.sharding import PartitionSpec as P

EPS = 1e-06
ROPE_BASE = 1000000.0
ROOT_HALF = 0.7071067811865476
GELU_A = 0.7978845608028654
GELU_B = 0.044715
STRETCH = 128
HEAD = 256
SLOTS = 64
PAD_SLOTS = 72
CHUNK = 4
D = 2048
VMEM_GRANT = 60 * 1024 * 1024
BF = jnp.bfloat16
F32 = jnp.float32


def hop(value, axis, mask):
    return lax.ppermute(value, axis, [(i, i ^ mask) for i in range(lax.axis_size(axis))])


def pick(value, index, axis):
    return lax.dynamic_index_in_dim(value, index, axis, keepdims=False)


def ctx_of(y, z, x):
    return (y * 2 + z) * 4 + x


GROUP_X = [[ctx_of(y, z, x) for x in range(4)] for y in range(4) for z in range(2)]
GROUP_Y = [[ctx_of(y, z, x) for y in range(4)] for z in range(2) for x in range(4)]
GROUP_Z = [[ctx_of(y, z, x) for z in range(2)] for y in range(4) for x in range(4)]


def gather_group(value, groups):
    return lax.all_gather(value, "ctx", axis=0, axis_index_groups=groups)


def scatter_group(value, groups):
    return lax.psum_scatter(
        value, "ctx", scatter_dimension=0, axis_index_groups=groups, tiled=True
    )


def gate_kernel(*refs):
    pass


def hold(values, event):
    return pl.pallas_call(
        gate_kernel,
        out_shape=tuple(jax.ShapeDtypeStruct(value.shape, value.dtype) for value in values),
        in_specs=[pl.BlockSpec(memory_space=pl.ANY)] * (len(values) + 1),
        out_specs=(pl.BlockSpec(memory_space=pl.ANY),) * len(values),
        input_output_aliases={i: i for i in range(len(values))},
        name="gate",
    )(*values, event)


def ring_gather(block, near, other):
    one = hop(block, "ctx", near)
    two = hop(block, "ctx", other)
    half = block.shape[0] // 2
    return [
        block,
        one,
        two,
        hop(one[:half], "ctx", other),
        hop(two[half:], "ctx", near),
    ]


def gather_wt(own):
    near = hop(own, "wt", 2)
    core = hop(own, "wt", 1)
    far = hop(near, "wt", 1)
    return own, near, core, far


def scatter_wt(kept, sent):
    kept = kept + hop(sent, "wt", 1).astype(F32)
    quarter = kept.shape[0] // 2
    return kept[:quarter], hop(kept[quarter:].astype(BF), "wt", 2)


def fold(kept, sent, mask):
    return (kept.astype(F32) + hop(sent, "ctx", mask).astype(F32)).astype(BF)


def swap_halves(value):
    half = value.shape[0] // 2
    return jnp.concatenate([value[half:], value[:half]], axis=0)


def dot(left, right):
    return jnp.dot(left, right, preferred_element_type=F32)


def dot_rows(left, right):
    return lax.dot_general(left, right, (((0,), (0,)), ((), ())), preferred_element_type=F32)


def dot_cols(left, right):
    return lax.dot_general(left, right, (((1,), (1,)), ((), ())), preferred_element_type=F32)


def halves_of(value):
    high = value.astype(BF)
    return high, (value - high.astype(F32)).astype(BF)


def fine(left, right):
    high, low = halves_of(left)
    return dot(high, right) + dot(low, right)


def fine_cols(left, right):
    high, low = halves_of(left)
    return dot_cols(high, right) + dot_cols(low, right)


def rms(values):
    return lax.rsqrt(jnp.mean(values * values, axis=-1, keepdims=True) + EPS)


def norm_back(grad, normal, scale, gain):
    inner = grad * gain
    back = scale * (inner - normal * jnp.mean(inner * normal, axis=-1, keepdims=True))
    return back, jnp.sum(grad * normal, axis=0, keepdims=grad.ndim == 2)


def rotate(values, cosine, sine):
    half = values.shape[-1] // 2
    front, rear = values[..., :half], values[..., half:]
    return jnp.concatenate([front * cosine - rear * sine, rear * cosine + front * sine], axis=-1)


def gelu_parts(value):
    square = value * value
    bend = jnp.tanh(GELU_A * value * (1.0 + GELU_B * square))
    half = 0.5 * (1.0 + bend)
    slope = half + 0.5 * value * (1.0 - bend * bend) * GELU_A * (1.0 + 3.0 * GELU_B * square)
    return value * half, slope


AT_V = PAD_SLOTS
AT_HI = 2 * PAD_SLOTS
AT_LO = AT_HI + 2
AT_Z = AT_LO + 2
AT_ENDS = AT_Z + 1


def piece_copies(pieces, held, sem):
    copies, at = [], 0
    for i, piece in enumerate(pieces):
        count = piece.shape[0]
        place = held.at[pl.ds(at, count)]
        copies.append(pltpu.make_async_copy(piece, place, sem.at[i]))
        at += count
    return copies


def load_pieces(pieces, held, sem):
    copies = piece_copies(pieces, held, sem)
    for copy in copies:
        copy.start()
    for copy in copies:
        copy.wait()


def query_places(meta, tile, shape, along):
    row = lax.broadcasted_iota(jnp.int32, shape, along) & (STRETCH - 1)
    row = (row + 64 * meta[AT_Z]) & (STRETCH - 1)
    place = meta[AT_HI + tile] * STRETCH + row
    start = jnp.zeros(shape, jnp.int32)
    for j in range(8):
        end = meta[AT_ENDS + j]
        start = jnp.maximum(start, jnp.where(place >= end, end, 0))
    return place, start


def key_places(meta, first, shape, along):
    at = lax.broadcasted_iota(jnp.int32, shape, along)
    row = ((at & (STRETCH - 1)) + 64 * meta[AT_Z]) & (STRETCH - 1)
    return first * STRETCH + (at - (at & (STRETCH - 1))) + row


def tile_of(ref, tile):
    rows = pl.ds(tile * STRETCH, STRETCH)
    return jnp.concatenate([ref[rows, :HEAD], ref[rows, HEAD:]], axis=0)


def stretches(meta, held, at, first):
    return jnp.concatenate([held[meta[at + first + u]] for u in range(CHUNK)], axis=0)


def turns_of(meta, tile):
    return (meta[AT_HI + tile] - meta[AT_LO + tile] + CHUNK) // CHUNK


def forward_kernel(meta, q_ref, w_ref, *refs):
    pieces, (low_ref, full_ref, lse_ref, kept_ref, sent_ref) = refs[:20], refs[20:25]
    held, acc, total, sem = refs[25:]
    load_pieces(pieces, held, sem)
    for tile in range(2):
        query = tile_of(q_ref, tile)
        place, start = query_places(meta, tile, (2 * STRETCH, 1), 0)
        acc[...] = jnp.zeros_like(acc)
        total[...] = jnp.zeros_like(total)

        def turn(i, carry):
            first = meta[AT_LO + tile] + CHUNK * i
            keys = stretches(meta, held, 0, first)
            values = stretches(meta, held, AT_V, first)
            scores = dot_cols(query, keys)
            key_at = key_places(meta, first, (1, CHUNK * STRETCH), 1)
            allowed = (key_at <= place) & (key_at >= start)
            weights = jnp.where(allowed, jnp.exp(scores), 0.0)
            part = weights[:, :STRETCH]
            for u in range(1, CHUNK):
                part = part + weights[:, u * STRETCH : (u + 1) * STRETCH]
            total[...] += part
            acc[...] += dot(weights.astype(BF), values)
            return carry

        lax.fori_loop(0, turns_of(meta, tile), turn, 0)
        row_total = jnp.sum(total[...], axis=1, keepdims=True)
        result = acc[...] / row_total
        rows = pl.ds(tile * STRETCH, STRETCH)
        for head in range(2):
            block = result[head * STRETCH : (head + 1) * STRETCH]
            low_ref[rows, head * HEAD : (head + 1) * HEAD] = block.astype(BF)
            full_ref[rows, head * HEAD : (head + 1) * HEAD] = block
        logs = jnp.broadcast_to(jnp.log(row_total), (2 * STRETCH, STRETCH))
        lse_ref[tile] = jnp.transpose(logs)[:8]
    kept_ref[...] = dot(low_ref[:STRETCH], w_ref[...])
    sent_ref[...] = dot(low_ref[STRETCH:], w_ref[...]).astype(BF)


def backward_kernel(meta, q_ref, full_ref, lse_ref, w_ref, *refs):
    parts, pieces, dq_ref, outs = refs[:4], refs[4:24], refs[-10], refs[-9:-5]
    held, grads, acc, g_ref, sem = refs[-5:]
    copies = piece_copies(pieces, held, sem)
    for copy in copies:
        copy.start()
    for i, part in enumerate(parts):
        g_ref[64 * i : 64 * (i + 1)] = dot_cols(part[...], w_ref[...]).astype(BF)
    grads[...] = jnp.zeros_like(grads)
    for copy in copies:
        copy.wait()
    for tile in range(2):
        query = tile_of(q_ref, tile)
        grad = tile_of(g_ref, tile)
        full = tile_of(full_ref, tile)
        place, start = query_places(meta, tile, (1, 2 * STRETCH), 1)
        lse = lse_ref[tile][:1]
        delta = jnp.sum(grad.astype(F32) * full, axis=1, keepdims=True)
        delta = jnp.transpose(jnp.broadcast_to(delta, (2 * STRETCH, STRETCH)))[:1]
        acc[...] = jnp.zeros_like(acc)

        def turn(i, carry):
            first = meta[AT_LO + tile] + CHUNK * i
            keys = stretches(meta, held, 0, first)
            values = stretches(meta, held, AT_V, first)
            key_at = key_places(meta, first, (CHUNK * STRETCH, 1), 0)
            allowed = (key_at <= place) & (key_at >= start)
            weights = jnp.where(allowed, jnp.exp(dot_cols(keys, query) - lse), 0.0)
            slopes = (weights * (dot_cols(values, grad) - delta)).astype(BF)
            key_term = dot(slopes, query)
            value_term = dot(weights.astype(BF), grad)
            acc[...] += dot_rows(slopes, keys)
            for u in range(CHUNK):
                part = slice(u * STRETCH, (u + 1) * STRETCH)
                for at, term in ((meta[first + u], key_term), (meta[AT_V + first + u], value_term)):
                    grads[at] = (grads[at].astype(F32) + term[part]).astype(BF)
            return carry

        lax.fori_loop(0, turns_of(meta, tile), turn, 0)
        rows = pl.ds(tile * STRETCH, STRETCH)
        for head in range(2):
            block = acc[head * STRETCH : (head + 1) * STRETCH]
            dq_ref[rows, head * HEAD : (head + 1) * HEAD] = block * (HEAD**-0.5)
    copies = []
    for side in range(2):
        for h in range(2):
            at = 64 * side + 32 * h
            for out, first, count, begin in ((0, 24, 8, 8 * h), (1, 0, 24, 24 * h)):
                copies.append(
                    pltpu.make_async_copy(
                        grads.at[pl.ds(at + first, count)],
                        outs[2 * side + out].at[pl.ds(begin, count)],
                        sem.at[len(copies)],
                    )
                )
    for copy in copies:
        copy.start()
    for copy in copies:
        copy.wait()


def in_vmem():
    return pl.BlockSpec(memory_space=pltpu.VMEM)


def anywhere():
    return pl.BlockSpec(memory_space=pl.ANY)


def attend_forward(meta, query, w_attn_out, pieces):
    rows, width = query.shape[0], w_attn_out.shape[1]
    return pl.pallas_call(
        forward_kernel,
        out_shape=(
            jax.ShapeDtypeStruct((rows, 2 * HEAD), BF),
            jax.ShapeDtypeStruct((rows, 2 * HEAD), F32),
            jax.ShapeDtypeStruct((2, 8, 2 * STRETCH), F32),
            jax.ShapeDtypeStruct((STRETCH, width), F32),
            jax.ShapeDtypeStruct((STRETCH, width), BF),
        ),
        in_specs=[pl.BlockSpec(memory_space=pltpu.SMEM), in_vmem(), in_vmem()] + [anywhere()] * 20,
        out_specs=(in_vmem(),) * 5,
        scratch_shapes=[
            pltpu.VMEM((2 * SLOTS, STRETCH, HEAD), BF),
            pltpu.VMEM((2 * STRETCH, HEAD), F32),
            pltpu.VMEM((2 * STRETCH, STRETCH), F32),
            pltpu.SemaphoreType.DMA((20,)),
        ],
        compiler_params=pltpu.CompilerParams(vmem_limit_bytes=VMEM_GRANT),
        cost_estimate=pl.CostEstimate(
            flops=3 * 10**9, bytes_accessed=10**7, transcendentals=2 * 10**6
        ),
        name="attend_forward",
    )(meta, query, w_attn_out, *pieces)


def attend_backward(meta, query, full, lse, w_attn_out, parts, pieces, *events):
    rows = query.shape[0]
    outs = pl.pallas_call(
        backward_kernel,
        out_shape=(jax.ShapeDtypeStruct((rows, 2 * HEAD), F32),)
        + tuple(jax.ShapeDtypeStruct((count, STRETCH, HEAD), BF) for count in (16, 48, 16, 48)),
        in_specs=[pl.BlockSpec(memory_space=pltpu.SMEM)] + [in_vmem()] * 8
        + [anywhere()] * (20 + len(events)),
        out_specs=(in_vmem(),) + (anywhere(),) * 4,
        scratch_shapes=[
            pltpu.VMEM((2 * SLOTS, STRETCH, HEAD), BF),
            pltpu.VMEM((2 * SLOTS, STRETCH, HEAD), BF),
            pltpu.VMEM((2 * STRETCH, HEAD), F32),
            pltpu.VMEM((rows, 2 * HEAD), BF),
            pltpu.SemaphoreType.DMA((20,)),
        ],
        compiler_params=pltpu.CompilerParams(vmem_limit_bytes=VMEM_GRANT),
        cost_estimate=pl.CostEstimate(
            flops=10**10, bytes_accessed=2 * 10**7, transcendentals=2 * 10**6
        ),
        name="attend_backward",
    )(meta, query, full, lse, w_attn_out, *parts, *pieces, *events)
    return outs[0], outs[1:]


UNITS = 512


def ff_forward_kernel(*refs):
    parts, (w_gate, w_up, w_down) = refs[:4], refs[4:7]
    gate_out, up_out, pre_out, act_out, kept, sent = refs[7:13]
    now, acc = refs[13:]
    turn = pl.program_id(0)

    @pl.when(turn == 0)
    def first():
        for i, part in enumerate(parts):
            pre_out[64 * i : 64 * (i + 1)] = part[...]
        acc[...] = jnp.zeros_like(acc)

    gate = dot(pre_out[...], w_gate[...])
    up = dot(pre_out[...], w_up[...])
    gate_out[...] = gate
    up_out[...] = up
    now[...] = (gelu_parts(gate)[0] * up).astype(BF)
    act_out[...] = now[...]
    acc[...] += dot(now[...], w_down[...])

    @pl.when(turn == pl.num_programs(0) - 1)
    def last():
        kept[...] = acc[:STRETCH]
        sent[...] = acc[STRETCH:].astype(BF)


def ff_forward(parts, w_gate, w_up, w_down):
    width, units = w_gate.shape
    rows = 4 * parts[0].shape[0]
    whole = lambda shape: pl.BlockSpec(shape, lambda i: (0, 0))
    tall, flat = pl.BlockSpec((width, UNITS), lambda i: (0, i)), pl.BlockSpec((UNITS, width), lambda i: (i, 0))
    strip = pl.BlockSpec((rows, UNITS), lambda i: (0, i))
    return pl.pallas_call(
        ff_forward_kernel,
        grid=(units // UNITS,),
        out_shape=(
            jax.ShapeDtypeStruct((rows, units), F32),
            jax.ShapeDtypeStruct((rows, units), F32),
            jax.ShapeDtypeStruct((rows, width), BF),
            jax.ShapeDtypeStruct((rows, units), BF),
            jax.ShapeDtypeStruct((rows // 2, width), F32),
            jax.ShapeDtypeStruct((rows // 2, width), BF),
        ),
        in_specs=[whole((rows // 4, width))] * 4 + [tall, tall, flat],
        out_specs=(
            strip,
            strip,
            whole((rows, width)),
            strip,
            whole((rows // 2, width)),
            whole((rows // 2, width)),
        ),
        scratch_shapes=[pltpu.VMEM((rows, UNITS), BF), pltpu.VMEM((rows, width), F32)],
        compiler_params=pltpu.CompilerParams(vmem_limit_bytes=VMEM_GRANT),
        cost_estimate=pl.CostEstimate(
            flops=6 * rows * width * units, bytes_accessed=3 * 10**7, transcendentals=rows * units
        ),
        name="ff_forward",
    )(*parts, w_gate, w_up, w_down)


def ff_grads_kernel(me, *refs):
    parts, (gate_ref, up_ref, w_down) = refs[:4], refs[4:7]
    cuts, quarters, all_in = refs[7:11], refs[11:15], refs[15]
    block = pl.program_id(0)

    @pl.when(block == 0)
    def first():
        for i, part in enumerate(parts):
            all_in[64 * i : 64 * (i + 1)] = part[...]
        for k in range(4):
            at = pl.multiple_of((me[1] ^ k) * 512, 512)
            quarters[k][...] = all_in[:, pl.ds(at, 512)]

    grad_act = dot_cols(all_in[...], w_down[...])
    value, slope = gelu_parts(gate_ref[...])
    for k in range(4):

        @pl.when(block == k)
        def store():
            cuts[k][:, :UNITS] = (grad_act * up_ref[...] * slope).astype(BF)
            cuts[k][:, UNITS:] = (grad_act * value).astype(BF)


def ff_grads(me, parts, gate_pre, up_pre, w_down):
    units, width = w_down.shape
    rows = gate_pre.shape[0]
    whole = lambda shape: pl.BlockSpec(shape, lambda k, me: (0, 0))
    flat = pl.BlockSpec((UNITS, width), lambda k, me: (k ^ me[0], 0))
    strip = pl.BlockSpec((rows, UNITS), lambda k, me: (0, k ^ me[0]))
    outs = pl.pallas_call(
        ff_grads_kernel,
        grid_spec=pltpu.PrefetchScalarGridSpec(
            num_scalar_prefetch=1,
            grid=(4,),
            in_specs=[whole((rows // 4, width))] * 4 + [strip, strip, flat],
            out_specs=(whole((rows, 2 * UNITS)),) * 4 + (whole((rows, width // 4)),) * 4,
            scratch_shapes=[pltpu.VMEM((rows, width), BF)],
        ),
        out_shape=(jax.ShapeDtypeStruct((rows, 2 * UNITS), BF),) * 4
        + (jax.ShapeDtypeStruct((rows, width // 4), BF),) * 4,
        compiler_params=pltpu.CompilerParams(vmem_limit_bytes=VMEM_GRANT),
        cost_estimate=pl.CostEstimate(
            flops=2 * rows * width * units, bytes_accessed=10**7, transcendentals=rows * units
        ),
        name="ff_grads",
    )(me, *parts, gate_pre, up_pre, w_down)
    return outs[:4], outs[4:]


def ff_back_kernel(me, *refs):
    cuts, (w_gate, w_up, kept, sent, acc) = refs[:4], refs[4:]
    block = pl.program_id(0)

    @pl.when(block == 0)
    def first():
        acc[...] = jnp.zeros_like(acc)

    for k in range(4):

        @pl.when(block == k)
        def add():
            term = dot_cols(cuts[k][:, :UNITS], w_gate[...])
            acc[...] += term + dot_cols(cuts[k][:, UNITS:], w_up[...])

    @pl.when(block == 3)
    def last():
        kept[...] = acc[:STRETCH]
        sent[...] = acc[STRETCH:].astype(BF)


def ff_back(me, cuts, w_gate, w_up):
    width, units = w_gate.shape
    rows = cuts[0].shape[0]
    whole = lambda shape: pl.BlockSpec(shape, lambda k, me: (0, 0))
    tall = pl.BlockSpec((width, UNITS), lambda k, me: (0, k ^ me[0]))
    return pl.pallas_call(
        ff_back_kernel,
        grid_spec=pltpu.PrefetchScalarGridSpec(
            num_scalar_prefetch=1,
            grid=(4,),
            in_specs=[whole((rows, 2 * UNITS))] * 4 + [tall, tall],
            out_specs=(whole((rows // 2, width)),) * 2,
            scratch_shapes=[pltpu.VMEM((rows, width), F32)],
        ),
        out_shape=(
            jax.ShapeDtypeStruct((rows // 2, width), F32),
            jax.ShapeDtypeStruct((rows // 2, width), BF),
        ),
        compiler_params=pltpu.CompilerParams(vmem_limit_bytes=VMEM_GRANT),
        cost_estimate=pl.CostEstimate(
            flops=4 * rows * width * units, bytes_accessed=2 * 10**7, transcendentals=0
        ),
        name="ff_back",
    )(me, *cuts, w_gate, w_up)


def relative_rows(spots, stream):
    return jnp.concatenate(
        [stream[pl.ds(pl.multiple_of(spots[i], 64), 64)] for i in range(4)], axis=0
    )


def swapped(value):
    return jnp.concatenate([value[STRETCH:], value[:STRETCH]], axis=0)


def input_kernel(spots, stream, w_key, w_value, g_in, normed_out, mine, theirs):
    rows = relative_rows(spots, stream).astype(F32)
    normed_out[...] = (rows * rms(rows) * g_in[...]).astype(BF)
    key, value = dot(normed_out[...], w_key[...]), dot(normed_out[...], w_value[...])
    first = spots[4] == 0
    mine[...] = jnp.where(first, key, value)
    theirs[...] = swapped(jnp.where(first, value, key))


def kind_kernel(spots, mine, came, cosine, sine, gain, low_out, full_out):
    first = spots[4] == 0
    kind = jnp.concatenate(
        [jnp.where(first, mine[...], came[...]), jnp.where(first, came[...], mine[...])], axis=1
    )
    full_out[...] = kind
    turn = (jnp.where(first, cosine[...], 1.0), jnp.where(first, sine[...], 0.0))
    scaled = kind * rms(kind) * jnp.where(first, gain[...], 1.0)
    low_out[...] = rotate(scaled, *turn).astype(BF)


def lay_kernel(*refs):
    for h in range(2):
        for i in range(4):
            refs[8 + h][256 * i : 256 * (i + 1)] = refs[4 * h + i][...]


def kind_back_kernel(spots, sums_a, sums_b, came, kind_ref, cosine, sine, gain, event, home, away, gains):
    first = spots[4] == 0
    turn = (jnp.where(first, cosine[...], 1.0), jnp.where(first, -sine[...], 0.0))
    grad = jnp.concatenate([sums_a[...] + came[0].astype(F32), sums_b[...] + came[1].astype(F32)], axis=0)
    kind = kind_ref[...]
    scale = rms(kind)
    grad, gain_part = norm_back(
        rotate(grad, *turn), kind * scale, scale, jnp.where(first, gain[...], 1.0)
    )
    gains[...] = jnp.where(first, gain_part, 0.0)
    half = HEAD // 2
    home[...] = jnp.where(first, grad[:, :half], grad[:, half:]).astype(BF)
    away[...] = swapped(jnp.where(first, grad[:, half:], grad[:, :half])).astype(BF)


def query_kernel(normed, w_query, cosine, sine, gain, event, low_out, raw_out):
    for head in range(2):
        at = slice(head * HEAD, (head + 1) * HEAD)
        raw = dot(normed[...], w_query[:, at])
        raw_out[:, at] = raw
        turned = rotate(raw * rms(raw) * gain[...], cosine[...], sine[...]).astype(BF)
        low_out[:, at] = (turned.astype(F32) * HEAD**-0.5).astype(BF)


def query_back_kernel(grad_ref, raw_ref, cosine, sine, gain, event, low_out, gains):
    gains[...] = jnp.zeros_like(gains)
    for head in range(2):
        at = slice(head * HEAD, (head + 1) * HEAD)
        raw = raw_ref[:, at]
        scale = rms(raw)
        grad, part = norm_back(
            rotate(grad_ref[:, at], cosine[...], -sine[...]), raw * scale, scale, gain[...]
        )
        low_out[:, at] = grad.astype(BF)
        gains[...] += part


def normed_back_kernel(spots, home, came, query, w_query, w_key, w_value, stream, *outs):
    kept, sent, gain_out, cuts = outs[-7], outs[-6], outs[-5], outs[-4:]
    first = spots[4] == 0
    key = jnp.where(first, home[...].astype(F32), came[...].astype(F32)).astype(BF)
    value = jnp.where(first, came[...].astype(F32), home[...].astype(F32)).astype(BF)
    part = dot_cols(query[...], w_query[...])
    part = part + dot_cols(key, w_key[...]) + dot_cols(value, w_value[...])
    kept[...] = part[:STRETCH]
    sent[...] = part[STRETCH:].astype(BF)
    rows = relative_rows(spots, stream).astype(F32)
    gain_out[...] = jnp.sum(part * (rows * rms(rows)), axis=0, keepdims=True)
    for k, cut in enumerate(cuts):
        at = spots[5] ^ k
        cut[:, :128] = query[:, pl.ds(pl.multiple_of(at * 128, 128), 128)]
        side = jnp.where(at >= 2, value.astype(F32), key.astype(F32))
        side = jnp.where((at & 1) == 1, side[:, 64:], side[:, :64])
        cut[:, 128:] = side.astype(BF)


def far_kernel(own, came, *refs):
    for i, out in enumerate(refs[-4:]):
        at = slice(4 * i, 4 * i + 4)
        out[...] = (own[at].astype(F32) + came[at].astype(F32)).astype(BF)


def near_kernel(own, came, *refs):
    passed, (base_a, base_b), sends = refs[:4], refs[-6:-4], refs[-4:]

    def summed(first, count):
        at = slice(first, first + count)
        return own[at].astype(F32) + came[at].astype(F32)

    for h, base in enumerate((base_a, base_b)):
        near, other = sends[2 * h], sends[2 * h + 1]
        base[...] = summed(24 * h, 8)
        near[:4] = summed(24 * h + 8, 4).astype(BF)
        near[4:] = (summed(24 * h + 12, 4) + passed[2 * h + 1][...].astype(F32)).astype(BF)
        other[:4] = (summed(24 * h + 16, 4) + passed[2 * h][...].astype(F32)).astype(BF)
        other[4:] = summed(24 * h + 20, 4).astype(BF)


def inner_kernel(base_a, base_b, *refs):
    came, kept, sends = refs[:4], refs[-8:-6], refs[-6:]
    for h, base in enumerate((base_a, base_b)):
        total = base[...] + came[2 * h][...].astype(F32) + came[2 * h + 1][...].astype(F32)
        kept[h][...] = total[:2]
        for k in (1, 2, 3):
            sends[3 * h + k - 1][...] = total[2 * k : 2 * k + 2].astype(BF)


def last_kernel(kept_a, kept_b, *refs):
    came, kept, send = refs[:6], refs[6:8], refs[8]
    for h, base in enumerate((kept_a, kept_b)):
        total = base[...]
        for k in range(3):
            total = total + came[3 * h + k][...].astype(F32)
        kept[h][...] = total[0]
        send[h] = total[1].astype(BF)


def mid_kernel(kept, came, stream, left, right, g_in, g_attn, g_laurel, g_pre, *outs):
    pre_out, resid_out, attn_out, laurel_out, low_out = outs
    rows = stream[...].astype(F32)
    normed = rows * rms(rows) * g_in[...]
    attn = kept[...] + came[...].astype(F32)
    low = dot_cols(normed.astype(BF), left[...])
    laurel = fine(low, right[...])
    resid = (
        rows + attn * rms(attn) * g_attn[...] + normed + laurel * rms(laurel) * g_laurel[...]
    ) * ROOT_HALF
    pre_out[...] = (resid * rms(resid) * g_pre[...]).astype(BF)
    resid_out[...] = resid
    attn_out[...] = attn
    laurel_out[...] = laurel
    low_out[...] = low


def join_kernel(kept, came, resid, top, inputs, gate_t, proj, g_post, g_join, event, *outs):
    ff_out, after_out, results, gains, mine, theirs = outs
    ff = kept[...] + came[...].astype(F32)
    ff_scale = rms(ff)
    ff_normal = ff * ff_scale
    after = resid[...] + ff_normal * g_post[...]
    value, slope = gelu_parts(fine_cols(after, gate_t[...]))
    channels = inputs[...].astype(F32)
    joined = value * channels
    join = fine(joined, proj[...])
    join_scale = rms(join)
    join_normal = join * join_scale
    results[:, :D] = (after + join_normal * g_join[...]).astype(BF)
    grad = top[...].astype(F32)
    grad_join, gain_join = norm_back(grad, join_normal, join_scale, g_join[...])
    grad_joined = fine_cols(grad_join, proj[...])
    grad_pre = grad_joined * channels * slope
    results[:, D:] = (grad_joined * value).astype(BF)
    grad_after = grad + fine(grad_pre, gate_t[...])
    after_out[...] = grad_after
    grad_ff, gain_post = norm_back(grad_after, ff_normal, ff_scale, g_post[...])
    ff_out[...] = grad_ff.astype(BF)
    gains[...] = jnp.zeros_like(gains)
    gains[0:1] = gain_post
    gains[1:2] = gain_join
    low_gate = dot_rows(grad_pre.astype(BF), after.astype(BF)).astype(BF)
    low_proj = dot_rows(joined.astype(BF), grad_join.astype(BF)).astype(BF)
    for k, (out, i) in enumerate(((mine, 0), (theirs, 0), (mine, 1), (theirs, 1))):
        out[i, :64] = low_gate[64 * k : 64 * (k + 1)]
        out[i, 64:] = low_proj[64 * k : 64 * (k + 1)]


def resid_kernel(
    kept,
    came,
    resid,
    after,
    attn,
    laurel,
    low,
    stream,
    left,
    right,
    g_in,
    g_attn,
    g_laurel,
    g_pre,
    gates_mine,
    gates_sent,
    *refs,
):
    attn_out, branch_out, own_out, gains, mine, theirs = refs[-6:]
    mine[:, 32:] = gates_mine[...]
    theirs[:, 32:] = gates_sent[...]
    scale = rms(resid[...])
    grad = kept[...] + came[...].astype(F32)
    grad_resid, gain_pre = norm_back(grad, resid[...] * scale, scale, g_pre[...])
    branch = (after[...] + grad_resid) * ROOT_HALF
    branch_out[...] = branch
    scale = rms(attn[...])
    grad_attn, gain_attn = norm_back(branch, attn[...] * scale, scale, g_attn[...])
    attn_out[...] = grad_attn.astype(BF)
    scale = rms(laurel[...])
    grad_laurel, gain_laurel = norm_back(branch, laurel[...] * scale, scale, g_laurel[...])
    grad_low = fine_cols(grad_laurel, right[...])
    own = branch + fine(grad_low, left[...])
    own_out[...] = own
    rows = stream[...].astype(F32)
    normal = rows * rms(rows)
    gains[...] = jnp.zeros_like(gains)
    gains[0:1] = gain_attn
    gains[1:2] = gain_laurel
    gains[2:3] = gain_pre
    gains[3:4] = jnp.sum(own * normal, axis=0, keepdims=True)
    low_left = dot_rows(grad_low.astype(BF), (normal * g_in[...]).astype(BF)).astype(BF)
    low_right = dot_rows(low[...].astype(BF), grad_laurel.astype(BF)).astype(BF)
    for k, (out, i) in enumerate(((mine, 0), (theirs, 0), (mine, 1), (theirs, 1))):
        out[i, :16] = low_left[16 * k : 16 * (k + 1)]
        out[i, 16:32] = low_right[16 * k : 16 * (k + 1)]


def final_kernel(kept, came, own, branch, stream, g_in, event, out):
    rows = stream[...].astype(F32)
    scale = rms(rows)
    grad = own[...] + kept[...] + came[...].astype(F32)
    extra, _ = norm_back(grad, rows * scale, scale, g_in[...])
    out[...] = (branch[...] + extra).astype(BF)


def in_one(kernel, shapes, args, name, event=(), spots=(), scratch=()):
    return pl.pallas_call(
        kernel,
        out_shape=tuple(jax.ShapeDtypeStruct(shape, kind) for shape, kind in shapes),
        in_specs=[pl.BlockSpec(memory_space=pltpu.SMEM)] * len(spots)
        + [in_vmem()] * len(args)
        + [anywhere()] * len(event),
        out_specs=(in_vmem(),) * len(shapes),
        scratch_shapes=list(scratch),
        compiler_params=pltpu.CompilerParams(vmem_limit_bytes=VMEM_GRANT),
        cost_estimate=pl.CostEstimate(flops=10**9, bytes_accessed=5 * 10**6, transcendentals=10**5),
        name=name,
    )(*spots, *args, *event)


def pack_kernel(left, right, gate_w, proj, inputs, event, out):
    unit = (
        lax.broadcasted_iota(jnp.int32, (64, 64), 0) == lax.broadcasted_iota(jnp.int32, (64, 64), 1)
    ).astype(BF)
    out[:16] = dot_cols(unit[:16, :16], left[...]).astype(BF)
    out[16:32] = right[...]
    out[32:96] = dot_cols(unit, gate_w[...]).astype(BF)
    out[96:160] = proj[...]
    turned = dot_cols(unit, inputs[...]).astype(BF)
    out[160:] = jnp.zeros_like(out[160:])
    for i in range(4):
        out[160:, 256 * i : 256 * (i + 1)] = turned[16 * i : 16 * (i + 1)]


Y_FIRST = (0, 3, 1, 2)
Y_OTHER = (0, 1, 3, 2)


def group_sum(me, group, cuts, at, size):
    total = None
    for k, cut in enumerate(cuts):
        term = dot_rows(group[me ^ k, :, pl.ds(at, size)], cut)
        total = term if total is None else total + term
    return total


def wide_kernel(where, group, *refs):
    cuts, out = refs[:4], refs[-1]
    for at in range(0, D, 256):
        total = group_sum(where[0], group, [cut[...] for cut in cuts], at, 256)
        out[at : at + 256] = total.astype(BF)


def wide_product(where, group, cuts, event):
    return pl.pallas_call(
        wide_kernel,
        out_shape=jax.ShapeDtypeStruct((D, cuts[0].shape[1]), BF),
        in_specs=[pl.BlockSpec(memory_space=pltpu.SMEM)] + [in_vmem()] * 5 + [anywhere()],
        out_specs=in_vmem(),
        compiler_params=pltpu.CompilerParams(vmem_limit_bytes=VMEM_GRANT),
        cost_estimate=pl.CostEstimate(flops=5 * 10**9, bytes_accessed=10**7, transcendentals=0),
        name="wide_product",
    )(where, group, *cuts, event)


def turn_kernel(small, attn, *refs):
    parts, out, grads = refs[:4], refs[-2], refs[-1]
    low = small.shape[0]
    for i, part in enumerate(parts):
        grads[64 * i : 64 * (i + 1)] = part[...]
    unit = (
        lax.broadcasted_iota(jnp.int32, (low, 256), 0)
        == lax.broadcasted_iota(jnp.int32, (low, 256), 1)
    ).astype(BF)
    out[:, :512] = dot_rows(grads[...], attn[...]).astype(BF)
    out[:, 512:] = dot_rows(small[...], unit).astype(BF)


def token_kernel(where, group, gains, *refs):
    cuts, (kept, sent) = refs[:4], refs[4:]
    x, y, z = where[0], where[1], where[2]
    unit = (
        lax.broadcasted_iota(jnp.int32, (16, 64), 0) == lax.broadcasted_iota(jnp.int32, (16, 64), 1)
    ).astype(BF)
    for i, far_y in enumerate(Y_FIRST):
        for far_z in range(2):
            at = pl.multiple_of(((y ^ far_y) * 2 + (z ^ far_z)) * 256, 256)
            total = group_sum(x, group, [cut[...] for cut in cuts], at, 256)
            more = dot_rows(gains[:, pl.ds(at, 256)], unit)
            total = jnp.concatenate([total, more], axis=1).astype(BF)
            (kept, sent)[i // 2][i % 2, far_z] = total


def token_product(where, group, gains, cuts):
    shape = (2, 2, 256, cuts[0].shape[1] + 64)
    return pl.pallas_call(
        token_kernel,
        out_shape=(jax.ShapeDtypeStruct(shape, BF),) * 2,
        in_specs=[pl.BlockSpec(memory_space=pltpu.SMEM)] + [in_vmem()] * 6,
        out_specs=(in_vmem(),) * 2,
        compiler_params=pltpu.CompilerParams(vmem_limit_bytes=VMEM_GRANT),
        cost_estimate=pl.CostEstimate(flops=10**9, bytes_accessed=6 * 10**6, transcendentals=0),
        name="token_product",
    )(where, group, gains, *cuts)


def payload_kernel(where, wide, tokens, turn, *outs):
    for k, out in enumerate(outs):
        at = pl.ds(pl.multiple_of((where[0] ^ k) * 64, 64), 64)
        out[:, :1024] = wide[at]
        out[:, 1024:1280] = tokens[at]
        out[:, 1280:] = turn[at]


def share_kernel(where, *refs):
    shares, down_kept, down_came = refs[:4], refs[4], refs[5]
    gate, up, query, key, value, attn, left, right, join_g, join_p, gains, down = refs[6:]
    x = where[0]

    def turned(rows):
        rows = jnp.concatenate([rows, jnp.zeros_like(rows)], axis=0)
        return jnp.transpose(rows)[:, :64]

    for k, share in enumerate(shares):
        gate[:, pl.ds(pl.multiple_of((x ^ k) * 512, 512), 512)] = share[:, :512].astype(F32)
        up[:, pl.ds(pl.multiple_of((x ^ k) * 512, 512), 512)] = share[:, 512:1024].astype(F32)
        query[:, pl.ds(pl.multiple_of((x ^ k) * 128, 128), 128)] = share[:, 1024:1152].astype(F32)
    quarters = [share[:, 1152:1216].astype(F32) for share in shares]
    placed = []
    for q in range(4):
        choice = quarters[3]
        for k in range(3):
            choice = jnp.where((x ^ k) == q, quarters[k], choice)
        placed.append(choice)
    key[:, :64], key[:, 64:] = placed[0], placed[1]
    value[:, :64], value[:, 64:] = placed[2], placed[3]
    total = shares[0][:, 1216:].astype(F32)
    for share in shares[1:]:
        total = total + share[:, 1216:].astype(F32)
    gains[...] = total[:, :16]
    attn[...] = total[:, 64:576]
    small = total[:, 576:736]
    join_g[...] = small[:, 32:96]
    lines = turned(jnp.concatenate([small, jnp.zeros((64, 96), F32)], axis=1))
    left[...] = lines[:16]
    right[...] = lines[16:32]
    join_p[...] = lines[96:160]
    down[...] = down_kept[...].astype(F32) + down_came[...].astype(F32)


def down_kernel(where, group, *refs):
    cuts, out, total = refs[:4], refs[5], refs[6]
    x, y = where[0], where[1]
    units = group.shape[2]
    for first in range(0, units, 512):
        value = None
        for k, cut in enumerate(cuts):
            term = dot_rows(cut[...], group[y ^ k, :, first : first + 512])
            value = term if value is None else value + term
        total[...] = value
        for i, far_x in enumerate(Y_FIRST):
            for z in range(2):
                at = pl.multiple_of((z * 4 + (x ^ far_x)) * 64, 64)
                out[z, i, :, first : first + 512] = total[pl.ds(at, 64)].astype(BF)


def down_product(where, group, cuts, event):
    return pl.pallas_call(
        down_kernel,
        out_shape=jax.ShapeDtypeStruct((2, 4, 64, group.shape[2]), BF),
        in_specs=[pl.BlockSpec(memory_space=pltpu.SMEM)] + [in_vmem()] * 5 + [anywhere()],
        out_specs=in_vmem(),
        scratch_shapes=[pltpu.VMEM((512, 512), F32)],
        compiler_params=pltpu.CompilerParams(vmem_limit_bytes=VMEM_GRANT),
        cost_estimate=pl.CostEstimate(flops=3 * 10**9, bytes_accessed=10**7, transcendentals=0),
        name="down_product",
    )(where, group, *cuts, event)


def local(
    stream,
    layer_input,
    out_grad,
    doc_lengths,
    stretch_slots,
    gain_input,
    gain_query,
    gain_key,
    w_query,
    w_key,
    w_value,
    w_attn_out,
    gain_attn,
    laurel_left,
    laurel_right,
    gain_laurel,
    gain_pre_ff,
    w_gate,
    w_up,
    w_down,
    gain_post_ff,
    join_gate,
    join_proj,
    gain_join,
):
    wt = lax.axis_index("wt")
    core, zlo = wt & 1, wt >> 1
    ctx = lax.axis_index("ctx")
    at_x, at_z, at_y = ctx & 3, (ctx >> 2) & 1, ctx >> 3
    first_core = core == 0
    half = HEAD // 2

    def starts(k):
        return ((core ^ (k & 1)) * 2 + (zlo ^ (k >> 1))) * 64

    def natural(blocks):
        stacked = jnp.stack(blocks)
        return jnp.concatenate(
            [pick(stacked, wt ^ ((b & 1) * 2 + (b >> 1)), 0) for b in range(4)], axis=0
        )

    stream_own = lax.dynamic_slice_in_dim(stream, starts(0), 64, 0)
    grad_top = lax.dynamic_slice_in_dim(out_grad, starts(0), 64, 0)
    where = jnp.stack([at_x, at_y, at_z])
    spots = (jnp.stack([starts(0), starts(2), starts(1), starts(3), core, at_x]),)
    g_in, g_attn, g_laurel, g_pre, g_post, g_join = (
        gain[None, :]
        for gain in (gain_input, gain_attn, gain_laurel, gain_pre_ff, gain_post_ff, gain_join)
    )

    doc_ends = jnp.cumsum(doc_lengths)
    tiles = [lax.dynamic_index_in_dim(stretch_slots, 2 * ctx + (core ^ t), 0) for t in range(2)]
    hi = jnp.concatenate(tiles)
    lo = jnp.max(
        jnp.where(doc_ends[None, :] <= hi[:, None] * STRETCH, doc_ends[None, :], 0), axis=1
    )
    lo = lo // STRETCH
    row = (jnp.arange(STRETCH, dtype=jnp.int32) + 64 * zlo) & (STRETCH - 1)
    positions = (hi[:, None] * STRETCH + row[None, :]).reshape(-1)
    names = jnp.arange(SLOTS, dtype=jnp.int32)
    slot_of = jnp.sum(jnp.where(stretch_slots[None, :] == names[:, None], names[None, :], 0), axis=1)
    relative = (slot_of >> 1) ^ ctx
    rel_x, rel_z, rel_y = relative & 3, (relative >> 2) & 1, relative >> 3
    places = (
        (rel_y ^ (rel_y >> 1)) * 8 + rel_x * 2 + rel_z,
        SLOTS // 2 + (rel_x ^ (rel_x >> 1)) * 8 + rel_y * 2 + rel_z,
    )
    second = (slot_of & 1) == 1
    key_at = core * SLOTS + jnp.where(second, places[1], places[0])
    value_at = (1 - core) * SLOTS + jnp.where(second, places[0], places[1])
    blank = jnp.zeros((PAD_SLOTS - SLOTS,), jnp.int32)
    meta = jnp.concatenate([key_at, blank, value_at, blank, hi, lo, zlo[None], doc_ends]).astype(
        jnp.int32
    )
    exponents = jnp.arange(half, dtype=F32) * (2.0 / HEAD)
    angles = positions.astype(F32)[:, None] * (1.0 / ROPE_BASE**exponents)[None, :]
    cosine, sine = jnp.cos(angles), jnp.sin(angles)

    half_rows, heads_b = ((2 * STRETCH, half), F32), ((2 * STRETCH, 2 * HEAD), BF)
    normed_b, mine, theirs = in_one(
        input_kernel,
        (((2 * STRETCH, D), BF), half_rows, half_rows),
        (stream, w_key, w_value, g_in),
        "input",
        spots=spots,
    )
    kind_b, kind = in_one(
        kind_kernel,
        (((2 * STRETCH, HEAD), BF), ((2 * STRETCH, HEAD), F32)),
        (mine, hop(theirs, "wt", 1), cosine, sine, gain_key[None, :]),
        "kind",
        spots=spots,
    )

    across = hop(kind_b, "ctx", 4)
    groups = []
    for h, one in enumerate((1, 8)):
        rows = slice(h * STRETCH, (h + 1) * STRETCH)
        block = jnp.concatenate([kind_b[rows], across[rows]], axis=0)
        groups.append([block] + [hop(block, "ctx", k * one) for k in (1, 2, 3)])
    quads = in_one(lay_kernel, (((1024, HEAD), BF),) * 2, (*groups[0], *groups[1]), "lay")
    pieces = ring_gather(quads[0], 8, 24) + ring_gather(quads[1], 1, 3)
    pieces += [hop(piece, "wt", 1) for piece in pieces]
    pieces = [piece.reshape(-1, STRETCH, HEAD) for piece in pieces]

    (pack,) = in_one(
        pack_kernel,
        (((176, D), BF),),
        (laurel_left, laurel_right, join_gate, join_proj, layer_input),
        "pack",
        (quads[0],),
    )
    packs = lax.all_gather(pack, "wt", axis=0)

    query_b, query_raw = in_one(
        query_kernel,
        (heads_b, ((2 * STRETCH, 2 * HEAD), F32)),
        (normed_b, w_query, cosine, sine, gain_query[None, :]),
        "query",
        (pieces[0],),
    )

    attn_b, attn_full, lse, kept, sent = attend_forward(meta, query_b, w_attn_out, pieces)

    kept, came = scatter_wt(kept, sent)

    def from_packs(first, last):
        return jnp.concatenate([pick(packs, wt ^ k, 0)[first:last] for k in range(4)], axis=0)

    left_t, right_w = from_packs(0, 16), from_packs(16, 32)
    gate_t, proj_w = from_packs(32, 96), from_packs(96, 160)
    inputs = packs[:, 160:, :1024].reshape(4, 16, 4, 256).transpose(0, 2, 1, 3)
    inputs = lax.dynamic_slice_in_dim(inputs.reshape(4, 64, 256), starts(0), 64, 2)
    inputs = jnp.concatenate([pick(inputs, wt ^ k, 0) for k in range(4)], axis=0).T
    normed_group = gather_group(normed_b, GROUP_X)
    wide_f, wide_b = ((64, D), F32), ((64, D), BF)
    pre_b, resid, attn_sum, laurel_sum, laurel_mid = in_one(
        mid_kernel,
        (wide_b, wide_f, wide_f, wide_f, ((64, 64), F32)),
        (kept, came, stream_own, left_t, right_w, g_in, g_attn, g_laurel, g_pre),
        "mid",
    )

    gate_pre, up_pre, pre_all, act_b, kept, sent = ff_forward(
        gather_wt(pre_b), w_gate, w_up, w_down
    )
    kept, came = scatter_wt(kept, sent)
    pre_group = gather_group(pre_all, GROUP_X)
    act_group = gather_group(act_b, GROUP_Y)

    grad_ff, grad_after, results, gains_join, gates_mine, gates_sent = in_one(
        join_kernel,
        (
            wide_b,
            wide_f,
            ((64, D + 256), BF),
            ((8, D), F32),
            ((2, 128, D), BF),
            ((2, 128, D), BF),
        ),
        (kept, came, resid, grad_top, inputs, gate_t, proj_w, g_post, g_join),
        "join",
        (normed_group,),
    )

    grad_ff_parts = gather_wt(grad_ff)
    wide_cuts, down_cuts = ff_grads(where, grad_ff_parts, gate_pre, up_pre, w_down)
    kept, sent = ff_back(where, wide_cuts, w_gate, w_up)
    wide_cuts = [wide_cuts[0]] + [hop(wide_cuts[k], "ctx", k) for k in (1, 2, 3)]
    down_cuts = [down_cuts[0]] + [hop(down_cuts[k], "ctx", 8 * k) for k in (1, 2, 3)]
    kept, came = scatter_wt(kept, sent)

    grad_attn, branch, own_part, gains_resid, small_mine, small_sent = in_one(
        resid_kernel,
        (wide_b, wide_f, wide_f, ((8, D), F32), ((2, 160, D), BF), ((2, 160, D), BF)),
        (
            kept,
            came,
            resid,
            grad_after,
            attn_sum,
            laurel_sum,
            laurel_mid,
            stream_own,
            left_t,
            right_w,
            g_in,
            g_attn,
            g_laurel,
            g_pre,
            gates_mine,
            gates_sent,
        ),
        "resid",
        (pre_group,),
    )
    grad_attn_parts = gather_wt(grad_attn)

    grad_query_rot, grad_pieces = attend_backward(
        meta, query_b, attn_full, lse, w_attn_out, grad_attn_parts, pieces, *wide_cuts[1:]
    )
    wide = wide_product(where, pre_group, wide_cuts, grad_query_rot)
    def blocks(count, kind):
        return ((count, STRETCH, HEAD), kind)

    def hops(values, masks):
        return [hop(value, "ctx", mask) for value, mask in zip(values, masks)]

    own_far, own_rest, sent_far, sent_rest = grad_pieces
    came_rest = hop(sent_rest, "wt", 1)
    far = in_one(
        far_kernel,
        (blocks(4, BF),) * 4,
        (own_far, hop(sent_far, "wt", 1)),
        "far",
        (came_rest, wide),
    )
    wide = scatter_group(wide, GROUP_Y)
    down = down_product(where, act_group, down_cuts, far[0])
    grad_query_b, gain_query_part = in_one(
        query_back_kernel,
        (heads_b, ((1, HEAD), F32)),
        (grad_query_rot, query_raw, cosine, sine, gain_query[None, :]),
        "query_back",
        (far[0],),
    )
    bases = in_one(
        near_kernel,
        (blocks(8, F32),) * 2 + (blocks(8, BF),) * 4,
        (own_rest, came_rest, *hops(far, (8, 24, 1, 3))),
        "near",
    )
    (small_sent,) = hold((small_sent,), bases[2])
    small = small_mine.astype(F32) + hop(small_sent, "wt", 1).astype(F32)
    small_far = small[1].astype(BF)
    small = (small[0] + hop(small_far, "wt", 2).astype(F32)).astype(BF)
    down_event = down
    down = scatter_group(down, GROUP_Z).reshape(4, 64, -1)
    inner = in_one(
        inner_kernel,
        (blocks(2, F32),) * 2 + (blocks(2, BF),) * 6,
        (*bases[:2], *hops(bases[2:], (8, 24, 1, 3))),
        "inner",
        (grad_query_b, down_event),
    )
    last = in_one(
        last_kernel,
        (((STRETCH, HEAD), F32),) * 2 + (blocks(2, BF),),
        (*inner[:2], *hops(inner[2:], (1, 2, 3, 8, 16, 24))),
        "last",
    )
    across = hop(last[2], "ctx", 4)
    (turn,) = in_one(
        turn_kernel,
        (((D, 768), BF),),
        (small, attn_b, *grad_attn_parts),
        "turn",
        (last[2],),
        scratch=(pltpu.VMEM((2 * STRETCH, D), BF),),
    )
    turn_event = turn
    turn = scatter_group(turn, GROUP_Y)
    home, away, gain_key_part = in_one(
        kind_back_kernel,
        (((2 * STRETCH, half), BF), ((2 * STRETCH, half), BF), ((1, HEAD), F32)),
        (*last[:2], across, kind, cosine, sine, gain_key[None, :]),
        "kind_back",
        (turn_event,),
        spots=spots,
    )

    outs = in_one(
        normed_back_kernel,
        (((STRETCH, D), F32), ((STRETCH, D), BF), ((1, D), F32))
        + (((2 * STRETCH, 192), BF),) * 4,
        (home, hop(away, "wt", 1), grad_query_b, w_query, w_key, w_value, stream),
        "normed_back",
        (wide,),
        spots=spots,
    )
    def fold_z(value):
        value = value.reshape(2, 256, -1)
        return fold(pick(value, at_z, 0), pick(value, 1 - at_z, 0), 4)

    wide = fold_z(wide)
    turn = fold_z(turn)
    kept, sent, gain_input_part, token_cuts = outs[0], outs[1], outs[2], outs[3:]
    kept, came = scatter_wt(kept, sent)
    (stream_grad,) = in_one(
        final_kernel, (wide_b,), (kept, came, own_part, branch, stream_own, g_in), "final", (turn,)
    )

    first, near, core_rows, far_rows = gather_wt(stream_grad)
    stream_grad_all = natural([first, core_rows, near, far_rows]).astype(F32)
    heads = jnp.concatenate(
        [gain_query_part.reshape(32, 8), gain_key_part.reshape(32, 8), jnp.zeros((32, 48), F32)],
        axis=1,
    ).reshape(1, -1)
    line = jnp.arange(8)[:, None]
    late_gains = jnp.where(line == 0, heads, 0.0) + jnp.where(
        line == 1, gain_input_part, 0.0
    )
    late_gains = jnp.concatenate(
        [late_gains + jnp.roll(gains_join, 2, axis=0), gains_resid], axis=0
    )

    late_gains = late_gains + hop(late_gains, "wt", 1)
    late_gains = late_gains + hop(late_gains, "wt", 2)
    token_cuts = [token_cuts[0]] + [hop(token_cuts[k], "ctx", k) for k in (1, 2, 3)]
    (results,) = hold((results,), token_cuts[1])
    results = lax.all_gather(results, "wt", axis=0)
    layer_out_all = jnp.concatenate([results[i, :, :D] for i in (0, 2, 1, 3)]).astype(F32)
    grad_input_all = jnp.concatenate(
        [
            lax.dynamic_slice_in_dim(results[i], D + 64 * (wt ^ i), 64, 1)
            for i in (0, 2, 1, 3)
        ]
    ).astype(F32)

    (down,) = hold((down,), token_cuts[1])
    down = fold(down[:2], down[2:], 1)
    tokens = fold(*token_product(where, normed_group, late_gains.astype(BF), token_cuts), 8)
    tokens = fold(tokens[0], tokens[1], 24)
    tokens = fold(tokens[0], tokens[1], 4)
    shares = in_one(
        payload_kernel,
        (((64, 2048), BF),) * 4,
        (wide, tokens, turn),
        "payload",
        spots=(where,),
    )
    shares = [shares[0]] + [hop(shares[k], "ctx", k) for k in (1, 2, 3)]
    (
        grad_w_gate,
        grad_w_up,
        grad_w_query,
        grad_w_key,
        grad_w_value,
        grad_w_attn_out,
        grad_left,
        grad_right,
        grad_gate,
        grad_proj,
        gains,
        grad_w_down,
    ) = in_one(
        share_kernel,
        tuple(
            (shape, F32)
            for shape in (
                (64, D),
                (64, D),
                (64, 512),
                (64, half),
                (64, half),
                (64, 512),
                (16, 64),
                (16, 64),
                (64, 64),
                (64, 64),
                (64, 16),
                (64, D),
            )
        ),
        (*shares, down[0], hop(down[1], "ctx", 3)),
        "share",
        spots=(where,),
    )

    return (
        layer_out_all,
        stream_grad_all,
        grad_input_all,
        gains[:, 1] + gains[:, 11],
        gains[:8, 0],
        gains[8:16, 0],
        grad_w_query,
        grad_w_key,
        grad_w_value,
        grad_w_attn_out.T,
        gains[:, 8],
        grad_left.T,
        grad_right,
        gains[:, 9],
        gains[:, 10],
        grad_w_gate,
        grad_w_up,
        grad_w_down.T,
        gains[:, 2],
        grad_gate,
        grad_proj,
        gains[:, 3],
    )


def solution(mesh):
    rows, cols, tops = P("ctx", "wt"), P("wt", "ctx"), P("ctx")
    down, across = P(None, "wt"), P("wt", None)
    return jax.shard_map(
        local,
        mesh=mesh,
        in_specs=(
            P("ctx", None),
            P("ctx", "wt"),
            P("ctx", None),
            P(),
            P(),
            P(),
            P(),
            P(),
            down,
            down,
            down,
            across,
            P(),
            down,
            across,
            P(),
            P(),
            down,
            down,
            across,
            P(),
            down,
            across,
            P(),
        ),
        out_specs=(
            P("ctx", None),
            P("ctx", None),
            rows,
            tops,
            tops,
            tops,
            rows,
            rows,
            rows,
            cols,
            tops,
            rows,
            cols,
            tops,
            tops,
            rows,
            rows,
            cols,
            tops,
            rows,
            cols,
            tops,
        ),
        check_vma=False,
    )
```

```python
import jax
import jax.numpy as jnp
from jax import lax
from jax.experimental import pallas as pl
from jax.experimental.pallas import tpu as pltpu
from jax.sharding import PartitionSpec as P

EPS = 1e-06
ROPE_BASE = 1000000.0
ROOT_HALF = 0.7071067811865476
GELU_A = 0.7978845608028654
GELU_B = 0.044715
STRETCH = 128
HEAD = 256
SLOTS = 64
PAD_SLOTS = 72
CHUNK = 4
D = 2048
VMEM_GRANT = 60 * 1024 * 1024
BF = jnp.bfloat16
F32 = jnp.float32


def hop(value, axis, mask):
    return lax.ppermute(value, axis, [(i, i ^ mask) for i in range(lax.axis_size(axis))])


def pick(value, index, axis):
    return lax.dynamic_index_in_dim(value, index, axis, keepdims=False)


def ctx_of(y, z, x):
    return (y * 2 + z) * 4 + x


GROUP_X = [[ctx_of(y, z, x) for x in range(4)] for y in range(4) for z in range(2)]
GROUP_Y = [[ctx_of(y, z, x) for y in range(4)] for z in range(2) for x in range(4)]
GROUP_Z = [[ctx_of(y, z, x) for z in range(2)] for y in range(4) for x in range(4)]


def gather_group(value, groups):
    return lax.all_gather(value, "ctx", axis=0, axis_index_groups=groups)


def scatter_group(value, groups):
    return lax.psum_scatter(
        value, "ctx", scatter_dimension=0, axis_index_groups=groups, tiled=True
    )


def gate_kernel(*refs):
    pass


def hold(values, event):
    return pl.pallas_call(
        gate_kernel,
        out_shape=tuple(jax.ShapeDtypeStruct(value.shape, value.dtype) for value in values),
        in_specs=[pl.BlockSpec(memory_space=pl.ANY)] * (len(values) + 1),
        out_specs=(pl.BlockSpec(memory_space=pl.ANY),) * len(values),
        input_output_aliases={i: i for i in range(len(values))},
        name="gate",
    )(*values, event)


def ring_gather(block, near, other):
    one = hop(block, "ctx", near)
    two = hop(block, "ctx", other)
    half = block.shape[0] // 2
    return [
        block,
        one,
        two,
        hop(one[:half], "ctx", other),
        hop(two[half:], "ctx", near),
    ]


def gather_wt(own):
    near = hop(own, "wt", 2)
    core = hop(own, "wt", 1)
    far = hop(near, "wt", 1)
    return own, near, core, far


def scatter_wt(kept, sent):
    kept = kept + hop(sent, "wt", 1).astype(F32)
    quarter = kept.shape[0] // 2
    return kept[:quarter], hop(kept[quarter:].astype(BF), "wt", 2)


def fold(kept, sent, mask):
    return (kept.astype(F32) + hop(sent, "ctx", mask).astype(F32)).astype(BF)


def swap_halves(value):
    half = value.shape[0] // 2
    return jnp.concatenate([value[half:], value[:half]], axis=0)


def dot(left, right):
    return jnp.dot(left, right, preferred_element_type=F32)


def dot_rows(left, right):
    return lax.dot_general(left, right, (((0,), (0,)), ((), ())), preferred_element_type=F32)


def dot_cols(left, right):
    return lax.dot_general(left, right, (((1,), (1,)), ((), ())), preferred_element_type=F32)


def halves_of(value):
    high = value.astype(BF)
    return high, (value - high.astype(F32)).astype(BF)


def fine(left, right):
    high, low = halves_of(left)
    return dot(high, right) + dot(low, right)


def fine_cols(left, right):
    high, low = halves_of(left)
    return dot_cols(high, right) + dot_cols(low, right)


def rms(values):
    return lax.rsqrt(jnp.mean(values * values, axis=-1, keepdims=True) + EPS)


def norm_back(grad, normal, scale, gain):
    inner = grad * gain
    back = scale * (inner - normal * jnp.mean(inner * normal, axis=-1, keepdims=True))
    return back, jnp.sum(grad * normal, axis=0, keepdims=grad.ndim == 2)


def rotate(values, cosine, sine):
    half = values.shape[-1] // 2
    front, rear = values[..., :half], values[..., half:]
    return jnp.concatenate([front * cosine - rear * sine, rear * cosine + front * sine], axis=-1)


def gelu_parts(value):
    square = value * value
    bend = jnp.tanh(GELU_A * value * (1.0 + GELU_B * square))
    half = 0.5 * (1.0 + bend)
    slope = half + 0.5 * value * (1.0 - bend * bend) * GELU_A * (1.0 + 3.0 * GELU_B * square)
    return value * half, slope


AT_V = PAD_SLOTS
AT_HI = 2 * PAD_SLOTS
AT_LO = AT_HI + 2
AT_Z = AT_LO + 2
AT_ENDS = AT_Z + 1


def piece_copies(pieces, held, sem):
    copies, at = [], 0
    for i, piece in enumerate(pieces):
        count = piece.shape[0]
        place = held.at[pl.ds(at, count)]
        copies.append(pltpu.make_async_copy(piece, place, sem.at[i]))
        at += count
    return copies


def load_pieces(pieces, held, sem):
    copies = piece_copies(pieces, held, sem)
    for copy in copies:
        copy.start()
    for copy in copies:
        copy.wait()


def query_places(meta, tile, shape, along):
    row = lax.broadcasted_iota(jnp.int32, shape, along) & (STRETCH - 1)
    row = (row + 64 * meta[AT_Z]) & (STRETCH - 1)
    place = meta[AT_HI + tile] * STRETCH + row
    start = jnp.zeros(shape, jnp.int32)
    for j in range(8):
        end = meta[AT_ENDS + j]
        start = jnp.maximum(start, jnp.where(place >= end, end, 0))
    return place, start


def key_places(meta, first, shape, along):
    at = lax.broadcasted_iota(jnp.int32, shape, along)
    row = ((at & (STRETCH - 1)) + 64 * meta[AT_Z]) & (STRETCH - 1)
    return first * STRETCH + (at - (at & (STRETCH - 1))) + row


def tile_of(ref, tile):
    rows = pl.ds(tile * STRETCH, STRETCH)
    return jnp.concatenate([ref[rows, :HEAD], ref[rows, HEAD:]], axis=0)


def stretches(meta, held, at, first):
    return jnp.concatenate([held[meta[at + first + u]] for u in range(CHUNK)], axis=0)


def turns_of(meta, tile):
    return (meta[AT_HI + tile] - meta[AT_LO + tile] + CHUNK) // CHUNK


def forward_kernel(meta, q_ref, w_ref, *refs):
    pieces, (low_ref, full_ref, lse_ref, kept_ref, sent_ref) = refs[:20], refs[20:25]
    held, acc, total, sem = refs[25:]
    load_pieces(pieces, held, sem)
    for tile in range(2):
        query = tile_of(q_ref, tile)
        place, start = query_places(meta, tile, (2 * STRETCH, 1), 0)
        acc[...] = jnp.zeros_like(acc)
        total[...] = jnp.zeros_like(total)

        def turn(i, carry):
            first = meta[AT_LO + tile] + CHUNK * i
            keys = stretches(meta, held, 0, first)
            values = stretches(meta, held, AT_V, first)
            scores = dot_cols(query, keys)
            key_at = key_places(meta, first, (1, CHUNK * STRETCH), 1)
            allowed = (key_at <= place) & (key_at >= start)
            weights = jnp.where(allowed, jnp.exp(scores), 0.0)
            part = weights[:, :STRETCH]
            for u in range(1, CHUNK):
                part = part + weights[:, u * STRETCH : (u + 1) * STRETCH]
            total[...] += part
            acc[...] += dot(weights.astype(BF), values)
            return carry

        lax.fori_loop(0, turns_of(meta, tile), turn, 0)
        row_total = jnp.sum(total[...], axis=1, keepdims=True)
        result = acc[...] / row_total
        rows = pl.ds(tile * STRETCH, STRETCH)
        for head in range(2):
            block = result[head * STRETCH : (head + 1) * STRETCH]
            low_ref[rows, head * HEAD : (head + 1) * HEAD] = block.astype(BF)
            full_ref[rows, head * HEAD : (head + 1) * HEAD] = block
        logs = jnp.broadcast_to(jnp.log(row_total), (2 * STRETCH, STRETCH))
        lse_ref[tile] = jnp.transpose(logs)[:8]
    kept_ref[...] = dot(low_ref[:STRETCH], w_ref[...])
    sent_ref[...] = dot(low_ref[STRETCH:], w_ref[...]).astype(BF)


def backward_kernel(meta, q_ref, full_ref, lse_ref, w_ref, *refs):
    parts, pieces, dq_ref, outs = refs[:4], refs[4:24], refs[-10], refs[-9:-5]
    held, grads, acc, g_ref, sem = refs[-5:]
    copies = piece_copies(pieces, held, sem)
    for copy in copies:
        copy.start()
    for i, part in enumerate(parts):
        g_ref[64 * i : 64 * (i + 1)] = dot_cols(part[...], w_ref[...]).astype(BF)
    grads[...] = jnp.zeros_like(grads)
    for copy in copies:
        copy.wait()
    for tile in range(2):
        query = tile_of(q_ref, tile)
        grad = tile_of(g_ref, tile)
        full = tile_of(full_ref, tile)
        place, start = query_places(meta, tile, (1, 2 * STRETCH), 1)
        lse = lse_ref[tile][:1]
        delta = jnp.sum(grad.astype(F32) * full, axis=1, keepdims=True)
        delta = jnp.transpose(jnp.broadcast_to(delta, (2 * STRETCH, STRETCH)))[:1]
        acc[...] = jnp.zeros_like(acc)

        def turn(i, carry):
            first = meta[AT_LO + tile] + CHUNK * i
            keys = stretches(meta, held, 0, first)
            values = stretches(meta, held, AT_V, first)
            key_at = key_places(meta, first, (CHUNK * STRETCH, 1), 0)
            allowed = (key_at <= place) & (key_at >= start)
            weights = jnp.where(allowed, jnp.exp(dot_cols(keys, query) - lse), 0.0)
            slopes = (weights * (dot_cols(values, grad) - delta)).astype(BF)
            key_term = dot(slopes, query)
            value_term = dot(weights.astype(BF), grad)
            acc[...] += dot_rows(slopes, keys)
            for u in range(CHUNK):
                part = slice(u * STRETCH, (u + 1) * STRETCH)
                for at, term in ((meta[first + u], key_term), (meta[AT_V + first + u], value_term)):
                    grads[at] = (grads[at].astype(F32) + term[part]).astype(BF)
            return carry

        lax.fori_loop(0, turns_of(meta, tile), turn, 0)
        rows = pl.ds(tile * STRETCH, STRETCH)
        for head in range(2):
            block = acc[head * STRETCH : (head + 1) * STRETCH]
            dq_ref[rows, head * HEAD : (head + 1) * HEAD] = block * (HEAD**-0.5)
    copies = []
    for side in range(2):
        for h in range(2):
            at = 64 * side + 32 * h
            for out, first, count, begin in ((0, 24, 8, 8 * h), (1, 0, 24, 24 * h)):
                copies.append(
                    pltpu.make_async_copy(
                        grads.at[pl.ds(at + first, count)],
                        outs[2 * side + out].at[pl.ds(begin, count)],
                        sem.at[len(copies)],
                    )
                )
    for copy in copies:
        copy.start()
    for copy in copies:
        copy.wait()


def in_vmem():
    return pl.BlockSpec(memory_space=pltpu.VMEM)


def anywhere():
    return pl.BlockSpec(memory_space=pl.ANY)


def attend_forward(meta, query, w_attn_out, pieces):
    rows, width = query.shape[0], w_attn_out.shape[1]
    return pl.pallas_call(
        forward_kernel,
        out_shape=(
            jax.ShapeDtypeStruct((rows, 2 * HEAD), BF),
            jax.ShapeDtypeStruct((rows, 2 * HEAD), F32),
            jax.ShapeDtypeStruct((2, 8, 2 * STRETCH), F32),
            jax.ShapeDtypeStruct((STRETCH, width), F32),
            jax.ShapeDtypeStruct((STRETCH, width), BF),
        ),
        in_specs=[pl.BlockSpec(memory_space=pltpu.SMEM), in_vmem(), in_vmem()] + [anywhere()] * 20,
        out_specs=(in_vmem(),) * 5,
        scratch_shapes=[
            pltpu.VMEM((2 * SLOTS, STRETCH, HEAD), BF),
            pltpu.VMEM((2 * STRETCH, HEAD), F32),
            pltpu.VMEM((2 * STRETCH, STRETCH), F32),
            pltpu.SemaphoreType.DMA((20,)),
        ],
        compiler_params=pltpu.CompilerParams(vmem_limit_bytes=VMEM_GRANT),
        cost_estimate=pl.CostEstimate(
            flops=3 * 10**9, bytes_accessed=10**7, transcendentals=2 * 10**6
        ),
        name="attend_forward",
    )(meta, query, w_attn_out, *pieces)


def attend_backward(meta, query, full, lse, w_attn_out, parts, pieces, *events):
    rows = query.shape[0]
    outs = pl.pallas_call(
        backward_kernel,
        out_shape=(jax.ShapeDtypeStruct((rows, 2 * HEAD), F32),)
        + tuple(jax.ShapeDtypeStruct((count, STRETCH, HEAD), BF) for count in (16, 48, 16, 48)),
        in_specs=[pl.BlockSpec(memory_space=pltpu.SMEM)] + [in_vmem()] * 8
        + [anywhere()] * (20 + len(events)),
        out_specs=(in_vmem(),) + (anywhere(),) * 4,
        scratch_shapes=[
            pltpu.VMEM((2 * SLOTS, STRETCH, HEAD), BF),
            pltpu.VMEM((2 * SLOTS, STRETCH, HEAD), BF),
            pltpu.VMEM((2 * STRETCH, HEAD), F32),
            pltpu.VMEM((rows, 2 * HEAD), BF),
            pltpu.SemaphoreType.DMA((20,)),
        ],
        compiler_params=pltpu.CompilerParams(vmem_limit_bytes=VMEM_GRANT),
        cost_estimate=pl.CostEstimate(
            flops=10**10, bytes_accessed=2 * 10**7, transcendentals=2 * 10**6
        ),
        name="attend_backward",
    )(meta, query, full, lse, w_attn_out, *parts, *pieces, *events)
    return outs[0], outs[1:]


UNITS = 512


def ff_forward_kernel(*refs):
    parts, (w_gate, w_up, w_down) = refs[:4], refs[4:7]
    gate_out, up_out, pre_out, act_out, kept, sent = refs[7:13]
    now, acc = refs[13:]
    turn = pl.program_id(0)

    @pl.when(turn == 0)
    def first():
        for i, part in enumerate(parts):
            pre_out[64 * i : 64 * (i + 1)] = part[...]
        acc[...] = jnp.zeros_like(acc)

    gate = dot(pre_out[...], w_gate[...])
    up = dot(pre_out[...], w_up[...])
    gate_out[...] = gate
    up_out[...] = up
    now[...] = (gelu_parts(gate)[0] * up).astype(BF)
    act_out[...] = now[...]
    acc[...] += dot(now[...], w_down[...])

    @pl.when(turn == pl.num_programs(0) - 1)
    def last():
        kept[...] = acc[:STRETCH]
        sent[...] = acc[STRETCH:].astype(BF)


def ff_forward(parts, w_gate, w_up, w_down):
    width, units = w_gate.shape
    rows = 4 * parts[0].shape[0]
    whole = lambda shape: pl.BlockSpec(shape, lambda i: (0, 0))
    tall, flat = pl.BlockSpec((width, UNITS), lambda i: (0, i)), pl.BlockSpec((UNITS, width), lambda i: (i, 0))
    strip = pl.BlockSpec((rows, UNITS), lambda i: (0, i))
    return pl.pallas_call(
        ff_forward_kernel,
        grid=(units // UNITS,),
        out_shape=(
            jax.ShapeDtypeStruct((rows, units), F32),
            jax.ShapeDtypeStruct((rows, units), F32),
            jax.ShapeDtypeStruct((rows, width), BF),
            jax.ShapeDtypeStruct((rows, units), BF),
            jax.ShapeDtypeStruct((rows // 2, width), F32),
            jax.ShapeDtypeStruct((rows // 2, width), BF),
        ),
        in_specs=[whole((rows // 4, width))] * 4 + [tall, tall, flat],
        out_specs=(
            strip,
            strip,
            whole((rows, width)),
            strip,
            whole((rows // 2, width)),
            whole((rows // 2, width)),
        ),
        scratch_shapes=[pltpu.VMEM((rows, UNITS), BF), pltpu.VMEM((rows, width), F32)],
        compiler_params=pltpu.CompilerParams(vmem_limit_bytes=VMEM_GRANT),
        cost_estimate=pl.CostEstimate(
            flops=6 * rows * width * units, bytes_accessed=3 * 10**7, transcendentals=rows * units
        ),
        name="ff_forward",
    )(*parts, w_gate, w_up, w_down)


def ff_grads_kernel(me, *refs):
    parts, (gate_ref, up_ref, w_down) = refs[:4], refs[4:7]
    cuts, quarters, all_in = refs[7:11], refs[11:15], refs[15]
    block = pl.program_id(0)

    @pl.when(block == 0)
    def first():
        for i, part in enumerate(parts):
            all_in[64 * i : 64 * (i + 1)] = part[...]
        for k in range(4):
            at = pl.multiple_of((me[1] ^ k) * 512, 512)
            quarters[k][...] = all_in[:, pl.ds(at, 512)]

    grad_act = dot_cols(all_in[...], w_down[...])
    value, slope = gelu_parts(gate_ref[...])
    for k in range(4):

        @pl.when(block == k)
        def store():
            cuts[k][:, :UNITS] = (grad_act * up_ref[...] * slope).astype(BF)
            cuts[k][:, UNITS:] = (grad_act * value).astype(BF)


def ff_grads(me, parts, gate_pre, up_pre, w_down):
    units, width = w_down.shape
    rows = gate_pre.shape[0]
    whole = lambda shape: pl.BlockSpec(shape, lambda k, me: (0, 0))
    flat = pl.BlockSpec((UNITS, width), lambda k, me: (k ^ me[0], 0))
    strip = pl.BlockSpec((rows, UNITS), lambda k, me: (0, k ^ me[0]))
    outs = pl.pallas_call(
        ff_grads_kernel,
        grid_spec=pltpu.PrefetchScalarGridSpec(
            num_scalar_prefetch=1,
            grid=(4,),
            in_specs=[whole((rows // 4, width))] * 4 + [strip, strip, flat],
            out_specs=(whole((rows, 2 * UNITS)),) * 4 + (whole((rows, width // 4)),) * 4,
            scratch_shapes=[pltpu.VMEM((rows, width), BF)],
        ),
        out_shape=(jax.ShapeDtypeStruct((rows, 2 * UNITS), BF),) * 4
        + (jax.ShapeDtypeStruct((rows, width // 4), BF),) * 4,
        compiler_params=pltpu.CompilerParams(vmem_limit_bytes=VMEM_GRANT),
        cost_estimate=pl.CostEstimate(
            flops=2 * rows * width * units, bytes_accessed=10**7, transcendentals=rows * units
        ),
        name="ff_grads",
    )(me, *parts, gate_pre, up_pre, w_down)
    return outs[:4], outs[4:]


def ff_back_kernel(me, *refs):
    cuts, (w_gate, w_up, kept, sent, acc) = refs[:4], refs[4:]
    block = pl.program_id(0)

    @pl.when(block == 0)
    def first():
        acc[...] = jnp.zeros_like(acc)

    for k in range(4):

        @pl.when(block == k)
        def add():
            term = dot_cols(cuts[k][:, :UNITS], w_gate[...])
            acc[...] += term + dot_cols(cuts[k][:, UNITS:], w_up[...])

    @pl.when(block == 3)
    def last():
        kept[...] = acc[:STRETCH]
        sent[...] = acc[STRETCH:].astype(BF)


def ff_back(me, cuts, w_gate, w_up):
    width, units = w_gate.shape
    rows = cuts[0].shape[0]
    whole = lambda shape: pl.BlockSpec(shape, lambda k, me: (0, 0))
    tall = pl.BlockSpec((width, UNITS), lambda k, me: (0, k ^ me[0]))
    return pl.pallas_call(
        ff_back_kernel,
        grid_spec=pltpu.PrefetchScalarGridSpec(
            num_scalar_prefetch=1,
            grid=(4,),
            in_specs=[whole((rows, 2 * UNITS))] * 4 + [tall, tall],
            out_specs=(whole((rows // 2, width)),) * 2,
            scratch_shapes=[pltpu.VMEM((rows, width), F32)],
        ),
        out_shape=(
            jax.ShapeDtypeStruct((rows // 2, width), F32),
            jax.ShapeDtypeStruct((rows // 2, width), BF),
        ),
        compiler_params=pltpu.CompilerParams(vmem_limit_bytes=VMEM_GRANT),
        cost_estimate=pl.CostEstimate(
            flops=4 * rows * width * units, bytes_accessed=2 * 10**7, transcendentals=0
        ),
        name="ff_back",
    )(me, *cuts, w_gate, w_up)


def relative_rows(spots, stream):
    return jnp.concatenate(
        [stream[pl.ds(pl.multiple_of(spots[i], 64), 64)] for i in range(4)], axis=0
    )


def swapped(value):
    return jnp.concatenate([value[STRETCH:], value[:STRETCH]], axis=0)


def input_kernel(spots, stream, w_key, w_value, g_in, normed_out, mine, theirs):
    rows = relative_rows(spots, stream).astype(F32)
    normed_out[...] = (rows * rms(rows) * g_in[...]).astype(BF)
    key, value = dot(normed_out[...], w_key[...]), dot(normed_out[...], w_value[...])
    first = spots[4] == 0
    mine[...] = jnp.where(first, key, value)
    theirs[...] = swapped(jnp.where(first, value, key))


def kind_kernel(spots, mine, came, cosine, sine, gain, low_out, full_out):
    first = spots[4] == 0
    kind = jnp.concatenate(
        [jnp.where(first, mine[...], came[...]), jnp.where(first, came[...], mine[...])], axis=1
    )
    full_out[...] = kind
    turn = (jnp.where(first, cosine[...], 1.0), jnp.where(first, sine[...], 0.0))
    scaled = kind * rms(kind) * jnp.where(first, gain[...], 1.0)
    low_out[...] = rotate(scaled, *turn).astype(BF)


def lay_kernel(*refs):
    for h in range(2):
        for i in range(4):
            refs[8 + h][256 * i : 256 * (i + 1)] = refs[4 * h + i][...]


def kind_back_kernel(spots, sums_a, sums_b, came, kind_ref, cosine, sine, gain, event, home, away, gains):
    first = spots[4] == 0
    turn = (jnp.where(first, cosine[...], 1.0), jnp.where(first, -sine[...], 0.0))
    grad = jnp.concatenate([sums_a[...] + came[0].astype(F32), sums_b[...] + came[1].astype(F32)], axis=0)
    kind = kind_ref[...]
    scale = rms(kind)
    grad, gain_part = norm_back(
        rotate(grad, *turn), kind * scale, scale, jnp.where(first, gain[...], 1.0)
    )
    gains[...] = jnp.where(first, gain_part, 0.0)
    half = HEAD // 2
    home[...] = jnp.where(first, grad[:, :half], grad[:, half:]).astype(BF)
    away[...] = swapped(jnp.where(first, grad[:, half:], grad[:, :half])).astype(BF)


def query_kernel(normed, w_query, cosine, sine, gain, event, low_out, raw_out):
    for head in range(2):
        at = slice(head * HEAD, (head + 1) * HEAD)
        raw = dot(normed[...], w_query[:, at])
        raw_out[:, at] = raw
        turned = rotate(raw * rms(raw) * gain[...], cosine[...], sine[...]).astype(BF)
        low_out[:, at] = (turned.astype(F32) * HEAD**-0.5).astype(BF)


def query_back_kernel(grad_ref, raw_ref, cosine, sine, gain, event, low_out, gains):
    gains[...] = jnp.zeros_like(gains)
    for head in range(2):
        at = slice(head * HEAD, (head + 1) * HEAD)
        raw = raw_ref[:, at]
        scale = rms(raw)
        grad, part = norm_back(
            rotate(grad_ref[:, at], cosine[...], -sine[...]), raw * scale, scale, gain[...]
        )
        low_out[:, at] = grad.astype(BF)
        gains[...] += part


def normed_back_kernel(spots, home, came, query, w_query, w_key, w_value, stream, *outs):
    kept, sent, gain_out, cuts = outs[-7], outs[-6], outs[-5], outs[-4:]
    first = spots[4] == 0
    key = jnp.where(first, home[...].astype(F32), came[...].astype(F32)).astype(BF)
    value = jnp.where(first, came[...].astype(F32), home[...].astype(F32)).astype(BF)
    part = dot_cols(query[...], w_query[...])
    part = part + dot_cols(key, w_key[...]) + dot_cols(value, w_value[...])
    kept[...] = part[:STRETCH]
    sent[...] = part[STRETCH:].astype(BF)
    rows = relative_rows(spots, stream).astype(F32)
    gain_out[...] = jnp.sum(part * (rows * rms(rows)), axis=0, keepdims=True)
    for k, cut in enumerate(cuts):
        at = spots[5] ^ k
        cut[:, :128] = query[:, pl.ds(pl.multiple_of(at * 128, 128), 128)]
        side = jnp.where(at >= 2, value.astype(F32), key.astype(F32))
        side = jnp.where((at & 1) == 1, side[:, 64:], side[:, :64])
        cut[:, 128:] = side.astype(BF)


def far_kernel(own, came, *refs):
    for i, out in enumerate(refs[-4:]):
        at = slice(4 * i, 4 * i + 4)
        out[...] = (own[at].astype(F32) + came[at].astype(F32)).astype(BF)


def near_kernel(own, came, *refs):
    passed, (base_a, base_b), sends = refs[:4], refs[-6:-4], refs[-4:]

    def summed(first, count):
        at = slice(first, first + count)
        return own[at].astype(F32) + came[at].astype(F32)

    for h, base in enumerate((base_a, base_b)):
        near, other = sends[2 * h], sends[2 * h + 1]
        base[...] = summed(24 * h, 8)
        near[:4] = summed(24 * h + 8, 4).astype(BF)
        near[4:] = (summed(24 * h + 12, 4) + passed[2 * h + 1][...].astype(F32)).astype(BF)
        other[:4] = (summed(24 * h + 16, 4) + passed[2 * h][...].astype(F32)).astype(BF)
        other[4:] = summed(24 * h + 20, 4).astype(BF)


def inner_kernel(base_a, base_b, *refs):
    came, kept, sends = refs[:4], refs[-8:-6], refs[-6:]
    for h, base in enumerate((base_a, base_b)):
        total = base[...] + came[2 * h][...].astype(F32) + came[2 * h + 1][...].astype(F32)
        kept[h][...] = total[:2]
        for k in (1, 2, 3):
            sends[3 * h + k - 1][...] = total[2 * k : 2 * k + 2].astype(BF)


def last_kernel(kept_a, kept_b, *refs):
    came, kept, send = refs[:6], refs[6:8], refs[8]
    for h, base in enumerate((kept_a, kept_b)):
        total = base[...]
        for k in range(3):
            total = total + came[3 * h + k][...].astype(F32)
        kept[h][...] = total[0]
        send[h] = total[1].astype(BF)


def mid_kernel(kept, came, stream, left, right, g_in, g_attn, g_laurel, g_pre, *outs):
    pre_out, resid_out, attn_out, laurel_out, low_out = outs
    rows = stream[...].astype(F32)
    normed = rows * rms(rows) * g_in[...]
    attn = kept[...] + came[...].astype(F32)
    low = dot_cols(normed.astype(BF), left[...])
    laurel = fine(low, right[...])
    resid = (
        rows + attn * rms(attn) * g_attn[...] + normed + laurel * rms(laurel) * g_laurel[...]
    ) * ROOT_HALF
    pre_out[...] = (resid * rms(resid) * g_pre[...]).astype(BF)
    resid_out[...] = resid
    attn_out[...] = attn
    laurel_out[...] = laurel
    low_out[...] = low


def join_kernel(kept, came, resid, top, inputs, gate_t, proj, g_post, g_join, event, *outs):
    ff_out, after_out, results, gains, mine, theirs = outs
    ff = kept[...] + came[...].astype(F32)
    ff_scale = rms(ff)
    ff_normal = ff * ff_scale
    after = resid[...] + ff_normal * g_post[...]
    value, slope = gelu_parts(fine_cols(after, gate_t[...]))
    channels = inputs[...].astype(F32)
    joined = value * channels
    join = fine(joined, proj[...])
    join_scale = rms(join)
    join_normal = join * join_scale
    results[:, :D] = (after + join_normal * g_join[...]).astype(BF)
    grad = top[...].astype(F32)
    grad_join, gain_join = norm_back(grad, join_normal, join_scale, g_join[...])
    grad_joined = fine_cols(grad_join, proj[...])
    grad_pre = grad_joined * channels * slope
    results[:, D:] = (grad_joined * value).astype(BF)
    grad_after = grad + fine(grad_pre, gate_t[...])
    after_out[...] = grad_after
    grad_ff, gain_post = norm_back(grad_after, ff_normal, ff_scale, g_post[...])
    ff_out[...] = grad_ff.astype(BF)
    gains[...] = jnp.zeros_like(gains)
    gains[0:1] = gain_post
    gains[1:2] = gain_join
    low_gate = dot_rows(grad_pre.astype(BF), after.astype(BF)).astype(BF)
    low_proj = dot_rows(joined.astype(BF), grad_join.astype(BF)).astype(BF)
    for k, (out, i) in enumerate(((mine, 0), (theirs, 0), (mine, 1), (theirs, 1))):
        out[i, :64] = low_gate[64 * k : 64 * (k + 1)]
        out[i, 64:] = low_proj[64 * k : 64 * (k + 1)]


def resid_kernel(
    kept,
    came,
    resid,
    after,
    attn,
    laurel,
    low,
    stream,
    left,
    right,
    g_in,
    g_attn,
    g_laurel,
    g_pre,
    gates_mine,
    gates_sent,
    *refs,
):
    attn_out, branch_out, own_out, gains, mine, theirs = refs[-6:]
    mine[:, 32:] = gates_mine[...]
    theirs[:, 32:] = gates_sent[...]
    scale = rms(resid[...])
    grad = kept[...] + came[...].astype(F32)
    grad_resid, gain_pre = norm_back(grad, resid[...] * scale, scale, g_pre[...])
    branch = (after[...] + grad_resid) * ROOT_HALF
    branch_out[...] = branch
    scale = rms(attn[...])
    grad_attn, gain_attn = norm_back(branch, attn[...] * scale, scale, g_attn[...])
    attn_out[...] = grad_attn.astype(BF)
    scale = rms(laurel[...])
    grad_laurel, gain_laurel = norm_back(branch, laurel[...] * scale, scale, g_laurel[...])
    grad_low = fine_cols(grad_laurel, right[...])
    own = branch + fine(grad_low, left[...])
    own_out[...] = own
    rows = stream[...].astype(F32)
    normal = rows * rms(rows)
    gains[...] = jnp.zeros_like(gains)
    gains[0:1] = gain_attn
    gains[1:2] = gain_laurel
    gains[2:3] = gain_pre
    gains[3:4] = jnp.sum(own * normal, axis=0, keepdims=True)
    low_left = dot_rows(grad_low.astype(BF), (normal * g_in[...]).astype(BF)).astype(BF)
    low_right = dot_rows(low[...].astype(BF), grad_laurel.astype(BF)).astype(BF)
    for k, (out, i) in enumerate(((mine, 0), (theirs, 0), (mine, 1), (theirs, 1))):
        out[i, :16] = low_left[16 * k : 16 * (k + 1)]
        out[i, 16:32] = low_right[16 * k : 16 * (k + 1)]


def final_kernel(kept, came, own, branch, stream, g_in, event, out):
    rows = stream[...].astype(F32)
    scale = rms(rows)
    grad = own[...] + kept[...] + came[...].astype(F32)
    extra, _ = norm_back(grad, rows * scale, scale, g_in[...])
    out[...] = (branch[...] + extra).astype(BF)


def in_one(kernel, shapes, args, name, event=(), spots=(), scratch=()):
    return pl.pallas_call(
        kernel,
        out_shape=tuple(jax.ShapeDtypeStruct(shape, kind) for shape, kind in shapes),
        in_specs=[pl.BlockSpec(memory_space=pltpu.SMEM)] * len(spots)
        + [in_vmem()] * len(args)
        + [anywhere()] * len(event),
        out_specs=(in_vmem(),) * len(shapes),
        scratch_shapes=list(scratch),
        compiler_params=pltpu.CompilerParams(vmem_limit_bytes=VMEM_GRANT),
        cost_estimate=pl.CostEstimate(flops=10**9, bytes_accessed=5 * 10**6, transcendentals=10**5),
        name=name,
    )(*spots, *args, *event)


def pack_kernel(left, right, gate_w, proj, inputs, event, out):
    unit = (
        lax.broadcasted_iota(jnp.int32, (64, 64), 0) == lax.broadcasted_iota(jnp.int32, (64, 64), 1)
    ).astype(BF)
    out[:16] = dot_cols(unit[:16, :16], left[...]).astype(BF)
    out[16:32] = right[...]
    out[32:96] = dot_cols(unit, gate_w[...]).astype(BF)
    out[96:160] = proj[...]
    turned = dot_cols(unit, inputs[...]).astype(BF)
    out[160:] = jnp.zeros_like(out[160:])
    for i in range(4):
        out[160:, 256 * i : 256 * (i + 1)] = turned[16 * i : 16 * (i + 1)]


Y_FIRST = (0, 3, 1, 2)
Y_OTHER = (0, 1, 3, 2)


def group_sum(me, group, cuts, at, size):
    total = None
    for k, cut in enumerate(cuts):
        term = dot_rows(group[me ^ k, :, pl.ds(at, size)], cut)
        total = term if total is None else total + term
    return total


def wide_kernel(where, group, *refs):
    cuts, out = refs[:4], refs[-1]
    for at in range(0, D, 256):
        total = group_sum(where[0], group, [cut[...] for cut in cuts], at, 256)
        out[at : at + 256] = total.astype(BF)


def wide_product(where, group, cuts, event):
    return pl.pallas_call(
        wide_kernel,
        out_shape=jax.ShapeDtypeStruct((D, cuts[0].shape[1]), BF),
        in_specs=[pl.BlockSpec(memory_space=pltpu.SMEM)] + [in_vmem()] * 5 + [anywhere()],
        out_specs=in_vmem(),
        compiler_params=pltpu.CompilerParams(vmem_limit_bytes=VMEM_GRANT),
        cost_estimate=pl.CostEstimate(flops=5 * 10**9, bytes_accessed=10**7, transcendentals=0),
        name="wide_product",
    )(where, group, *cuts, event)


def turn_kernel(small, attn, *refs):
    parts, out, grads = refs[:4], refs[-2], refs[-1]
    low = small.shape[0]
    for i, part in enumerate(parts):
        grads[64 * i : 64 * (i + 1)] = part[...]
    unit = (
        lax.broadcasted_iota(jnp.int32, (low, 256), 0)
        == lax.broadcasted_iota(jnp.int32, (low, 256), 1)
    ).astype(BF)
    out[:, :512] = dot_rows(grads[...], attn[...]).astype(BF)
    out[:, 512:] = dot_rows(small[...], unit).astype(BF)


def token_kernel(where, group, gains, *refs):
    cuts, (kept, sent) = refs[:4], refs[4:]
    x, y, z = where[0], where[1], where[2]
    unit = (
        lax.broadcasted_iota(jnp.int32, (16, 64), 0) == lax.broadcasted_iota(jnp.int32, (16, 64), 1)
    ).astype(BF)
    for i, far_y in enumerate(Y_FIRST):
        for far_z in range(2):
            at = pl.multiple_of(((y ^ far_y) * 2 + (z ^ far_z)) * 256, 256)
            total = group_sum(x, group, [cut[...] for cut in cuts], at, 256)
            more = dot_rows(gains[:, pl.ds(at, 256)], unit)
            total = jnp.concatenate([total, more], axis=1).astype(BF)
            (kept, sent)[i // 2][i % 2, far_z] = total


def token_product(where, group, gains, cuts):
    shape = (2, 2, 256, cuts[0].shape[1] + 64)
    return pl.pallas_call(
        token_kernel,
        out_shape=(jax.ShapeDtypeStruct(shape, BF),) * 2,
        in_specs=[pl.BlockSpec(memory_space=pltpu.SMEM)] + [in_vmem()] * 6,
        out_specs=(in_vmem(),) * 2,
        compiler_params=pltpu.CompilerParams(vmem_limit_bytes=VMEM_GRANT),
        cost_estimate=pl.CostEstimate(flops=10**9, bytes_accessed=6 * 10**6, transcendentals=0),
        name="token_product",
    )(where, group, gains, *cuts)


def payload_kernel(where, wide, tokens, turn, *outs):
    for k, out in enumerate(outs):
        at = pl.ds(pl.multiple_of((where[0] ^ k) * 64, 64), 64)
        out[:, :1024] = wide[at]
        out[:, 1024:1280] = tokens[at]
        out[:, 1280:] = turn[at]


def share_kernel(where, *refs):
    shares, down_kept, down_came = refs[:4], refs[4], refs[5]
    gate, up, query, key, value, attn, left, right, join_g, join_p, gains, down = refs[6:]
    x = where[0]

    def turned(rows):
        rows = jnp.concatenate([rows, jnp.zeros_like(rows)], axis=0)
        return jnp.transpose(rows)[:, :64]

    for k, share in enumerate(shares):
        gate[:, pl.ds(pl.multiple_of((x ^ k) * 512, 512), 512)] = share[:, :512].astype(F32)
        up[:, pl.ds(pl.multiple_of((x ^ k) * 512, 512), 512)] = share[:, 512:1024].astype(F32)
        query[:, pl.ds(pl.multiple_of((x ^ k) * 128, 128), 128)] = share[:, 1024:1152].astype(F32)
    quarters = [share[:, 1152:1216].astype(F32) for share in shares]
    placed = []
    for q in range(4):
        choice = quarters[3]
        for k in range(3):
            choice = jnp.where((x ^ k) == q, quarters[k], choice)
        placed.append(choice)
    key[:, :64], key[:, 64:] = placed[0], placed[1]
    value[:, :64], value[:, 64:] = placed[2], placed[3]
    total = shares[0][:, 1216:].astype(F32)
    for share in shares[1:]:
        total = total + share[:, 1216:].astype(F32)
    gains[...] = total[:, :16]
    attn[...] = total[:, 64:576]
    small = total[:, 576:736]
    join_g[...] = small[:, 32:96]
    lines = turned(jnp.concatenate([small, jnp.zeros((64, 96), F32)], axis=1))
    left[...] = lines[:16]
    right[...] = lines[16:32]
    join_p[...] = lines[96:160]
    down[...] = down_kept[...].astype(F32) + down_came[...].astype(F32)


def down_kernel(where, group, *refs):
    cuts, out, total = refs[:4], refs[5], refs[6]
    x, y = where[0], where[1]
    units = group.shape[2]
    for first in range(0, units, 512):
        value = None
        for k, cut in enumerate(cuts):
            term = dot_rows(cut[...], group[y ^ k, :, first : first + 512])
            value = term if value is None else value + term
        total[...] = value
        for i, far_x in enumerate(Y_FIRST):
            for z in range(2):
                at = pl.multiple_of((z * 4 + (x ^ far_x)) * 64, 64)
                out[z, i, :, first : first + 512] = total[pl.ds(at, 64)].astype(BF)


def down_product(where, group, cuts, event):
    return pl.pallas_call(
        down_kernel,
        out_shape=jax.ShapeDtypeStruct((2, 4, 64, group.shape[2]), BF),
        in_specs=[pl.BlockSpec(memory_space=pltpu.SMEM)] + [in_vmem()] * 5 + [anywhere()],
        out_specs=in_vmem(),
        scratch_shapes=[pltpu.VMEM((512, 512), F32)],
        compiler_params=pltpu.CompilerParams(vmem_limit_bytes=VMEM_GRANT),
        cost_estimate=pl.CostEstimate(flops=3 * 10**9, bytes_accessed=10**7, transcendentals=0),
        name="down_product",
    )(where, group, *cuts, event)


def local(
    stream,
    layer_input,
    out_grad,
    doc_lengths,
    stretch_slots,
    gain_input,
    gain_query,
    gain_key,
    w_query,
    w_key,
    w_value,
    w_attn_out,
    gain_attn,
    laurel_left,
    laurel_right,
    gain_laurel,
    gain_pre_ff,
    w_gate,
    w_up,
    w_down,
    gain_post_ff,
    join_gate,
    join_proj,
    gain_join,
):
    wt = lax.axis_index("wt")
    core, zlo = wt & 1, wt >> 1
    ctx = lax.axis_index("ctx")
    at_x, at_z, at_y = ctx & 3, (ctx >> 2) & 1, ctx >> 3
    first_core = core == 0
    half = HEAD // 2

    def starts(k):
        return ((core ^ (k & 1)) * 2 + (zlo ^ (k >> 1))) * 64

    def natural(blocks):
        stacked = jnp.stack(blocks)
        return jnp.concatenate(
            [pick(stacked, wt ^ ((b & 1) * 2 + (b >> 1)), 0) for b in range(4)], axis=0
        )

    stream_own = lax.dynamic_slice_in_dim(stream, starts(0), 64, 0)
    grad_top = lax.dynamic_slice_in_dim(out_grad, starts(0), 64, 0)
    where = jnp.stack([at_x, at_y, at_z])
    spots = (jnp.stack([starts(0), starts(2), starts(1), starts(3), core, at_x]),)
    g_in, g_attn, g_laurel, g_pre, g_post, g_join = (
        gain[None, :]
        for gain in (gain_input, gain_attn, gain_laurel, gain_pre_ff, gain_post_ff, gain_join)
    )

    doc_ends = jnp.cumsum(doc_lengths)
    tiles = [lax.dynamic_index_in_dim(stretch_slots, 2 * ctx + (core ^ t), 0) for t in range(2)]
    hi = jnp.concatenate(tiles)
    lo = jnp.max(
        jnp.where(doc_ends[None, :] <= hi[:, None] * STRETCH, doc_ends[None, :], 0), axis=1
    )
    lo = lo // STRETCH
    row = (jnp.arange(STRETCH, dtype=jnp.int32) + 64 * zlo) & (STRETCH - 1)
    positions = (hi[:, None] * STRETCH + row[None, :]).reshape(-1)
    names = jnp.arange(SLOTS, dtype=jnp.int32)
    slot_of = jnp.sum(jnp.where(stretch_slots[None, :] == names[:, None], names[None, :], 0), axis=1)
    relative = (slot_of >> 1) ^ ctx
    rel_x, rel_z, rel_y = relative & 3, (relative >> 2) & 1, relative >> 3
    places = (
        (rel_y ^ (rel_y >> 1)) * 8 + rel_x * 2 + rel_z,
        SLOTS // 2 + (rel_x ^ (rel_x >> 1)) * 8 + rel_y * 2 + rel_z,
    )
    second = (slot_of & 1) == 1
    key_at = core * SLOTS + jnp.where(second, places[1], places[0])
    value_at = (1 - core) * SLOTS + jnp.where(second, places[0], places[1])
    blank = jnp.zeros((PAD_SLOTS - SLOTS,), jnp.int32)
    meta = jnp.concatenate([key_at, blank, value_at, blank, hi, lo, zlo[None], doc_ends]).astype(
        jnp.int32
    )
    exponents = jnp.arange(half, dtype=F32) * (2.0 / HEAD)
    angles = positions.astype(F32)[:, None] * (1.0 / ROPE_BASE**exponents)[None, :]
    cosine, sine = jnp.cos(angles), jnp.sin(angles)

    half_rows, heads_b = ((2 * STRETCH, half), F32), ((2 * STRETCH, 2 * HEAD), BF)
    normed_b, mine, theirs = in_one(
        input_kernel,
        (((2 * STRETCH, D), BF), half_rows, half_rows),
        (stream, w_key, w_value, g_in),
        "input",
        spots=spots,
    )
    kind_b, kind = in_one(
        kind_kernel,
        (((2 * STRETCH, HEAD), BF), ((2 * STRETCH, HEAD), F32)),
        (mine, hop(theirs, "wt", 1), cosine, sine, gain_key[None, :]),
        "kind",
        spots=spots,
    )

    across = hop(kind_b, "ctx", 4)
    groups = []
    for h, one in enumerate((1, 8)):
        rows = slice(h * STRETCH, (h + 1) * STRETCH)
        block = jnp.concatenate([kind_b[rows], across[rows]], axis=0)
        groups.append([block] + [hop(block, "ctx", k * one) for k in (1, 2, 3)])
    quads = in_one(lay_kernel, (((1024, HEAD), BF),) * 2, (*groups[0], *groups[1]), "lay")
    pieces = ring_gather(quads[0], 8, 24) + ring_gather(quads[1], 1, 3)
    pieces += [hop(piece, "wt", 1) for piece in pieces]
    pieces = [piece.reshape(-1, STRETCH, HEAD) for piece in pieces]

    (pack,) = in_one(
        pack_kernel,
        (((176, D), BF),),
        (laurel_left, laurel_right, join_gate, join_proj, layer_input),
        "pack",
        (quads[0],),
    )
    packs = lax.all_gather(pack, "wt", axis=0)

    query_b, query_raw = in_one(
        query_kernel,
        (heads_b, ((2 * STRETCH, 2 * HEAD), F32)),
        (normed_b, w_query, cosine, sine, gain_query[None, :]),
        "query",
        (pieces[0],),
    )

    attn_b, attn_full, lse, kept, sent = attend_forward(meta, query_b, w_attn_out, pieces)

    kept, came = scatter_wt(kept, sent)

    def from_packs(first, last):
        return jnp.concatenate([pick(packs, wt ^ k, 0)[first:last] for k in range(4)], axis=0)

    left_t, right_w = from_packs(0, 16), from_packs(16, 32)
    gate_t, proj_w = from_packs(32, 96), from_packs(96, 160)
    inputs = packs[:, 160:, :1024].reshape(4, 16, 4, 256).transpose(0, 2, 1, 3)
    inputs = lax.dynamic_slice_in_dim(inputs.reshape(4, 64, 256), starts(0), 64, 2)
    inputs = jnp.concatenate([pick(inputs, wt ^ k, 0) for k in range(4)], axis=0).T
    normed_group = gather_group(normed_b, GROUP_X)
    wide_f, wide_b = ((64, D), F32), ((64, D), BF)
    pre_b, resid, attn_sum, laurel_sum, laurel_mid = in_one(
        mid_kernel,
        (wide_b, wide_f, wide_f, wide_f, ((64, 64), F32)),
        (kept, came, stream_own, left_t, right_w, g_in, g_attn, g_laurel, g_pre),
        "mid",
    )

    gate_pre, up_pre, pre_all, act_b, kept, sent = ff_forward(
        gather_wt(pre_b), w_gate, w_up, w_down
    )
    kept, came = scatter_wt(kept, sent)
    pre_group = gather_group(pre_all, GROUP_X)
    act_group = gather_group(act_b, GROUP_Y)

    grad_ff, grad_after, results, gains_join, gates_mine, gates_sent = in_one(
        join_kernel,
        (
            wide_b,
            wide_f,
            ((64, D + 256), BF),
            ((8, D), F32),
            ((2, 128, D), BF),
            ((2, 128, D), BF),
        ),
        (kept, came, resid, grad_top, inputs, gate_t, proj_w, g_post, g_join),
        "join",
        (normed_group,),
    )

    grad_ff_parts = gather_wt(grad_ff)
    wide_cuts, down_cuts = ff_grads(where, grad_ff_parts, gate_pre, up_pre, w_down)
    kept, sent = ff_back(where, wide_cuts, w_gate, w_up)
    wide_cuts = [wide_cuts[0]] + [hop(wide_cuts[k], "ctx", k) for k in (1, 2, 3)]
    down_cuts = [down_cuts[0]] + [hop(down_cuts[k], "ctx", 8 * k) for k in (1, 2, 3)]
    kept, came = scatter_wt(kept, sent)

    grad_attn, branch, own_part, gains_resid, small_mine, small_sent = in_one(
        resid_kernel,
        (wide_b, wide_f, wide_f, ((8, D), F32), ((2, 160, D), BF), ((2, 160, D), BF)),
        (
            kept,
            came,
            resid,
            grad_after,
            attn_sum,
            laurel_sum,
            laurel_mid,
            stream_own,
            left_t,
            right_w,
            g_in,
            g_attn,
            g_laurel,
            g_pre,
            gates_mine,
            gates_sent,
        ),
        "resid",
        (pre_group,),
    )
    grad_attn_parts = gather_wt(grad_attn)

    grad_query_rot, grad_pieces = attend_backward(
        meta, query_b, attn_full, lse, w_attn_out, grad_attn_parts, pieces, *wide_cuts[1:]
    )
    wide = wide_product(where, pre_group, wide_cuts, grad_query_rot)
    def blocks(count, kind):
        return ((count, STRETCH, HEAD), kind)

    def hops(values, masks):
        return [hop(value, "ctx", mask) for value, mask in zip(values, masks)]

    own_far, own_rest, sent_far, sent_rest = grad_pieces
    came_rest = hop(sent_rest, "wt", 1)
    far = in_one(
        far_kernel,
        (blocks(4, BF),) * 4,
        (own_far, hop(sent_far, "wt", 1)),
        "far",
        (came_rest, wide, *down_cuts[1:]),
    )
    wide = scatter_group(wide, GROUP_Y)
    down = down_product(where, act_group, down_cuts, far[0])
    grad_query_b, gain_query_part = in_one(
        query_back_kernel,
        (heads_b, ((1, HEAD), F32)),
        (grad_query_rot, query_raw, cosine, sine, gain_query[None, :]),
        "query_back",
        (far[0],),
    )
    bases = in_one(
        near_kernel,
        (blocks(8, F32),) * 2 + (blocks(8, BF),) * 4,
        (own_rest, came_rest, *hops(far, (8, 24, 1, 3))),
        "near",
        (down,),
    )
    (small_sent,) = hold((small_sent,), bases[2])
    small = small_mine.astype(F32) + hop(small_sent, "wt", 1).astype(F32)
    small_far = small[1].astype(BF)
    small = (small[0] + hop(small_far, "wt", 2).astype(F32)).astype(BF)
    down = scatter_group(down, GROUP_Z).reshape(4, 64, -1)
    inner = in_one(
        inner_kernel,
        (blocks(2, F32),) * 2 + (blocks(2, BF),) * 6,
        (*bases[:2], *hops(bases[2:], (8, 24, 1, 3))),
        "inner",
        (grad_query_b,),
    )
    last = in_one(
        last_kernel,
        (((STRETCH, HEAD), F32),) * 2 + (blocks(2, BF),),
        (*inner[:2], *hops(inner[2:], (1, 2, 3, 8, 16, 24))),
        "last",
    )
    across = hop(last[2], "ctx", 4)
    (turn,) = in_one(
        turn_kernel,
        (((D, 768), BF),),
        (small, attn_b, *grad_attn_parts),
        "turn",
        (last[2],),
        scratch=(pltpu.VMEM((2 * STRETCH, D), BF),),
    )
    turn_event = turn
    turn = scatter_group(turn, GROUP_Y)
    home, away, gain_key_part = in_one(
        kind_back_kernel,
        (((2 * STRETCH, half), BF), ((2 * STRETCH, half), BF), ((1, HEAD), F32)),
        (*last[:2], across, kind, cosine, sine, gain_key[None, :]),
        "kind_back",
        (turn_event,),
        spots=spots,
    )

    outs = in_one(
        normed_back_kernel,
        (((STRETCH, D), F32), ((STRETCH, D), BF), ((1, D), F32))
        + (((2 * STRETCH, 192), BF),) * 4,
        (home, hop(away, "wt", 1), grad_query_b, w_query, w_key, w_value, stream),
        "normed_back",
        (wide,),
        spots=spots,
    )
    def fold_z(value):
        value = value.reshape(2, 256, -1)
        return fold(pick(value, at_z, 0), pick(value, 1 - at_z, 0), 4)

    wide = fold_z(wide)
    turn = fold_z(turn)
    kept, sent, gain_input_part, token_cuts = outs[0], outs[1], outs[2], outs[3:]
    kept, came = scatter_wt(kept, sent)
    (stream_grad,) = in_one(
        final_kernel, (wide_b,), (kept, came, own_part, branch, stream_own, g_in), "final", (turn,)
    )

    (results,) = hold((results,), turn)
    results = lax.all_gather(results, "wt", axis=0)
    layer_out_all = jnp.concatenate([results[i, :, :D] for i in (0, 2, 1, 3)]).astype(F32)
    grad_input_all = jnp.concatenate(
        [
            lax.dynamic_slice_in_dim(results[i], D + 64 * (wt ^ i), 64, 1)
            for i in (0, 2, 1, 3)
        ]
    ).astype(F32)

    first, near, core_rows, far_rows = gather_wt(stream_grad)
    stream_grad_all = natural([first, core_rows, near, far_rows]).astype(F32)
    heads = jnp.concatenate(
        [gain_query_part.reshape(32, 8), gain_key_part.reshape(32, 8), jnp.zeros((32, 48), F32)],
        axis=1,
    ).reshape(1, -1)
    line = jnp.arange(8)[:, None]
    late_gains = jnp.where(line == 0, heads, 0.0) + jnp.where(
        line == 1, gain_input_part, 0.0
    )
    late_gains = jnp.concatenate(
        [late_gains + jnp.roll(gains_join, 2, axis=0), gains_resid], axis=0
    )

    late_gains = late_gains + hop(late_gains, "wt", 1)
    late_gains = late_gains + hop(late_gains, "wt", 2)
    token_cuts = [token_cuts[0]] + [hop(token_cuts[k], "ctx", k) for k in (1, 2, 3)]
    (down,) = hold((down,), token_cuts[1])
    down = fold(down[:2], down[2:], 1)
    tokens = fold(*token_product(where, normed_group, late_gains.astype(BF), token_cuts), 8)
    tokens = fold(tokens[0], tokens[1], 24)
    tokens = fold(tokens[0], tokens[1], 4)
    shares = in_one(
        payload_kernel,
        (((64, 2048), BF),) * 4,
        (wide, tokens, turn),
        "payload",
        spots=(where,),
    )
    shares = [shares[0]] + [hop(shares[k], "ctx", k) for k in (1, 2, 3)]
    (
        grad_w_gate,
        grad_w_up,
        grad_w_query,
        grad_w_key,
        grad_w_value,
        grad_w_attn_out,
        grad_left,
        grad_right,
        grad_gate,
        grad_proj,
        gains,
        grad_w_down,
    ) = in_one(
        share_kernel,
        tuple(
            (shape, F32)
            for shape in (
                (64, D),
                (64, D),
                (64, 512),
                (64, half),
                (64, half),
                (64, 512),
                (16, 64),
                (16, 64),
                (64, 64),
                (64, 64),
                (64, 16),
                (64, D),
            )
        ),
        (*shares, down[0], hop(down[1], "ctx", 3)),
        "share",
        spots=(where,),
    )

    return (
        layer_out_all,
        stream_grad_all,
        grad_input_all,
        gains[:, 1] + gains[:, 11],
        gains[:8, 0],
        gains[8:16, 0],
        grad_w_query,
        grad_w_key,
        grad_w_value,
        grad_w_attn_out.T,
        gains[:, 8],
        grad_left.T,
        grad_right,
        gains[:, 9],
        gains[:, 10],
        grad_w_gate,
        grad_w_up,
        grad_w_down.T,
        gains[:, 2],
        grad_gate,
        grad_proj,
        gains[:, 3],
    )


def solution(mesh):
    rows, cols, tops = P("ctx", "wt"), P("wt", "ctx"), P("ctx")
    down, across = P(None, "wt"), P("wt", None)
    return jax.shard_map(
        local,
        mesh=mesh,
        in_specs=(
            P("ctx", None),
            P("ctx", "wt"),
            P("ctx", None),
            P(),
            P(),
            P(),
            P(),
            P(),
            down,
            down,
            down,
            across,
            P(),
            down,
            across,
            P(),
            P(),
            down,
            down,
            across,
            P(),
            down,
            across,
            P(),
        ),
        out_specs=(
            P("ctx", None),
            P("ctx", None),
            rows,
            tops,
            tops,
            tops,
            rows,
            rows,
            rows,
            cols,
            tops,
            rows,
            cols,
            tops,
            tops,
            rows,
            rows,
            cols,
            tops,
            rows,
            cols,
            tops,
        ),
        check_vma=False,
    )
```

```python
import jax
import jax.numpy as jnp
from jax import lax
from jax.experimental import pallas as pl
from jax.experimental.pallas import tpu as pltpu
from jax.sharding import PartitionSpec as P

EPS = 1e-06
ROPE_BASE = 1000000.0
ROOT_HALF = 0.7071067811865476
GELU_A = 0.7978845608028654
GELU_B = 0.044715
STRETCH = 128
HEAD = 256
SLOTS = 64
PAD_SLOTS = 72
CHUNK = 4
D = 2048
VMEM_GRANT = 60 * 1024 * 1024
BF = jnp.bfloat16
F32 = jnp.float32


def hop(value, axis, mask):
    return lax.ppermute(value, axis, [(i, i ^ mask) for i in range(lax.axis_size(axis))])


def pick(value, index, axis):
    return lax.dynamic_index_in_dim(value, index, axis, keepdims=False)


def ctx_of(y, z, x):
    return (y * 2 + z) * 4 + x


GROUP_X = [[ctx_of(y, z, x) for x in range(4)] for y in range(4) for z in range(2)]
GROUP_Y = [[ctx_of(y, z, x) for y in range(4)] for z in range(2) for x in range(4)]
GROUP_Z = [[ctx_of(y, z, x) for z in range(2)] for y in range(4) for x in range(4)]


def gather_group(value, groups):
    return lax.all_gather(value, "ctx", axis=0, axis_index_groups=groups)


def scatter_group(value, groups):
    return lax.psum_scatter(
        value, "ctx", scatter_dimension=0, axis_index_groups=groups, tiled=True
    )


def gate_kernel(*refs):
    pass


def hold(values, event):
    return pl.pallas_call(
        gate_kernel,
        out_shape=tuple(jax.ShapeDtypeStruct(value.shape, value.dtype) for value in values),
        in_specs=[pl.BlockSpec(memory_space=pl.ANY)] * (len(values) + 1),
        out_specs=(pl.BlockSpec(memory_space=pl.ANY),) * len(values),
        input_output_aliases={i: i for i in range(len(values))},
        name="gate",
    )(*values, event)


def ring_gather(block, near, other):
    one = hop(block, "ctx", near)
    two = hop(block, "ctx", other)
    half = block.shape[0] // 2
    return [
        block,
        one,
        two,
        hop(one[:half], "ctx", other),
        hop(two[half:], "ctx", near),
    ]


def gather_wt(own):
    near = hop(own, "wt", 2)
    core = hop(own, "wt", 1)
    far = hop(near, "wt", 1)
    return own, near, core, far


def scatter_wt(kept, sent):
    kept = kept + hop(sent, "wt", 1).astype(F32)
    quarter = kept.shape[0] // 2
    return kept[:quarter], hop(kept[quarter:].astype(BF), "wt", 2)


def fold(kept, sent, mask):
    return (kept.astype(F32) + hop(sent, "ctx", mask).astype(F32)).astype(BF)


def swap_halves(value):
    half = value.shape[0] // 2
    return jnp.concatenate([value[half:], value[:half]], axis=0)


def dot(left, right):
    return jnp.dot(left, right, preferred_element_type=F32)


def dot_rows(left, right):
    return lax.dot_general(left, right, (((0,), (0,)), ((), ())), preferred_element_type=F32)


def dot_cols(left, right):
    return lax.dot_general(left, right, (((1,), (1,)), ((), ())), preferred_element_type=F32)


def halves_of(value):
    high = value.astype(BF)
    return high, (value - high.astype(F32)).astype(BF)


def fine(left, right):
    high, low = halves_of(left)
    return dot(high, right) + dot(low, right)


def fine_cols(left, right):
    high, low = halves_of(left)
    return dot_cols(high, right) + dot_cols(low, right)


def rms(values):
    return lax.rsqrt(jnp.mean(values * values, axis=-1, keepdims=True) + EPS)


def norm_back(grad, normal, scale, gain):
    inner = grad * gain
    back = scale * (inner - normal * jnp.mean(inner * normal, axis=-1, keepdims=True))
    return back, jnp.sum(grad * normal, axis=0, keepdims=grad.ndim == 2)


def rotate(values, cosine, sine):
    half = values.shape[-1] // 2
    front, rear = values[..., :half], values[..., half:]
    return jnp.concatenate([front * cosine - rear * sine, rear * cosine + front * sine], axis=-1)


def gelu_parts(value):
    square = value * value
    bend = jnp.tanh(GELU_A * value * (1.0 + GELU_B * square))
    half = 0.5 * (1.0 + bend)
    slope = half + 0.5 * value * (1.0 - bend * bend) * GELU_A * (1.0 + 3.0 * GELU_B * square)
    return value * half, slope


AT_V = PAD_SLOTS
AT_HI = 2 * PAD_SLOTS
AT_LO = AT_HI + 2
AT_Z = AT_LO + 2
AT_ENDS = AT_Z + 1


def piece_copies(pieces, held, sem):
    copies, at = [], 0
    for i, piece in enumerate(pieces):
        count = piece.shape[0]
        place = held.at[pl.ds(at, count)]
        copies.append(pltpu.make_async_copy(piece, place, sem.at[i]))
        at += count
    return copies


def load_pieces(pieces, held, sem):
    copies = piece_copies(pieces, held, sem)
    for copy in copies:
        copy.start()
    for copy in copies:
        copy.wait()


def query_places(meta, tile, shape, along):
    row = lax.broadcasted_iota(jnp.int32, shape, along) & (STRETCH - 1)
    row = (row + 64 * meta[AT_Z]) & (STRETCH - 1)
    place = meta[AT_HI + tile] * STRETCH + row
    start = jnp.zeros(shape, jnp.int32)
    for j in range(8):
        end = meta[AT_ENDS + j]
        start = jnp.maximum(start, jnp.where(place >= end, end, 0))
    return place, start


def key_places(meta, first, shape, along):
    at = lax.broadcasted_iota(jnp.int32, shape, along)
    row = ((at & (STRETCH - 1)) + 64 * meta[AT_Z]) & (STRETCH - 1)
    return first * STRETCH + (at - (at & (STRETCH - 1))) + row


def tile_of(ref, tile):
    rows = pl.ds(tile * STRETCH, STRETCH)
    return jnp.concatenate([ref[rows, :HEAD], ref[rows, HEAD:]], axis=0)


def stretches(meta, held, at, first):
    return jnp.concatenate([held[meta[at + first + u]] for u in range(CHUNK)], axis=0)


def turns_of(meta, tile):
    return (meta[AT_HI + tile] - meta[AT_LO + tile] + CHUNK) // CHUNK


def forward_kernel(meta, q_ref, w_ref, *refs):
    pieces, (low_ref, full_ref, lse_ref, kept_ref, sent_ref) = refs[:20], refs[20:25]
    held, acc, total, sem = refs[25:]
    load_pieces(pieces, held, sem)
    for tile in range(2):
        query = tile_of(q_ref, tile)
        place, start = query_places(meta, tile, (2 * STRETCH, 1), 0)
        acc[...] = jnp.zeros_like(acc)
        total[...] = jnp.zeros_like(total)

        def turn(i, carry):
            first = meta[AT_LO + tile] + CHUNK * i
            keys = stretches(meta, held, 0, first)
            values = stretches(meta, held, AT_V, first)
            scores = dot_cols(query, keys)
            key_at = key_places(meta, first, (1, CHUNK * STRETCH), 1)
            allowed = (key_at <= place) & (key_at >= start)
            weights = jnp.where(allowed, jnp.exp(scores), 0.0)
            part = weights[:, :STRETCH]
            for u in range(1, CHUNK):
                part = part + weights[:, u * STRETCH : (u + 1) * STRETCH]
            total[...] += part
            acc[...] += dot(weights.astype(BF), values)
            return carry

        lax.fori_loop(0, turns_of(meta, tile), turn, 0)
        row_total = jnp.sum(total[...], axis=1, keepdims=True)
        result = acc[...] / row_total
        rows = pl.ds(tile * STRETCH, STRETCH)
        for head in range(2):
            block = result[head * STRETCH : (head + 1) * STRETCH]
            low_ref[rows, head * HEAD : (head + 1) * HEAD] = block.astype(BF)
            full_ref[rows, head * HEAD : (head + 1) * HEAD] = block
        logs = jnp.broadcast_to(jnp.log(row_total), (2 * STRETCH, STRETCH))
        lse_ref[tile] = jnp.transpose(logs)[:8]
    kept_ref[...] = dot(low_ref[:STRETCH], w_ref[...])
    sent_ref[...] = dot(low_ref[STRETCH:], w_ref[...]).astype(BF)


def backward_kernel(meta, q_ref, full_ref, lse_ref, w_ref, *refs):
    parts, pieces, dq_ref, outs = refs[:4], refs[4:24], refs[-10], refs[-9:-5]
    held, grads, acc, g_ref, sem = refs[-5:]
    copies = piece_copies(pieces, held, sem)
    for copy in copies:
        copy.start()
    for i, part in enumerate(parts):
        g_ref[64 * i : 64 * (i + 1)] = dot_cols(part[...], w_ref[...]).astype(BF)
    grads[...] = jnp.zeros_like(grads)
    for copy in copies:
        copy.wait()
    for tile in range(2):
        query = tile_of(q_ref, tile)
        grad = tile_of(g_ref, tile)
        full = tile_of(full_ref, tile)
        place, start = query_places(meta, tile, (1, 2 * STRETCH), 1)
        lse = lse_ref[tile][:1]
        delta = jnp.sum(grad.astype(F32) * full, axis=1, keepdims=True)
        delta = jnp.transpose(jnp.broadcast_to(delta, (2 * STRETCH, STRETCH)))[:1]
        acc[...] = jnp.zeros_like(acc)

        def turn(i, carry):
            first = meta[AT_LO + tile] + CHUNK * i
            keys = stretches(meta, held, 0, first)
            values = stretches(meta, held, AT_V, first)
            key_at = key_places(meta, first, (CHUNK * STRETCH, 1), 0)
            allowed = (key_at <= place) & (key_at >= start)
            weights = jnp.where(allowed, jnp.exp(dot_cols(keys, query) - lse), 0.0)
            slopes = (weights * (dot_cols(values, grad) - delta)).astype(BF)
            key_term = dot(slopes, query)
            value_term = dot(weights.astype(BF), grad)
            acc[...] += dot_rows(slopes, keys)
            for u in range(CHUNK):
                part = slice(u * STRETCH, (u + 1) * STRETCH)
                for at, term in ((meta[first + u], key_term), (meta[AT_V + first + u], value_term)):
                    grads[at] = (grads[at].astype(F32) + term[part]).astype(BF)
            return carry

        lax.fori_loop(0, turns_of(meta, tile), turn, 0)
        rows = pl.ds(tile * STRETCH, STRETCH)
        for head in range(2):
            block = acc[head * STRETCH : (head + 1) * STRETCH]
            dq_ref[rows, head * HEAD : (head + 1) * HEAD] = block * (HEAD**-0.5)
    copies = []
    for side in range(2):
        for h in range(2):
            at = 64 * side + 32 * h
            for out, first, count, begin in ((0, 24, 8, 8 * h), (1, 0, 24, 24 * h)):
                copies.append(
                    pltpu.make_async_copy(
                        grads.at[pl.ds(at + first, count)],
                        outs[2 * side + out].at[pl.ds(begin, count)],
                        sem.at[len(copies)],
                    )
                )
    for copy in copies:
        copy.start()
    for copy in copies:
        copy.wait()


def in_vmem():
    return pl.BlockSpec(memory_space=pltpu.VMEM)


def anywhere():
    return pl.BlockSpec(memory_space=pl.ANY)


def attend_forward(meta, query, w_attn_out, pieces):
    rows, width = query.shape[0], w_attn_out.shape[1]
    return pl.pallas_call(
        forward_kernel,
        out_shape=(
            jax.ShapeDtypeStruct((rows, 2 * HEAD), BF),
            jax.ShapeDtypeStruct((rows, 2 * HEAD), F32),
            jax.ShapeDtypeStruct((2, 8, 2 * STRETCH), F32),
            jax.ShapeDtypeStruct((STRETCH, width), F32),
            jax.ShapeDtypeStruct((STRETCH, width), BF),
        ),
        in_specs=[pl.BlockSpec(memory_space=pltpu.SMEM), in_vmem(), in_vmem()] + [anywhere()] * 20,
        out_specs=(in_vmem(),) * 5,
        scratch_shapes=[
            pltpu.VMEM((2 * SLOTS, STRETCH, HEAD), BF),
            pltpu.VMEM((2 * STRETCH, HEAD), F32),
            pltpu.VMEM((2 * STRETCH, STRETCH), F32),
            pltpu.SemaphoreType.DMA((20,)),
        ],
        compiler_params=pltpu.CompilerParams(vmem_limit_bytes=VMEM_GRANT),
        cost_estimate=pl.CostEstimate(
            flops=3 * 10**9, bytes_accessed=10**7, transcendentals=2 * 10**6
        ),
        name="attend_forward",
    )(meta, query, w_attn_out, *pieces)


def attend_backward(meta, query, full, lse, w_attn_out, parts, pieces, *events):
    rows = query.shape[0]
    outs = pl.pallas_call(
        backward_kernel,
        out_shape=(jax.ShapeDtypeStruct((rows, 2 * HEAD), F32),)
        + tuple(jax.ShapeDtypeStruct((count, STRETCH, HEAD), BF) for count in (16, 48, 16, 48)),
        in_specs=[pl.BlockSpec(memory_space=pltpu.SMEM)] + [in_vmem()] * 8
        + [anywhere()] * (20 + len(events)),
        out_specs=(in_vmem(),) + (anywhere(),) * 4,
        scratch_shapes=[
            pltpu.VMEM((2 * SLOTS, STRETCH, HEAD), BF),
            pltpu.VMEM((2 * SLOTS, STRETCH, HEAD), BF),
            pltpu.VMEM((2 * STRETCH, HEAD), F32),
            pltpu.VMEM((rows, 2 * HEAD), BF),
            pltpu.SemaphoreType.DMA((20,)),
        ],
        compiler_params=pltpu.CompilerParams(vmem_limit_bytes=VMEM_GRANT),
        cost_estimate=pl.CostEstimate(
            flops=10**10, bytes_accessed=2 * 10**7, transcendentals=2 * 10**6
        ),
        name="attend_backward",
    )(meta, query, full, lse, w_attn_out, *parts, *pieces, *events)
    return outs[0], outs[1:]


UNITS = 512


def ff_forward_kernel(*refs):
    parts, (w_gate, w_up, w_down) = refs[:4], refs[4:7]
    gate_out, up_out, pre_out, act_out, kept, sent = refs[7:13]
    now, acc = refs[13:]
    turn = pl.program_id(0)

    @pl.when(turn == 0)
    def first():
        for i, part in enumerate(parts):
            pre_out[64 * i : 64 * (i + 1)] = part[...]
        acc[...] = jnp.zeros_like(acc)

    gate = dot(pre_out[...], w_gate[...])
    up = dot(pre_out[...], w_up[...])
    gate_out[...] = gate
    up_out[...] = up
    now[...] = (gelu_parts(gate)[0] * up).astype(BF)
    act_out[...] = now[...]
    acc[...] += dot(now[...], w_down[...])

    @pl.when(turn == pl.num_programs(0) - 1)
    def last():
        kept[...] = acc[:STRETCH]
        sent[...] = acc[STRETCH:].astype(BF)


def ff_forward(parts, w_gate, w_up, w_down):
    width, units = w_gate.shape
    rows = 4 * parts[0].shape[0]
    whole = lambda shape: pl.BlockSpec(shape, lambda i: (0, 0))
    tall, flat = pl.BlockSpec((width, UNITS), lambda i: (0, i)), pl.BlockSpec((UNITS, width), lambda i: (i, 0))
    strip = pl.BlockSpec((rows, UNITS), lambda i: (0, i))
    return pl.pallas_call(
        ff_forward_kernel,
        grid=(units // UNITS,),
        out_shape=(
            jax.ShapeDtypeStruct((rows, units), F32),
            jax.ShapeDtypeStruct((rows, units), F32),
            jax.ShapeDtypeStruct((rows, width), BF),
            jax.ShapeDtypeStruct((rows, units), BF),
            jax.ShapeDtypeStruct((rows // 2, width), F32),
            jax.ShapeDtypeStruct((rows // 2, width), BF),
        ),
        in_specs=[whole((rows // 4, width))] * 4 + [tall, tall, flat],
        out_specs=(
            strip,
            strip,
            whole((rows, width)),
            strip,
            whole((rows // 2, width)),
            whole((rows // 2, width)),
        ),
        scratch_shapes=[pltpu.VMEM((rows, UNITS), BF), pltpu.VMEM((rows, width), F32)],
        compiler_params=pltpu.CompilerParams(vmem_limit_bytes=VMEM_GRANT),
        cost_estimate=pl.CostEstimate(
            flops=6 * rows * width * units, bytes_accessed=3 * 10**7, transcendentals=rows * units
        ),
        name="ff_forward",
    )(*parts, w_gate, w_up, w_down)


def ff_grads_kernel(me, *refs):
    parts, (gate_ref, up_ref, w_down) = refs[:4], refs[4:7]
    cuts, quarters, all_in = refs[7:11], refs[11:15], refs[15]
    block = pl.program_id(0)

    @pl.when(block == 0)
    def first():
        for i, part in enumerate(parts):
            all_in[64 * i : 64 * (i + 1)] = part[...]
        for k in range(4):
            at = pl.multiple_of((me[1] ^ k) * 512, 512)
            quarters[k][...] = all_in[:, pl.ds(at, 512)]

    grad_act = dot_cols(all_in[...], w_down[...])
    value, slope = gelu_parts(gate_ref[...])
    for k in range(4):

        @pl.when(block == k)
        def store():
            cuts[k][:, :UNITS] = (grad_act * up_ref[...] * slope).astype(BF)
            cuts[k][:, UNITS:] = (grad_act * value).astype(BF)


def ff_grads(me, parts, gate_pre, up_pre, w_down):
    units, width = w_down.shape
    rows = gate_pre.shape[0]
    whole = lambda shape: pl.BlockSpec(shape, lambda k, me: (0, 0))
    flat = pl.BlockSpec((UNITS, width), lambda k, me: (k ^ me[0], 0))
    strip = pl.BlockSpec((rows, UNITS), lambda k, me: (0, k ^ me[0]))
    outs = pl.pallas_call(
        ff_grads_kernel,
        grid_spec=pltpu.PrefetchScalarGridSpec(
            num_scalar_prefetch=1,
            grid=(4,),
            in_specs=[whole((rows // 4, width))] * 4 + [strip, strip, flat],
            out_specs=(whole((rows, 2 * UNITS)),) * 4 + (whole((rows, width // 4)),) * 4,
            scratch_shapes=[pltpu.VMEM((rows, width), BF)],
        ),
        out_shape=(jax.ShapeDtypeStruct((rows, 2 * UNITS), BF),) * 4
        + (jax.ShapeDtypeStruct((rows, width // 4), BF),) * 4,
        compiler_params=pltpu.CompilerParams(vmem_limit_bytes=VMEM_GRANT),
        cost_estimate=pl.CostEstimate(
            flops=2 * rows * width * units, bytes_accessed=10**7, transcendentals=rows * units
        ),
        name="ff_grads",
    )(me, *parts, gate_pre, up_pre, w_down)
    return outs[:4], outs[4:]


def ff_back_kernel(me, *refs):
    cuts, (w_gate, w_up, kept, sent, acc) = refs[:4], refs[4:]
    block = pl.program_id(0)

    @pl.when(block == 0)
    def first():
        acc[...] = jnp.zeros_like(acc)

    for k in range(4):

        @pl.when(block == k)
        def add():
            term = dot_cols(cuts[k][:, :UNITS], w_gate[...])
            acc[...] += term + dot_cols(cuts[k][:, UNITS:], w_up[...])

    @pl.when(block == 3)
    def last():
        kept[...] = acc[:STRETCH]
        sent[...] = acc[STRETCH:].astype(BF)


def ff_back(me, cuts, w_gate, w_up):
    width, units = w_gate.shape
    rows = cuts[0].shape[0]
    whole = lambda shape: pl.BlockSpec(shape, lambda k, me: (0, 0))
    tall = pl.BlockSpec((width, UNITS), lambda k, me: (0, k ^ me[0]))
    return pl.pallas_call(
        ff_back_kernel,
        grid_spec=pltpu.PrefetchScalarGridSpec(
            num_scalar_prefetch=1,
            grid=(4,),
            in_specs=[whole((rows, 2 * UNITS))] * 4 + [tall, tall],
            out_specs=(whole((rows // 2, width)),) * 2,
            scratch_shapes=[pltpu.VMEM((rows, width), F32)],
        ),
        out_shape=(
            jax.ShapeDtypeStruct((rows // 2, width), F32),
            jax.ShapeDtypeStruct((rows // 2, width), BF),
        ),
        compiler_params=pltpu.CompilerParams(vmem_limit_bytes=VMEM_GRANT),
        cost_estimate=pl.CostEstimate(
            flops=4 * rows * width * units, bytes_accessed=2 * 10**7, transcendentals=0
        ),
        name="ff_back",
    )(me, *cuts, w_gate, w_up)


def relative_rows(spots, stream):
    return jnp.concatenate(
        [stream[pl.ds(pl.multiple_of(spots[i], 64), 64)] for i in range(4)], axis=0
    )


def swapped(value):
    return jnp.concatenate([value[STRETCH:], value[:STRETCH]], axis=0)


def input_kernel(spots, stream, w_key, w_value, g_in, normed_out, mine, theirs):
    rows = relative_rows(spots, stream).astype(F32)
    normed_out[...] = (rows * rms(rows) * g_in[...]).astype(BF)
    key, value = dot(normed_out[...], w_key[...]), dot(normed_out[...], w_value[...])
    first = spots[4] == 0
    mine[...] = jnp.where(first, key, value)
    theirs[...] = swapped(jnp.where(first, value, key))


def kind_kernel(spots, mine, came, cosine, sine, gain, low_out, full_out):
    first = spots[4] == 0
    kind = jnp.concatenate(
        [jnp.where(first, mine[...], came[...]), jnp.where(first, came[...], mine[...])], axis=1
    )
    full_out[...] = kind
    turn = (jnp.where(first, cosine[...], 1.0), jnp.where(first, sine[...], 0.0))
    scaled = kind * rms(kind) * jnp.where(first, gain[...], 1.0)
    low_out[...] = rotate(scaled, *turn).astype(BF)


def lay_kernel(*refs):
    for h in range(2):
        for i in range(4):
            refs[8 + h][256 * i : 256 * (i + 1)] = refs[4 * h + i][...]


def kind_back_kernel(spots, sums_a, sums_b, came, kind_ref, cosine, sine, gain, event, home, away, gains):
    first = spots[4] == 0
    turn = (jnp.where(first, cosine[...], 1.0), jnp.where(first, -sine[...], 0.0))
    grad = jnp.concatenate([sums_a[...] + came[0].astype(F32), sums_b[...] + came[1].astype(F32)], axis=0)
    kind = kind_ref[...]
    scale = rms(kind)
    grad, gain_part = norm_back(
        rotate(grad, *turn), kind * scale, scale, jnp.where(first, gain[...], 1.0)
    )
    gains[...] = jnp.where(first, gain_part, 0.0)
    half = HEAD // 2
    home[...] = jnp.where(first, grad[:, :half], grad[:, half:]).astype(BF)
    away[...] = swapped(jnp.where(first, grad[:, half:], grad[:, :half])).astype(BF)


def query_kernel(normed, w_query, cosine, sine, gain, event, low_out, raw_out):
    for head in range(2):
        at = slice(head * HEAD, (head + 1) * HEAD)
        raw = dot(normed[...], w_query[:, at])
        raw_out[:, at] = raw
        turned = rotate(raw * rms(raw) * gain[...], cosine[...], sine[...]).astype(BF)
        low_out[:, at] = (turned.astype(F32) * HEAD**-0.5).astype(BF)


def query_back_kernel(grad_ref, raw_ref, cosine, sine, gain, event, low_out, gains):
    gains[...] = jnp.zeros_like(gains)
    for head in range(2):
        at = slice(head * HEAD, (head + 1) * HEAD)
        raw = raw_ref[:, at]
        scale = rms(raw)
        grad, part = norm_back(
            rotate(grad_ref[:, at], cosine[...], -sine[...]), raw * scale, scale, gain[...]
        )
        low_out[:, at] = grad.astype(BF)
        gains[...] += part


def normed_back_kernel(spots, home, came, query, w_query, w_key, w_value, stream, *outs):
    kept, sent, gain_out, cuts = outs[-7], outs[-6], outs[-5], outs[-4:]
    first = spots[4] == 0
    key = jnp.where(first, home[...].astype(F32), came[...].astype(F32)).astype(BF)
    value = jnp.where(first, came[...].astype(F32), home[...].astype(F32)).astype(BF)
    part = dot_cols(query[...], w_query[...])
    part = part + dot_cols(key, w_key[...]) + dot_cols(value, w_value[...])
    kept[...] = part[:STRETCH]
    sent[...] = part[STRETCH:].astype(BF)
    rows = relative_rows(spots, stream).astype(F32)
    gain_out[...] = jnp.sum(part * (rows * rms(rows)), axis=0, keepdims=True)
    for k, cut in enumerate(cuts):
        at = spots[5] ^ k
        cut[:, :128] = query[:, pl.ds(pl.multiple_of(at * 128, 128), 128)]
        side = jnp.where(at >= 2, value.astype(F32), key.astype(F32))
        side = jnp.where((at & 1) == 1, side[:, 64:], side[:, :64])
        cut[:, 128:] = side.astype(BF)


def far_kernel(own, came, *refs):
    for i, out in enumerate(refs[-4:]):
        at = slice(4 * i, 4 * i + 4)
        out[...] = (own[at].astype(F32) + came[at].astype(F32)).astype(BF)


def near_kernel(own, came, *refs):
    passed, (base_a, base_b), sends = refs[:4], refs[-6:-4], refs[-4:]

    def summed(first, count):
        at = slice(first, first + count)
        return own[at].astype(F32) + came[at].astype(F32)

    for h, base in enumerate((base_a, base_b)):
        near, other = sends[2 * h], sends[2 * h + 1]
        base[...] = summed(24 * h, 8)
        near[:4] = summed(24 * h + 8, 4).astype(BF)
        near[4:] = (summed(24 * h + 12, 4) + passed[2 * h + 1][...].astype(F32)).astype(BF)
        other[:4] = (summed(24 * h + 16, 4) + passed[2 * h][...].astype(F32)).astype(BF)
        other[4:] = summed(24 * h + 20, 4).astype(BF)


def inner_kernel(base_a, base_b, *refs):
    came, kept, sends = refs[:4], refs[-8:-6], refs[-6:]
    for h, base in enumerate((base_a, base_b)):
        total = base[...] + came[2 * h][...].astype(F32) + came[2 * h + 1][...].astype(F32)
        kept[h][...] = total[:2]
        for k in (1, 2, 3):
            sends[3 * h + k - 1][...] = total[2 * k : 2 * k + 2].astype(BF)


def last_kernel(kept_a, kept_b, *refs):
    came, kept, send = refs[:6], refs[6:8], refs[8]
    for h, base in enumerate((kept_a, kept_b)):
        total = base[...]
        for k in range(3):
            total = total + came[3 * h + k][...].astype(F32)
        kept[h][...] = total[0]
        send[h] = total[1].astype(BF)


def mid_kernel(kept, came, stream, left, right, g_in, g_attn, g_laurel, g_pre, *outs):
    pre_out, resid_out, attn_out, laurel_out, low_out = outs
    rows = stream[...].astype(F32)
    normed = rows * rms(rows) * g_in[...]
    attn = kept[...] + came[...].astype(F32)
    low = dot_cols(normed.astype(BF), left[...])
    laurel = fine(low, right[...])
    resid = (
        rows + attn * rms(attn) * g_attn[...] + normed + laurel * rms(laurel) * g_laurel[...]
    ) * ROOT_HALF
    pre_out[...] = (resid * rms(resid) * g_pre[...]).astype(BF)
    resid_out[...] = resid
    attn_out[...] = attn
    laurel_out[...] = laurel
    low_out[...] = low


def join_kernel(kept, came, resid, top, inputs, gate_t, proj, g_post, g_join, event, *outs):
    ff_out, after_out, results, gains, mine, theirs = outs
    ff = kept[...] + came[...].astype(F32)
    ff_scale = rms(ff)
    ff_normal = ff * ff_scale
    after = resid[...] + ff_normal * g_post[...]
    value, slope = gelu_parts(fine_cols(after, gate_t[...]))
    channels = inputs[...].astype(F32)
    joined = value * channels
    join = fine(joined, proj[...])
    join_scale = rms(join)
    join_normal = join * join_scale
    results[:, :D] = (after + join_normal * g_join[...]).astype(BF)
    grad = top[...].astype(F32)
    grad_join, gain_join = norm_back(grad, join_normal, join_scale, g_join[...])
    grad_joined = fine_cols(grad_join, proj[...])
    grad_pre = grad_joined * channels * slope
    results[:, D:] = (grad_joined * value).astype(BF)
    grad_after = grad + fine(grad_pre, gate_t[...])
    after_out[...] = grad_after
    grad_ff, gain_post = norm_back(grad_after, ff_normal, ff_scale, g_post[...])
    ff_out[...] = grad_ff.astype(BF)
    gains[...] = jnp.zeros_like(gains)
    gains[0:1] = gain_post
    gains[1:2] = gain_join
    low_gate = dot_rows(grad_pre.astype(BF), after.astype(BF)).astype(BF)
    low_proj = dot_rows(joined.astype(BF), grad_join.astype(BF)).astype(BF)
    for k, (out, i) in enumerate(((mine, 0), (theirs, 0), (mine, 1), (theirs, 1))):
        out[i, :64] = low_gate[64 * k : 64 * (k + 1)]
        out[i, 64:] = low_proj[64 * k : 64 * (k + 1)]


def resid_kernel(
    kept,
    came,
    resid,
    after,
    attn,
    laurel,
    low,
    stream,
    left,
    right,
    g_in,
    g_attn,
    g_laurel,
    g_pre,
    gates_mine,
    gates_sent,
    *refs,
):
    attn_out, branch_out, own_out, gains, mine, theirs = refs[-6:]
    mine[:, 32:] = gates_mine[...]
    theirs[:, 32:] = gates_sent[...]
    scale = rms(resid[...])
    grad = kept[...] + came[...].astype(F32)
    grad_resid, gain_pre = norm_back(grad, resid[...] * scale, scale, g_pre[...])
    branch = (after[...] + grad_resid) * ROOT_HALF
    branch_out[...] = branch
    scale = rms(attn[...])
    grad_attn, gain_attn = norm_back(branch, attn[...] * scale, scale, g_attn[...])
    attn_out[...] = grad_attn.astype(BF)
    scale = rms(laurel[...])
    grad_laurel, gain_laurel = norm_back(branch, laurel[...] * scale, scale, g_laurel[...])
    grad_low = fine_cols(grad_laurel, right[...])
    own = branch + fine(grad_low, left[...])
    own_out[...] = own
    rows = stream[...].astype(F32)
    normal = rows * rms(rows)
    gains[...] = jnp.zeros_like(gains)
    gains[0:1] = gain_attn
    gains[1:2] = gain_laurel
    gains[2:3] = gain_pre
    gains[3:4] = jnp.sum(own * normal, axis=0, keepdims=True)
    low_left = dot_rows(grad_low.astype(BF), (normal * g_in[...]).astype(BF)).astype(BF)
    low_right = dot_rows(low[...].astype(BF), grad_laurel.astype(BF)).astype(BF)
    for k, (out, i) in enumerate(((mine, 0), (theirs, 0), (mine, 1), (theirs, 1))):
        out[i, :16] = low_left[16 * k : 16 * (k + 1)]
        out[i, 16:32] = low_right[16 * k : 16 * (k + 1)]


def final_kernel(kept, came, own, branch, stream, g_in, event, out):
    rows = stream[...].astype(F32)
    scale = rms(rows)
    grad = own[...] + kept[...] + came[...].astype(F32)
    extra, _ = norm_back(grad, rows * scale, scale, g_in[...])
    out[...] = (branch[...] + extra).astype(BF)


def in_one(kernel, shapes, args, name, event=(), spots=(), scratch=()):
    return pl.pallas_call(
        kernel,
        out_shape=tuple(jax.ShapeDtypeStruct(shape, kind) for shape, kind in shapes),
        in_specs=[pl.BlockSpec(memory_space=pltpu.SMEM)] * len(spots)
        + [in_vmem()] * len(args)
        + [anywhere()] * len(event),
        out_specs=(in_vmem(),) * len(shapes),
        scratch_shapes=list(scratch),
        compiler_params=pltpu.CompilerParams(vmem_limit_bytes=VMEM_GRANT),
        cost_estimate=pl.CostEstimate(flops=10**9, bytes_accessed=5 * 10**6, transcendentals=10**5),
        name=name,
    )(*spots, *args, *event)


def pack_kernel(left, right, gate_w, proj, inputs, event, out):
    unit = (
        lax.broadcasted_iota(jnp.int32, (64, 64), 0) == lax.broadcasted_iota(jnp.int32, (64, 64), 1)
    ).astype(BF)
    out[:16] = dot_cols(unit[:16, :16], left[...]).astype(BF)
    out[16:32] = right[...]
    out[32:96] = dot_cols(unit, gate_w[...]).astype(BF)
    out[96:160] = proj[...]
    turned = dot_cols(unit, inputs[...]).astype(BF)
    out[160:] = jnp.zeros_like(out[160:])
    for i in range(4):
        out[160:, 256 * i : 256 * (i + 1)] = turned[16 * i : 16 * (i + 1)]


Y_FIRST = (0, 3, 1, 2)
Y_OTHER = (0, 1, 3, 2)


def group_sum(me, group, cuts, at, size):
    total = None
    for k, cut in enumerate(cuts):
        term = dot_rows(group[me ^ k, :, pl.ds(at, size)], cut)
        total = term if total is None else total + term
    return total


def wide_kernel(where, group, *refs):
    cuts, out = refs[:4], refs[-1]
    for at in range(0, D, 256):
        total = group_sum(where[0], group, [cut[...] for cut in cuts], at, 256)
        out[at : at + 256] = total.astype(BF)


def wide_product(where, group, cuts, event):
    return pl.pallas_call(
        wide_kernel,
        out_shape=jax.ShapeDtypeStruct((D, cuts[0].shape[1]), BF),
        in_specs=[pl.BlockSpec(memory_space=pltpu.SMEM)] + [in_vmem()] * 5 + [anywhere()],
        out_specs=in_vmem(),
        compiler_params=pltpu.CompilerParams(vmem_limit_bytes=VMEM_GRANT),
        cost_estimate=pl.CostEstimate(flops=5 * 10**9, bytes_accessed=10**7, transcendentals=0),
        name="wide_product",
    )(where, group, *cuts, event)


def turn_kernel(small, attn, *refs):
    parts, out, grads = refs[:4], refs[-2], refs[-1]
    low = small.shape[0]
    for i, part in enumerate(parts):
        grads[64 * i : 64 * (i + 1)] = part[...]
    unit = (
        lax.broadcasted_iota(jnp.int32, (low, 256), 0)
        == lax.broadcasted_iota(jnp.int32, (low, 256), 1)
    ).astype(BF)
    out[:, :512] = dot_rows(grads[...], attn[...]).astype(BF)
    out[:, 512:] = dot_rows(small[...], unit).astype(BF)


def token_kernel(where, group, gains, *refs):
    cuts, (kept, sent) = refs[:4], refs[4:]
    x, y, z = where[0], where[1], where[2]
    unit = (
        lax.broadcasted_iota(jnp.int32, (16, 64), 0) == lax.broadcasted_iota(jnp.int32, (16, 64), 1)
    ).astype(BF)
    for i, far_y in enumerate(Y_FIRST):
        for far_z in range(2):
            at = pl.multiple_of(((y ^ far_y) * 2 + (z ^ far_z)) * 256, 256)
            total = group_sum(x, group, [cut[...] for cut in cuts], at, 256)
            more = dot_rows(gains[:, pl.ds(at, 256)], unit)
            total = jnp.concatenate([total, more], axis=1).astype(BF)
            (kept, sent)[i // 2][i % 2, far_z] = total


def token_product(where, group, gains, cuts):
    shape = (2, 2, 256, cuts[0].shape[1] + 64)
    return pl.pallas_call(
        token_kernel,
        out_shape=(jax.ShapeDtypeStruct(shape, BF),) * 2,
        in_specs=[pl.BlockSpec(memory_space=pltpu.SMEM)] + [in_vmem()] * 6,
        out_specs=(in_vmem(),) * 2,
        compiler_params=pltpu.CompilerParams(vmem_limit_bytes=VMEM_GRANT),
        cost_estimate=pl.CostEstimate(flops=10**9, bytes_accessed=6 * 10**6, transcendentals=0),
        name="token_product",
    )(where, group, gains, *cuts)


def payload_kernel(where, wide, tokens, turn, *outs):
    for k, out in enumerate(outs):
        at = pl.ds(pl.multiple_of((where[0] ^ k) * 64, 64), 64)
        out[:, :1024] = wide[at]
        out[:, 1024:1280] = tokens[at]
        out[:, 1280:] = turn[at]


def share_kernel(where, *refs):
    shares, down_kept, down_came = refs[:4], refs[4], refs[5]
    gate, up, query, key, value, attn, left, right, join_g, join_p, gains, down = refs[6:]
    x = where[0]

    def turned(rows):
        rows = jnp.concatenate([rows, jnp.zeros_like(rows)], axis=0)
        return jnp.transpose(rows)[:, :64]

    for k, share in enumerate(shares):
        gate[:, pl.ds(pl.multiple_of((x ^ k) * 512, 512), 512)] = share[:, :512].astype(F32)
        up[:, pl.ds(pl.multiple_of((x ^ k) * 512, 512), 512)] = share[:, 512:1024].astype(F32)
        query[:, pl.ds(pl.multiple_of((x ^ k) * 128, 128), 128)] = share[:, 1024:1152].astype(F32)
    quarters = [share[:, 1152:1216].astype(F32) for share in shares]
    placed = []
    for q in range(4):
        choice = quarters[3]
        for k in range(3):
            choice = jnp.where((x ^ k) == q, quarters[k], choice)
        placed.append(choice)
    key[:, :64], key[:, 64:] = placed[0], placed[1]
    value[:, :64], value[:, 64:] = placed[2], placed[3]
    total = shares[0][:, 1216:].astype(F32)
    for share in shares[1:]:
        total = total + share[:, 1216:].astype(F32)
    gains[...] = total[:, :16]
    attn[...] = total[:, 64:576]
    small = total[:, 576:736]
    join_g[...] = small[:, 32:96]
    lines = turned(jnp.concatenate([small, jnp.zeros((64, 96), F32)], axis=1))
    left[...] = lines[:16]
    right[...] = lines[16:32]
    join_p[...] = lines[96:160]
    down[...] = down_kept[...].astype(F32) + down_came[...].astype(F32)


def down_kernel(where, group, *refs):
    cuts, out, total = refs[:4], refs[5], refs[6]
    x, y = where[0], where[1]
    units = group.shape[2]
    for first in range(0, units, 512):
        value = None
        for k, cut in enumerate(cuts):
            term = dot_rows(cut[...], group[y ^ k, :, first : first + 512])
            value = term if value is None else value + term
        total[...] = value
        for i, far_x in enumerate(Y_FIRST):
            for z in range(2):
                at = pl.multiple_of((z * 4 + (x ^ far_x)) * 64, 64)
                out[z, i, :, first : first + 512] = total[pl.ds(at, 64)].astype(BF)


def down_product(where, group, cuts, event):
    return pl.pallas_call(
        down_kernel,
        out_shape=jax.ShapeDtypeStruct((2, 4, 64, group.shape[2]), BF),
        in_specs=[pl.BlockSpec(memory_space=pltpu.SMEM)] + [in_vmem()] * 5 + [anywhere()],
        out_specs=in_vmem(),
        scratch_shapes=[pltpu.VMEM((512, 512), F32)],
        compiler_params=pltpu.CompilerParams(vmem_limit_bytes=VMEM_GRANT),
        cost_estimate=pl.CostEstimate(flops=3 * 10**9, bytes_accessed=10**7, transcendentals=0),
        name="down_product",
    )(where, group, *cuts, event)


def local(
    stream,
    layer_input,
    out_grad,
    doc_lengths,
    stretch_slots,
    gain_input,
    gain_query,
    gain_key,
    w_query,
    w_key,
    w_value,
    w_attn_out,
    gain_attn,
    laurel_left,
    laurel_right,
    gain_laurel,
    gain_pre_ff,
    w_gate,
    w_up,
    w_down,
    gain_post_ff,
    join_gate,
    join_proj,
    gain_join,
):
    wt = lax.axis_index("wt")
    core, zlo = wt & 1, wt >> 1
    ctx = lax.axis_index("ctx")
    at_x, at_z, at_y = ctx & 3, (ctx >> 2) & 1, ctx >> 3
    first_core = core == 0
    half = HEAD // 2

    def starts(k):
        return ((core ^ (k & 1)) * 2 + (zlo ^ (k >> 1))) * 64

    def natural(blocks):
        stacked = jnp.stack(blocks)
        return jnp.concatenate(
            [pick(stacked, wt ^ ((b & 1) * 2 + (b >> 1)), 0) for b in range(4)], axis=0
        )

    stream_own = lax.dynamic_slice_in_dim(stream, starts(0), 64, 0)
    grad_top = lax.dynamic_slice_in_dim(out_grad, starts(0), 64, 0)
    where = jnp.stack([at_x, at_y, at_z])
    spots = (jnp.stack([starts(0), starts(2), starts(1), starts(3), core, at_x]),)
    g_in, g_attn, g_laurel, g_pre, g_post, g_join = (
        gain[None, :]
        for gain in (gain_input, gain_attn, gain_laurel, gain_pre_ff, gain_post_ff, gain_join)
    )

    doc_ends = jnp.cumsum(doc_lengths)
    tiles = [lax.dynamic_index_in_dim(stretch_slots, 2 * ctx + (core ^ t), 0) for t in range(2)]
    hi = jnp.concatenate(tiles)
    lo = jnp.max(
        jnp.where(doc_ends[None, :] <= hi[:, None] * STRETCH, doc_ends[None, :], 0), axis=1
    )
    lo = lo // STRETCH
    row = (jnp.arange(STRETCH, dtype=jnp.int32) + 64 * zlo) & (STRETCH - 1)
    positions = (hi[:, None] * STRETCH + row[None, :]).reshape(-1)
    names = jnp.arange(SLOTS, dtype=jnp.int32)
    slot_of = jnp.sum(jnp.where(stretch_slots[None, :] == names[:, None], names[None, :], 0), axis=1)
    relative = (slot_of >> 1) ^ ctx
    rel_x, rel_z, rel_y = relative & 3, (relative >> 2) & 1, relative >> 3
    places = (
        (rel_y ^ (rel_y >> 1)) * 8 + rel_x * 2 + rel_z,
        SLOTS // 2 + (rel_x ^ (rel_x >> 1)) * 8 + rel_y * 2 + rel_z,
    )
    second = (slot_of & 1) == 1
    key_at = core * SLOTS + jnp.where(second, places[1], places[0])
    value_at = (1 - core) * SLOTS + jnp.where(second, places[0], places[1])
    blank = jnp.zeros((PAD_SLOTS - SLOTS,), jnp.int32)
    meta = jnp.concatenate([key_at, blank, value_at, blank, hi, lo, zlo[None], doc_ends]).astype(
        jnp.int32
    )
    exponents = jnp.arange(half, dtype=F32) * (2.0 / HEAD)
    angles = positions.astype(F32)[:, None] * (1.0 / ROPE_BASE**exponents)[None, :]
    cosine, sine = jnp.cos(angles), jnp.sin(angles)

    half_rows, heads_b = ((2 * STRETCH, half), F32), ((2 * STRETCH, 2 * HEAD), BF)
    normed_b, mine, theirs = in_one(
        input_kernel,
        (((2 * STRETCH, D), BF), half_rows, half_rows),
        (stream, w_key, w_value, g_in),
        "input",
        spots=spots,
    )
    kind_b, kind = in_one(
        kind_kernel,
        (((2 * STRETCH, HEAD), BF), ((2 * STRETCH, HEAD), F32)),
        (mine, hop(theirs, "wt", 1), cosine, sine, gain_key[None, :]),
        "kind",
        spots=spots,
    )

    across = hop(kind_b, "ctx", 4)
    groups = []
    for h, one in enumerate((1, 8)):
        rows = slice(h * STRETCH, (h + 1) * STRETCH)
        block = jnp.concatenate([kind_b[rows], across[rows]], axis=0)
        groups.append([block] + [hop(block, "ctx", k * one) for k in (1, 2, 3)])
    quads = in_one(lay_kernel, (((1024, HEAD), BF),) * 2, (*groups[0], *groups[1]), "lay")
    pieces = ring_gather(quads[0], 8, 24) + ring_gather(quads[1], 1, 3)
    pieces += [hop(piece, "wt", 1) for piece in pieces]
    pieces = [piece.reshape(-1, STRETCH, HEAD) for piece in pieces]

    (pack,) = in_one(
        pack_kernel,
        (((176, D), BF),),
        (laurel_left, laurel_right, join_gate, join_proj, layer_input),
        "pack",
        (quads[0],),
    )
    packs = lax.all_gather(pack, "wt", axis=0)

    query_b, query_raw = in_one(
        query_kernel,
        (heads_b, ((2 * STRETCH, 2 * HEAD), F32)),
        (normed_b, w_query, cosine, sine, gain_query[None, :]),
        "query",
        (pieces[0],),
    )

    attn_b, attn_full, lse, kept, sent = attend_forward(meta, query_b, w_attn_out, pieces)

    kept, came = scatter_wt(kept, sent)

    def from_packs(first, last):
        return jnp.concatenate([pick(packs, wt ^ k, 0)[first:last] for k in range(4)], axis=0)

    left_t, right_w = from_packs(0, 16), from_packs(16, 32)
    gate_t, proj_w = from_packs(32, 96), from_packs(96, 160)
    inputs = packs[:, 160:, :1024].reshape(4, 16, 4, 256).transpose(0, 2, 1, 3)
    inputs = lax.dynamic_slice_in_dim(inputs.reshape(4, 64, 256), starts(0), 64, 2)
    inputs = jnp.concatenate([pick(inputs, wt ^ k, 0) for k in range(4)], axis=0).T
    normed_group = gather_group(normed_b, GROUP_X)
    wide_f, wide_b = ((64, D), F32), ((64, D), BF)
    pre_b, resid, attn_sum, laurel_sum, laurel_mid = in_one(
        mid_kernel,
        (wide_b, wide_f, wide_f, wide_f, ((64, 64), F32)),
        (kept, came, stream_own, left_t, right_w, g_in, g_attn, g_laurel, g_pre),
        "mid",
    )

    gate_pre, up_pre, pre_all, act_b, kept, sent = ff_forward(
        gather_wt(pre_b), w_gate, w_up, w_down
    )
    kept, came = scatter_wt(kept, sent)
    pre_group = gather_group(pre_all, GROUP_X)
    act_group = gather_group(act_b, GROUP_Y)

    grad_ff, grad_after, results, gains_join, gates_mine, gates_sent = in_one(
        join_kernel,
        (
            wide_b,
            wide_f,
            ((64, D + 256), BF),
            ((8, D), F32),
            ((2, 128, D), BF),
            ((2, 128, D), BF),
        ),
        (kept, came, resid, grad_top, inputs, gate_t, proj_w, g_post, g_join),
        "join",
        (normed_group,),
    )

    grad_ff_parts = gather_wt(grad_ff)
    wide_cuts, down_cuts = ff_grads(where, grad_ff_parts, gate_pre, up_pre, w_down)
    kept, sent = ff_back(where, wide_cuts, w_gate, w_up)
    wide_cuts = [wide_cuts[0]] + [hop(wide_cuts[k], "ctx", k) for k in (1, 2, 3)]
    down_cuts = [down_cuts[0]] + [hop(down_cuts[k], "ctx", 8 * k) for k in (1, 2, 3)]
    kept, came = scatter_wt(kept, sent)

    grad_attn, branch, own_part, gains_resid, small_mine, small_sent = in_one(
        resid_kernel,
        (wide_b, wide_f, wide_f, ((8, D), F32), ((2, 160, D), BF), ((2, 160, D), BF)),
        (
            kept,
            came,
            resid,
            grad_after,
            attn_sum,
            laurel_sum,
            laurel_mid,
            stream_own,
            left_t,
            right_w,
            g_in,
            g_attn,
            g_laurel,
            g_pre,
            gates_mine,
            gates_sent,
        ),
        "resid",
        (pre_group,),
    )
    grad_attn_parts = gather_wt(grad_attn)

    grad_query_rot, grad_pieces = attend_backward(
        meta, query_b, attn_full, lse, w_attn_out, grad_attn_parts, pieces, *wide_cuts[1:]
    )
    wide = wide_product(where, pre_group, wide_cuts, grad_query_rot)
    def blocks(count, kind):
        return ((count, STRETCH, HEAD), kind)

    def hops(values, masks):
        return [hop(value, "ctx", mask) for value, mask in zip(values, masks)]

    own_far, own_rest, sent_far, sent_rest = grad_pieces
    came_rest = hop(sent_rest, "wt", 1)
    far = in_one(
        far_kernel,
        (blocks(4, BF),) * 4,
        (own_far, hop(sent_far, "wt", 1)),
        "far",
        (came_rest, wide),
    )
    wide = scatter_group(wide, GROUP_Y)
    down = down_product(where, act_group, down_cuts, far[0])
    grad_query_b, gain_query_part = in_one(
        query_back_kernel,
        (heads_b, ((1, HEAD), F32)),
        (grad_query_rot, query_raw, cosine, sine, gain_query[None, :]),
        "query_back",
        (far[0],),
    )
    bases = in_one(
        near_kernel,
        (blocks(8, F32),) * 2 + (blocks(8, BF),) * 4,
        (own_rest, came_rest, *hops(far, (8, 24, 1, 3))),
        "near",
    )
    (small_sent,) = hold((small_sent,), bases[2])
    small = small_mine.astype(F32) + hop(small_sent, "wt", 1).astype(F32)
    small_far = small[1].astype(BF)
    small = (small[0] + hop(small_far, "wt", 2).astype(F32)).astype(BF)
    down_event = down
    down = scatter_group(down, GROUP_Z).reshape(4, 64, -1)
    inner = in_one(
        inner_kernel,
        (blocks(2, F32),) * 2 + (blocks(2, BF),) * 6,
        (*bases[:2], *hops(bases[2:], (8, 24, 1, 3))),
        "inner",
        (grad_query_b, down_event),
    )
    last = in_one(
        last_kernel,
        (((STRETCH, HEAD), F32),) * 2 + (blocks(2, BF),),
        (*inner[:2], *hops(inner[2:], (1, 2, 3, 8, 16, 24))),
        "last",
    )
    across = hop(last[2], "ctx", 4)
    (turn,) = in_one(
        turn_kernel,
        (((D, 768), BF),),
        (small, attn_b, *grad_attn_parts),
        "turn",
        (last[2],),
        scratch=(pltpu.VMEM((2 * STRETCH, D), BF),),
    )
    turn_event = turn
    turn = scatter_group(turn, GROUP_Y)
    home, away, gain_key_part = in_one(
        kind_back_kernel,
        (((2 * STRETCH, half), BF), ((2 * STRETCH, half), BF), ((1, HEAD), F32)),
        (*last[:2], across, kind, cosine, sine, gain_key[None, :]),
        "kind_back",
        (turn_event,),
        spots=spots,
    )

    outs = in_one(
        normed_back_kernel,
        (((STRETCH, D), F32), ((STRETCH, D), BF), ((1, D), F32))
        + (((2 * STRETCH, 192), BF),) * 4,
        (home, hop(away, "wt", 1), grad_query_b, w_query, w_key, w_value, stream),
        "normed_back",
        (wide,),
        spots=spots,
    )
    def fold_z(value):
        value = value.reshape(2, 256, -1)
        return fold(pick(value, at_z, 0), pick(value, 1 - at_z, 0), 4)

    wide = fold_z(wide)
    turn = fold_z(turn)
    kept, sent, gain_input_part, token_cuts = outs[0], outs[1], outs[2], outs[3:]
    kept, came = scatter_wt(kept, sent)
    (stream_grad,) = in_one(
        final_kernel, (wide_b,), (kept, came, own_part, branch, stream_own, g_in), "final", (turn,)
    )

    first, near, core_rows, far_rows = gather_wt(stream_grad)
    stream_grad_all = natural([first, core_rows, near, far_rows]).astype(F32)
    heads = jnp.concatenate(
        [gain_query_part.reshape(32, 8), gain_key_part.reshape(32, 8), jnp.zeros((32, 48), F32)],
        axis=1,
    ).reshape(1, -1)
    line = jnp.arange(8)[:, None]
    late_gains = jnp.where(line == 0, heads, 0.0) + jnp.where(
        line == 1, gain_input_part, 0.0
    )
    late_gains = jnp.concatenate(
        [late_gains + jnp.roll(gains_join, 2, axis=0), gains_resid], axis=0
    )

    late_gains = late_gains + hop(late_gains, "wt", 1)
    late_gains = late_gains + hop(late_gains, "wt", 2)
    token_cuts = [token_cuts[0]] + [hop(token_cuts[k], "ctx", k) for k in (1, 2, 3)]
    (results,) = hold((results,), turn)
    results = lax.all_gather(results, "wt", axis=0)
    layer_out_all = jnp.concatenate([results[i, :, :D] for i in (0, 2, 1, 3)]).astype(F32)
    grad_input_all = jnp.concatenate(
        [
            lax.dynamic_slice_in_dim(results[i], D + 64 * (wt ^ i), 64, 1)
            for i in (0, 2, 1, 3)
        ]
    ).astype(F32)

    (down,) = hold((down,), token_cuts[1])
    down = fold(down[:2], down[2:], 1)
    tokens = fold(*token_product(where, normed_group, late_gains.astype(BF), token_cuts), 8)
    tokens = fold(tokens[0], tokens[1], 24)
    tokens = fold(tokens[0], tokens[1], 4)
    shares = in_one(
        payload_kernel,
        (((64, 2048), BF),) * 4,
        (wide, tokens, turn),
        "payload",
        spots=(where,),
    )
    shares = [shares[0]] + [hop(shares[k], "ctx", k) for k in (1, 2, 3)]
    (
        grad_w_gate,
        grad_w_up,
        grad_w_query,
        grad_w_key,
        grad_w_value,
        grad_w_attn_out,
        grad_left,
        grad_right,
        grad_gate,
        grad_proj,
        gains,
        grad_w_down,
    ) = in_one(
        share_kernel,
        tuple(
            (shape, F32)
            for shape in (
                (64, D),
                (64, D),
                (64, 512),
                (64, half),
                (64, half),
                (64, 512),
                (16, 64),
                (16, 64),
                (64, 64),
                (64, 64),
                (64, 16),
                (64, D),
            )
        ),
        (*shares, down[0], hop(down[1], "ctx", 3)),
        "share",
        spots=(where,),
    )

    return (
        layer_out_all,
        stream_grad_all,
        grad_input_all,
        gains[:, 1] + gains[:, 11],
        gains[:8, 0],
        gains[8:16, 0],
        grad_w_query,
        grad_w_key,
        grad_w_value,
        grad_w_attn_out.T,
        gains[:, 8],
        grad_left.T,
        grad_right,
        gains[:, 9],
        gains[:, 10],
        grad_w_gate,
        grad_w_up,
        grad_w_down.T,
        gains[:, 2],
        grad_gate,
        grad_proj,
        gains[:, 3],
    )


def solution(mesh):
    rows, cols, tops = P("ctx", "wt"), P("wt", "ctx"), P("ctx")
    down, across = P(None, "wt"), P("wt", None)
    return jax.shard_map(
        local,
        mesh=mesh,
        in_specs=(
            P("ctx", None),
            P("ctx", "wt"),
            P("ctx", None),
            P(),
            P(),
            P(),
            P(),
            P(),
            down,
            down,
            down,
            across,
            P(),
            down,
            across,
            P(),
            P(),
            down,
            down,
            across,
            P(),
            down,
            across,
            P(),
        ),
        out_specs=(
            P("ctx", None),
            P("ctx", None),
            rows,
            tops,
            tops,
            tops,
            rows,
            rows,
            rows,
            cols,
            tops,
            rows,
            cols,
            tops,
            tops,
            rows,
            rows,
            cols,
            tops,
            rows,
            cols,
            tops,
        ),
        check_vma=False,
    )
```

```python
import jax
import jax.numpy as jnp
from jax import lax
from jax.experimental import pallas as pl
from jax.experimental.pallas import tpu as pltpu
from jax.sharding import PartitionSpec as P

EPS = 1e-06
ROPE_BASE = 1000000.0
ROOT_HALF = 0.7071067811865476
GELU_A = 0.7978845608028654
GELU_B = 0.044715
STRETCH = 128
HEAD = 256
SLOTS = 64
PAD_SLOTS = 72
CHUNK = 4
D = 2048
VMEM_GRANT = 60 * 1024 * 1024
BF = jnp.bfloat16
F32 = jnp.float32


def hop(value, axis, mask):
    return lax.ppermute(value, axis, [(i, i ^ mask) for i in range(lax.axis_size(axis))])


def pick(value, index, axis):
    return lax.dynamic_index_in_dim(value, index, axis, keepdims=False)


def ctx_of(y, z, x):
    return (y * 2 + z) * 4 + x


GROUP_X = [[ctx_of(y, z, x) for x in range(4)] for y in range(4) for z in range(2)]
GROUP_Y = [[ctx_of(y, z, x) for y in range(4)] for z in range(2) for x in range(4)]
GROUP_Z = [[ctx_of(y, z, x) for z in range(2)] for y in range(4) for x in range(4)]


def gather_group(value, groups):
    return lax.all_gather(value, "ctx", axis=0, axis_index_groups=groups)


def scatter_group(value, groups):
    return lax.psum_scatter(
        value, "ctx", scatter_dimension=0, axis_index_groups=groups, tiled=True
    )


def gate_kernel(*refs):
    pass


def hold(values, event):
    return pl.pallas_call(
        gate_kernel,
        out_shape=tuple(jax.ShapeDtypeStruct(value.shape, value.dtype) for value in values),
        in_specs=[pl.BlockSpec(memory_space=pl.ANY)] * (len(values) + 1),
        out_specs=(pl.BlockSpec(memory_space=pl.ANY),) * len(values),
        input_output_aliases={i: i for i in range(len(values))},
        name="gate",
    )(*values, event)


def ring_gather(block, near, other):
    one = hop(block, "ctx", near)
    two = hop(block, "ctx", other)
    half = block.shape[0] // 2
    return [
        block,
        one,
        two,
        hop(one[:half], "ctx", other),
        hop(two[half:], "ctx", near),
    ]


def gather_wt(own):
    near = hop(own, "wt", 2)
    core = hop(own, "wt", 1)
    far = hop(near, "wt", 1)
    return own, near, core, far


def scatter_wt(kept, sent):
    kept = kept + hop(sent, "wt", 1).astype(F32)
    quarter = kept.shape[0] // 2
    return kept[:quarter], hop(kept[quarter:].astype(BF), "wt", 2)


def fold(kept, sent, mask):
    return (kept.astype(F32) + hop(sent, "ctx", mask).astype(F32)).astype(BF)


def swap_halves(value):
    half = value.shape[0] // 2
    return jnp.concatenate([value[half:], value[:half]], axis=0)


def dot(left, right):
    return jnp.dot(left, right, preferred_element_type=F32)


def dot_rows(left, right):
    return lax.dot_general(left, right, (((0,), (0,)), ((), ())), preferred_element_type=F32)


def dot_cols(left, right):
    return lax.dot_general(left, right, (((1,), (1,)), ((), ())), preferred_element_type=F32)


def halves_of(value):
    high = value.astype(BF)
    return high, (value - high.astype(F32)).astype(BF)


def fine(left, right):
    high, low = halves_of(left)
    return dot(high, right) + dot(low, right)


def fine_cols(left, right):
    high, low = halves_of(left)
    return dot_cols(high, right) + dot_cols(low, right)


def rms(values):
    return lax.rsqrt(jnp.mean(values * values, axis=-1, keepdims=True) + EPS)


def norm_back(grad, normal, scale, gain):
    inner = grad * gain
    back = scale * (inner - normal * jnp.mean(inner * normal, axis=-1, keepdims=True))
    return back, jnp.sum(grad * normal, axis=0, keepdims=grad.ndim == 2)


def rotate(values, cosine, sine):
    half = values.shape[-1] // 2
    front, rear = values[..., :half], values[..., half:]
    return jnp.concatenate([front * cosine - rear * sine, rear * cosine + front * sine], axis=-1)


def gelu_parts(value):
    square = value * value
    bend = jnp.tanh(GELU_A * value * (1.0 + GELU_B * square))
    half = 0.5 * (1.0 + bend)
    slope = half + 0.5 * value * (1.0 - bend * bend) * GELU_A * (1.0 + 3.0 * GELU_B * square)
    return value * half, slope


AT_V = PAD_SLOTS
AT_HI = 2 * PAD_SLOTS
AT_LO = AT_HI + 2
AT_Z = AT_LO + 2
AT_ENDS = AT_Z + 1


def piece_copies(pieces, held, sem):
    copies, at = [], 0
    for i, piece in enumerate(pieces):
        count = piece.shape[0]
        place = held.at[pl.ds(at, count)]
        copies.append(pltpu.make_async_copy(piece, place, sem.at[i]))
        at += count
    return copies


def load_pieces(pieces, held, sem):
    copies = piece_copies(pieces, held, sem)
    for copy in copies:
        copy.start()
    for copy in copies:
        copy.wait()


def query_places(meta, tile, shape, along):
    row = lax.broadcasted_iota(jnp.int32, shape, along) & (STRETCH - 1)
    row = (row + 64 * meta[AT_Z]) & (STRETCH - 1)
    place = meta[AT_HI + tile] * STRETCH + row
    start = jnp.zeros(shape, jnp.int32)
    for j in range(8):
        end = meta[AT_ENDS + j]
        start = jnp.maximum(start, jnp.where(place >= end, end, 0))
    return place, start


def key_places(meta, first, shape, along):
    at = lax.broadcasted_iota(jnp.int32, shape, along)
    row = ((at & (STRETCH - 1)) + 64 * meta[AT_Z]) & (STRETCH - 1)
    return first * STRETCH + (at - (at & (STRETCH - 1))) + row


def tile_of(ref, tile):
    rows = pl.ds(tile * STRETCH, STRETCH)
    return jnp.concatenate([ref[rows, :HEAD], ref[rows, HEAD:]], axis=0)


def stretches(meta, held, at, first):
    return jnp.concatenate([held[meta[at + first + u]] for u in range(CHUNK)], axis=0)


def turns_of(meta, tile):
    return (meta[AT_HI + tile] - meta[AT_LO + tile] + CHUNK) // CHUNK


def forward_kernel(meta, q_ref, w_ref, *refs):
    pieces, (low_ref, full_ref, lse_ref, kept_ref, sent_ref) = refs[:20], refs[20:25]
    held, acc, total, sem = refs[25:]
    load_pieces(pieces, held, sem)
    for tile in range(2):
        query = tile_of(q_ref, tile)
        place, start = query_places(meta, tile, (2 * STRETCH, 1), 0)
        acc[...] = jnp.zeros_like(acc)
        total[...] = jnp.zeros_like(total)

        def turn(i, carry):
            first = meta[AT_LO + tile] + CHUNK * i
            keys = stretches(meta, held, 0, first)
            values = stretches(meta, held, AT_V, first)
            scores = dot_cols(query, keys)
            key_at = key_places(meta, first, (1, CHUNK * STRETCH), 1)
            allowed = (key_at <= place) & (key_at >= start)
            weights = jnp.where(allowed, jnp.exp(scores), 0.0)
            part = weights[:, :STRETCH]
            for u in range(1, CHUNK):
                part = part + weights[:, u * STRETCH : (u + 1) * STRETCH]
            total[...] += part
            acc[...] += dot(weights.astype(BF), values)
            return carry

        lax.fori_loop(0, turns_of(meta, tile), turn, 0)
        row_total = jnp.sum(total[...], axis=1, keepdims=True)
        result = acc[...] / row_total
        rows = pl.ds(tile * STRETCH, STRETCH)
        for head in range(2):
            block = result[head * STRETCH : (head + 1) * STRETCH]
            low_ref[rows, head * HEAD : (head + 1) * HEAD] = block.astype(BF)
            full_ref[rows, head * HEAD : (head + 1) * HEAD] = block
        logs = jnp.broadcast_to(jnp.log(row_total), (2 * STRETCH, STRETCH))
        lse_ref[tile] = jnp.transpose(logs)[:8]
    kept_ref[...] = dot(low_ref[:STRETCH], w_ref[...])
    sent_ref[...] = dot(low_ref[STRETCH:], w_ref[...]).astype(BF)


def backward_kernel(meta, q_ref, full_ref, lse_ref, w_ref, *refs):
    parts, pieces, dq_ref, outs = refs[:4], refs[4:24], refs[-10], refs[-9:-5]
    held, grads, acc, g_ref, sem = refs[-5:]
    copies = piece_copies(pieces, held, sem)
    for copy in copies:
        copy.start()
    for i, part in enumerate(parts):
        g_ref[64 * i : 64 * (i + 1)] = dot_cols(part[...], w_ref[...]).astype(BF)
    grads[...] = jnp.zeros_like(grads)
    for copy in copies:
        copy.wait()
    for tile in range(2):
        query = tile_of(q_ref, tile)
        grad = tile_of(g_ref, tile)
        full = tile_of(full_ref, tile)
        place, start = query_places(meta, tile, (1, 2 * STRETCH), 1)
        lse = lse_ref[tile][:1]
        delta = jnp.sum(grad.astype(F32) * full, axis=1, keepdims=True)
        delta = jnp.transpose(jnp.broadcast_to(delta, (2 * STRETCH, STRETCH)))[:1]
        acc[...] = jnp.zeros_like(acc)

        def turn(i, carry):
            first = meta[AT_LO + tile] + CHUNK * i
            keys = stretches(meta, held, 0, first)
            values = stretches(meta, held, AT_V, first)
            key_at = key_places(meta, first, (CHUNK * STRETCH, 1), 0)
            allowed = (key_at <= place) & (key_at >= start)
            weights = jnp.where(allowed, jnp.exp(dot_cols(keys, query) - lse), 0.0)
            slopes = (weights * (dot_cols(values, grad) - delta)).astype(BF)
            key_term = dot(slopes, query)
            value_term = dot(weights.astype(BF), grad)
            acc[...] += dot_rows(slopes, keys)
            for u in range(CHUNK):
                part = slice(u * STRETCH, (u + 1) * STRETCH)
                for at, term in ((meta[first + u], key_term), (meta[AT_V + first + u], value_term)):
                    grads[at] = (grads[at].astype(F32) + term[part]).astype(BF)
            return carry

        lax.fori_loop(0, turns_of(meta, tile), turn, 0)
        rows = pl.ds(tile * STRETCH, STRETCH)
        for head in range(2):
            block = acc[head * STRETCH : (head + 1) * STRETCH]
            dq_ref[rows, head * HEAD : (head + 1) * HEAD] = block * (HEAD**-0.5)
    copies = []
    for side in range(2):
        for h in range(2):
            at = 64 * side + 32 * h
            for out, first, count, begin in ((0, 24, 8, 8 * h), (1, 0, 24, 24 * h)):
                copies.append(
                    pltpu.make_async_copy(
                        grads.at[pl.ds(at + first, count)],
                        outs[2 * side + out].at[pl.ds(begin, count)],
                        sem.at[len(copies)],
                    )
                )
    for copy in copies:
        copy.start()
    for copy in copies:
        copy.wait()


def in_vmem():
    return pl.BlockSpec(memory_space=pltpu.VMEM)


def anywhere():
    return pl.BlockSpec(memory_space=pl.ANY)


def attend_forward(meta, query, w_attn_out, pieces):
    rows, width = query.shape[0], w_attn_out.shape[1]
    return pl.pallas_call(
        forward_kernel,
        out_shape=(
            jax.ShapeDtypeStruct((rows, 2 * HEAD), BF),
            jax.ShapeDtypeStruct((rows, 2 * HEAD), F32),
            jax.ShapeDtypeStruct((2, 8, 2 * STRETCH), F32),
            jax.ShapeDtypeStruct((STRETCH, width), F32),
            jax.ShapeDtypeStruct((STRETCH, width), BF),
        ),
        in_specs=[pl.BlockSpec(memory_space=pltpu.SMEM), in_vmem(), in_vmem()] + [anywhere()] * 20,
        out_specs=(in_vmem(),) * 5,
        scratch_shapes=[
            pltpu.VMEM((2 * SLOTS, STRETCH, HEAD), BF),
            pltpu.VMEM((2 * STRETCH, HEAD), F32),
            pltpu.VMEM((2 * STRETCH, STRETCH), F32),
            pltpu.SemaphoreType.DMA((20,)),
        ],
        compiler_params=pltpu.CompilerParams(vmem_limit_bytes=VMEM_GRANT),
        cost_estimate=pl.CostEstimate(
            flops=3 * 10**9, bytes_accessed=10**7, transcendentals=2 * 10**6
        ),
        name="attend_forward",
    )(meta, query, w_attn_out, *pieces)


def attend_backward(meta, query, full, lse, w_attn_out, parts, pieces, *events):
    rows = query.shape[0]
    outs = pl.pallas_call(
        backward_kernel,
        out_shape=(jax.ShapeDtypeStruct((rows, 2 * HEAD), F32),)
        + tuple(jax.ShapeDtypeStruct((count, STRETCH, HEAD), BF) for count in (16, 48, 16, 48)),
        in_specs=[pl.BlockSpec(memory_space=pltpu.SMEM)] + [in_vmem()] * 8
        + [anywhere()] * (20 + len(events)),
        out_specs=(in_vmem(),) + (anywhere(),) * 4,
        scratch_shapes=[
            pltpu.VMEM((2 * SLOTS, STRETCH, HEAD), BF),
            pltpu.VMEM((2 * SLOTS, STRETCH, HEAD), BF),
            pltpu.VMEM((2 * STRETCH, HEAD), F32),
            pltpu.VMEM((rows, 2 * HEAD), BF),
            pltpu.SemaphoreType.DMA((20,)),
        ],
        compiler_params=pltpu.CompilerParams(vmem_limit_bytes=VMEM_GRANT),
        cost_estimate=pl.CostEstimate(
            flops=10**10, bytes_accessed=2 * 10**7, transcendentals=2 * 10**6
        ),
        name="attend_backward",
    )(meta, query, full, lse, w_attn_out, *parts, *pieces, *events)
    return outs[0], outs[1:]


UNITS = 512


def ff_forward_kernel(*refs):
    parts, (w_gate, w_up, w_down) = refs[:4], refs[4:7]
    gate_out, up_out, pre_out, act_out, kept, sent = refs[7:13]
    now, acc = refs[13:]
    turn = pl.program_id(0)

    @pl.when(turn == 0)
    def first():
        for i, part in enumerate(parts):
            pre_out[64 * i : 64 * (i + 1)] = part[...]
        acc[...] = jnp.zeros_like(acc)

    gate = dot(pre_out[...], w_gate[...])
    up = dot(pre_out[...], w_up[...])
    gate_out[...] = gate
    up_out[...] = up
    now[...] = (gelu_parts(gate)[0] * up).astype(BF)
    act_out[...] = now[...]
    acc[...] += dot(now[...], w_down[...])

    @pl.when(turn == pl.num_programs(0) - 1)
    def last():
        kept[...] = acc[:STRETCH]
        sent[...] = acc[STRETCH:].astype(BF)


def ff_forward(parts, w_gate, w_up, w_down):
    width, units = w_gate.shape
    rows = 4 * parts[0].shape[0]
    whole = lambda shape: pl.BlockSpec(shape, lambda i: (0, 0))
    tall, flat = pl.BlockSpec((width, UNITS), lambda i: (0, i)), pl.BlockSpec((UNITS, width), lambda i: (i, 0))
    strip = pl.BlockSpec((rows, UNITS), lambda i: (0, i))
    return pl.pallas_call(
        ff_forward_kernel,
        grid=(units // UNITS,),
        out_shape=(
            jax.ShapeDtypeStruct((rows, units), F32),
            jax.ShapeDtypeStruct((rows, units), F32),
            jax.ShapeDtypeStruct((rows, width), BF),
            jax.ShapeDtypeStruct((rows, units), BF),
            jax.ShapeDtypeStruct((rows // 2, width), F32),
            jax.ShapeDtypeStruct((rows // 2, width), BF),
        ),
        in_specs=[whole((rows // 4, width))] * 4 + [tall, tall, flat],
        out_specs=(
            strip,
            strip,
            whole((rows, width)),
            strip,
            whole((rows // 2, width)),
            whole((rows // 2, width)),
        ),
        scratch_shapes=[pltpu.VMEM((rows, UNITS), BF), pltpu.VMEM((rows, width), F32)],
        compiler_params=pltpu.CompilerParams(vmem_limit_bytes=VMEM_GRANT),
        cost_estimate=pl.CostEstimate(
            flops=6 * rows * width * units, bytes_accessed=3 * 10**7, transcendentals=rows * units
        ),
        name="ff_forward",
    )(*parts, w_gate, w_up, w_down)


def ff_grads_kernel(me, *refs):
    parts, (gate_ref, up_ref, w_down) = refs[:4], refs[4:7]
    cuts, quarters, all_in = refs[7:11], refs[11:15], refs[15]
    block = pl.program_id(0)

    @pl.when(block == 0)
    def first():
        for i, part in enumerate(parts):
            all_in[64 * i : 64 * (i + 1)] = part[...]
        for k in range(4):
            at = pl.multiple_of((me[1] ^ k) * 512, 512)
            quarters[k][...] = all_in[:, pl.ds(at, 512)]

    grad_act = dot_cols(all_in[...], w_down[...])
    value, slope = gelu_parts(gate_ref[...])
    for k in range(4):

        @pl.when(block == k)
        def store():
            cuts[k][:, :UNITS] = (grad_act * up_ref[...] * slope).astype(BF)
            cuts[k][:, UNITS:] = (grad_act * value).astype(BF)


def ff_grads(me, parts, gate_pre, up_pre, w_down):
    units, width = w_down.shape
    rows = gate_pre.shape[0]
    whole = lambda shape: pl.BlockSpec(shape, lambda k, me: (0, 0))
    flat = pl.BlockSpec((UNITS, width), lambda k, me: (k ^ me[0], 0))
    strip = pl.BlockSpec((rows, UNITS), lambda k, me: (0, k ^ me[0]))
    outs = pl.pallas_call(
        ff_grads_kernel,
        grid_spec=pltpu.PrefetchScalarGridSpec(
            num_scalar_prefetch=1,
            grid=(4,),
            in_specs=[whole((rows // 4, width))] * 4 + [strip, strip, flat],
            out_specs=(whole((rows, 2 * UNITS)),) * 4 + (whole((rows, width // 4)),) * 4,
            scratch_shapes=[pltpu.VMEM((rows, width), BF)],
        ),
        out_shape=(jax.ShapeDtypeStruct((rows, 2 * UNITS), BF),) * 4
        + (jax.ShapeDtypeStruct((rows, width // 4), BF),) * 4,
        compiler_params=pltpu.CompilerParams(vmem_limit_bytes=VMEM_GRANT),
        cost_estimate=pl.CostEstimate(
            flops=2 * rows * width * units, bytes_accessed=10**7, transcendentals=rows * units
        ),
        name="ff_grads",
    )(me, *parts, gate_pre, up_pre, w_down)
    return outs[:4], outs[4:]


def ff_back_kernel(me, *refs):
    cuts, (w_gate, w_up, kept, sent, acc) = refs[:4], refs[4:]
    block = pl.program_id(0)

    @pl.when(block == 0)
    def first():
        acc[...] = jnp.zeros_like(acc)

    for k in range(4):

        @pl.when(block == k)
        def add():
            term = dot_cols(cuts[k][:, :UNITS], w_gate[...])
            acc[...] += term + dot_cols(cuts[k][:, UNITS:], w_up[...])

    @pl.when(block == 3)
    def last():
        kept[...] = acc[:STRETCH]
        sent[...] = acc[STRETCH:].astype(BF)


def ff_back(me, cuts, w_gate, w_up):
    width, units = w_gate.shape
    rows = cuts[0].shape[0]
    whole = lambda shape: pl.BlockSpec(shape, lambda k, me: (0, 0))
    tall = pl.BlockSpec((width, UNITS), lambda k, me: (0, k ^ me[0]))
    return pl.pallas_call(
        ff_back_kernel,
        grid_spec=pltpu.PrefetchScalarGridSpec(
            num_scalar_prefetch=1,
            grid=(4,),
            in_specs=[whole((rows, 2 * UNITS))] * 4 + [tall, tall],
            out_specs=(whole((rows // 2, width)),) * 2,
            scratch_shapes=[pltpu.VMEM((rows, width), F32)],
        ),
        out_shape=(
            jax.ShapeDtypeStruct((rows // 2, width), F32),
            jax.ShapeDtypeStruct((rows // 2, width), BF),
        ),
        compiler_params=pltpu.CompilerParams(vmem_limit_bytes=VMEM_GRANT),
        cost_estimate=pl.CostEstimate(
            flops=4 * rows * width * units, bytes_accessed=2 * 10**7, transcendentals=0
        ),
        name="ff_back",
    )(me, *cuts, w_gate, w_up)


def relative_rows(spots, stream):
    return jnp.concatenate(
        [stream[pl.ds(pl.multiple_of(spots[i], 64), 64)] for i in range(4)], axis=0
    )


def swapped(value):
    return jnp.concatenate([value[STRETCH:], value[:STRETCH]], axis=0)


def input_kernel(spots, stream, w_key, w_value, g_in, normed_out, mine, theirs):
    rows = relative_rows(spots, stream).astype(F32)
    normed_out[...] = (rows * rms(rows) * g_in[...]).astype(BF)
    key, value = dot(normed_out[...], w_key[...]), dot(normed_out[...], w_value[...])
    first = spots[4] == 0
    mine[...] = jnp.where(first, key, value)
    theirs[...] = swapped(jnp.where(first, value, key))


def kind_kernel(spots, mine, came, cosine, sine, gain, low_out, full_out):
    first = spots[4] == 0
    kind = jnp.concatenate(
        [jnp.where(first, mine[...], came[...]), jnp.where(first, came[...], mine[...])], axis=1
    )
    full_out[...] = kind
    turn = (jnp.where(first, cosine[...], 1.0), jnp.where(first, sine[...], 0.0))
    scaled = kind * rms(kind) * jnp.where(first, gain[...], 1.0)
    low_out[...] = rotate(scaled, *turn).astype(BF)


def lay_kernel(*refs):
    for h in range(2):
        for i in range(4):
            refs[8 + h][256 * i : 256 * (i + 1)] = refs[4 * h + i][...]


def kind_back_kernel(spots, sums_a, sums_b, came, kind_ref, cosine, sine, gain, event, home, away, gains):
    first = spots[4] == 0
    turn = (jnp.where(first, cosine[...], 1.0), jnp.where(first, -sine[...], 0.0))
    grad = jnp.concatenate([sums_a[...] + came[0].astype(F32), sums_b[...] + came[1].astype(F32)], axis=0)
    kind = kind_ref[...]
    scale = rms(kind)
    grad, gain_part = norm_back(
        rotate(grad, *turn), kind * scale, scale, jnp.where(first, gain[...], 1.0)
    )
    gains[...] = jnp.where(first, gain_part, 0.0)
    half = HEAD // 2
    home[...] = jnp.where(first, grad[:, :half], grad[:, half:]).astype(BF)
    away[...] = swapped(jnp.where(first, grad[:, half:], grad[:, :half])).astype(BF)


def query_kernel(normed, w_query, cosine, sine, gain, event, low_out, raw_out):
    for head in range(2):
        at = slice(head * HEAD, (head + 1) * HEAD)
        raw = dot(normed[...], w_query[:, at])
        raw_out[:, at] = raw
        turned = rotate(raw * rms(raw) * gain[...], cosine[...], sine[...]).astype(BF)
        low_out[:, at] = (turned.astype(F32) * HEAD**-0.5).astype(BF)


def query_back_kernel(grad_ref, raw_ref, cosine, sine, gain, event, low_out, gains):
    gains[...] = jnp.zeros_like(gains)
    for head in range(2):
        at = slice(head * HEAD, (head + 1) * HEAD)
        raw = raw_ref[:, at]
        scale = rms(raw)
        grad, part = norm_back(
            rotate(grad_ref[:, at], cosine[...], -sine[...]), raw * scale, scale, gain[...]
        )
        low_out[:, at] = grad.astype(BF)
        gains[...] += part


def normed_back_kernel(spots, home, came, query, w_query, w_key, w_value, stream, *outs):
    kept, sent, gain_out, cuts = outs[-7], outs[-6], outs[-5], outs[-4:]
    first = spots[4] == 0
    key = jnp.where(first, home[...].astype(F32), came[...].astype(F32)).astype(BF)
    value = jnp.where(first, came[...].astype(F32), home[...].astype(F32)).astype(BF)
    part = dot_cols(query[...], w_query[...])
    part = part + dot_cols(key, w_key[...]) + dot_cols(value, w_value[...])
    kept[...] = part[:STRETCH]
    sent[...] = part[STRETCH:].astype(BF)
    rows = relative_rows(spots, stream).astype(F32)
    gain_out[...] = jnp.sum(part * (rows * rms(rows)), axis=0, keepdims=True)
    for k, cut in enumerate(cuts):
        at = spots[5] ^ k
        cut[:, :128] = query[:, pl.ds(pl.multiple_of(at * 128, 128), 128)]
        side = jnp.where(at >= 2, value.astype(F32), key.astype(F32))
        side = jnp.where((at & 1) == 1, side[:, 64:], side[:, :64])
        cut[:, 128:] = side.astype(BF)


def far_kernel(own, came, *refs):
    for i, out in enumerate(refs[-4:]):
        at = slice(4 * i, 4 * i + 4)
        out[...] = (own[at].astype(F32) + came[at].astype(F32)).astype(BF)


def near_kernel(own, came, *refs):
    passed, (base_a, base_b), sends = refs[:4], refs[-6:-4], refs[-4:]

    def summed(first, count):
        at = slice(first, first + count)
        return own[at].astype(F32) + came[at].astype(F32)

    for h, base in enumerate((base_a, base_b)):
        near, other = sends[2 * h], sends[2 * h + 1]
        base[...] = summed(24 * h, 8)
        near[:4] = summed(24 * h + 8, 4).astype(BF)
        near[4:] = (summed(24 * h + 12, 4) + passed[2 * h + 1][...].astype(F32)).astype(BF)
        other[:4] = (summed(24 * h + 16, 4) + passed[2 * h][...].astype(F32)).astype(BF)
        other[4:] = summed(24 * h + 20, 4).astype(BF)


def inner_kernel(base_a, base_b, *refs):
    came, kept, sends = refs[:4], refs[-8:-6], refs[-6:]
    for h, base in enumerate((base_a, base_b)):
        total = base[...] + came[2 * h][...].astype(F32) + came[2 * h + 1][...].astype(F32)
        kept[h][...] = total[:2]
        for k in (1, 2, 3):
            sends[3 * h + k - 1][...] = total[2 * k : 2 * k + 2].astype(BF)


def last_kernel(kept_a, kept_b, *refs):
    came, kept, send = refs[:6], refs[6:8], refs[8]
    for h, base in enumerate((kept_a, kept_b)):
        total = base[...]
        for k in range(3):
            total = total + came[3 * h + k][...].astype(F32)
        kept[h][...] = total[0]
        send[h] = total[1].astype(BF)


def mid_kernel(kept, came, stream, left, right, g_in, g_attn, g_laurel, g_pre, *outs):
    pre_out, resid_out, attn_out, laurel_out, low_out = outs
    rows = stream[...].astype(F32)
    normed = rows * rms(rows) * g_in[...]
    attn = kept[...] + came[...].astype(F32)
    low = dot_cols(normed.astype(BF), left[...])
    laurel = fine(low, right[...])
    resid = (
        rows + attn * rms(attn) * g_attn[...] + normed + laurel * rms(laurel) * g_laurel[...]
    ) * ROOT_HALF
    pre_out[...] = (resid * rms(resid) * g_pre[...]).astype(BF)
    resid_out[...] = resid
    attn_out[...] = attn
    laurel_out[...] = laurel
    low_out[...] = low


def join_kernel(kept, came, resid, top, inputs, gate_t, proj, g_post, g_join, event, *outs):
    ff_out, after_out, results, gains, mine, theirs = outs
    ff = kept[...] + came[...].astype(F32)
    ff_scale = rms(ff)
    ff_normal = ff * ff_scale
    after = resid[...] + ff_normal * g_post[...]
    value, slope = gelu_parts(fine_cols(after, gate_t[...]))
    channels = inputs[...].astype(F32)
    joined = value * channels
    join = fine(joined, proj[...])
    join_scale = rms(join)
    join_normal = join * join_scale
    results[:, :D] = (after + join_normal * g_join[...]).astype(BF)
    grad = top[...].astype(F32)
    grad_join, gain_join = norm_back(grad, join_normal, join_scale, g_join[...])
    grad_joined = fine_cols(grad_join, proj[...])
    grad_pre = grad_joined * channels * slope
    results[:, D:] = (grad_joined * value).astype(BF)
    grad_after = grad + fine(grad_pre, gate_t[...])
    after_out[...] = grad_after
    grad_ff, gain_post = norm_back(grad_after, ff_normal, ff_scale, g_post[...])
    ff_out[...] = grad_ff.astype(BF)
    gains[...] = jnp.zeros_like(gains)
    gains[0:1] = gain_post
    gains[1:2] = gain_join
    low_gate = dot_rows(grad_pre.astype(BF), after.astype(BF)).astype(BF)
    low_proj = dot_rows(joined.astype(BF), grad_join.astype(BF)).astype(BF)
    for k, (out, i) in enumerate(((mine, 0), (theirs, 0), (mine, 1), (theirs, 1))):
        out[i, :64] = low_gate[64 * k : 64 * (k + 1)]
        out[i, 64:] = low_proj[64 * k : 64 * (k + 1)]


def resid_kernel(
    kept,
    came,
    resid,
    after,
    attn,
    laurel,
    low,
    stream,
    left,
    right,
    g_in,
    g_attn,
    g_laurel,
    g_pre,
    gates_mine,
    gates_sent,
    *refs,
):
    attn_out, branch_out, own_out, gains, mine, theirs = refs[-6:]
    mine[:, 32:] = gates_mine[...]
    theirs[:, 32:] = gates_sent[...]
    scale = rms(resid[...])
    grad = kept[...] + came[...].astype(F32)
    grad_resid, gain_pre = norm_back(grad, resid[...] * scale, scale, g_pre[...])
    branch = (after[...] + grad_resid) * ROOT_HALF
    branch_out[...] = branch
    scale = rms(attn[...])
    grad_attn, gain_attn = norm_back(branch, attn[...] * scale, scale, g_attn[...])
    attn_out[...] = grad_attn.astype(BF)
    scale = rms(laurel[...])
    grad_laurel, gain_laurel = norm_back(branch, laurel[...] * scale, scale, g_laurel[...])
    grad_low = fine_cols(grad_laurel, right[...])
    own = branch + fine(grad_low, left[...])
    own_out[...] = own
    rows = stream[...].astype(F32)
    normal = rows * rms(rows)
    gains[...] = jnp.zeros_like(gains)
    gains[0:1] = gain_attn
    gains[1:2] = gain_laurel
    gains[2:3] = gain_pre
    gains[3:4] = jnp.sum(own * normal, axis=0, keepdims=True)
    low_left = dot_rows(grad_low.astype(BF), (normal * g_in[...]).astype(BF)).astype(BF)
    low_right = dot_rows(low[...].astype(BF), grad_laurel.astype(BF)).astype(BF)
    for k, (out, i) in enumerate(((mine, 0), (theirs, 0), (mine, 1), (theirs, 1))):
        out[i, :16] = low_left[16 * k : 16 * (k + 1)]
        out[i, 16:32] = low_right[16 * k : 16 * (k + 1)]


def final_kernel(kept, came, own, branch, stream, g_in, event, out):
    rows = stream[...].astype(F32)
    scale = rms(rows)
    grad = own[...] + kept[...] + came[...].astype(F32)
    extra, _ = norm_back(grad, rows * scale, scale, g_in[...])
    out[...] = (branch[...] + extra).astype(BF)


def in_one(kernel, shapes, args, name, event=(), spots=(), scratch=()):
    return pl.pallas_call(
        kernel,
        out_shape=tuple(jax.ShapeDtypeStruct(shape, kind) for shape, kind in shapes),
        in_specs=[pl.BlockSpec(memory_space=pltpu.SMEM)] * len(spots)
        + [in_vmem()] * len(args)
        + [anywhere()] * len(event),
        out_specs=(in_vmem(),) * len(shapes),
        scratch_shapes=list(scratch),
        compiler_params=pltpu.CompilerParams(vmem_limit_bytes=VMEM_GRANT),
        cost_estimate=pl.CostEstimate(flops=10**9, bytes_accessed=5 * 10**6, transcendentals=10**5),
        name=name,
    )(*spots, *args, *event)


def pack_kernel(left, right, gate_w, proj, inputs, event, out):
    unit = (
        lax.broadcasted_iota(jnp.int32, (64, 64), 0) == lax.broadcasted_iota(jnp.int32, (64, 64), 1)
    ).astype(BF)
    out[:16] = dot_cols(unit[:16, :16], left[...]).astype(BF)
    out[16:32] = right[...]
    out[32:96] = dot_cols(unit, gate_w[...]).astype(BF)
    out[96:160] = proj[...]
    turned = dot_cols(unit, inputs[...]).astype(BF)
    out[160:] = jnp.zeros_like(out[160:])
    for i in range(4):
        out[160:, 256 * i : 256 * (i + 1)] = turned[16 * i : 16 * (i + 1)]


Y_FIRST = (0, 3, 1, 2)
Y_OTHER = (0, 1, 3, 2)


def group_sum(me, group, cuts, at, size):
    total = None
    for k, cut in enumerate(cuts):
        term = dot_rows(group[me ^ k, :, pl.ds(at, size)], cut)
        total = term if total is None else total + term
    return total


def wide_kernel(where, group, *refs):
    cuts, out = refs[:4], refs[-1]
    for at in range(0, D, 256):
        total = group_sum(where[0], group, [cut[...] for cut in cuts], at, 256)
        out[at : at + 256] = total.astype(BF)


def wide_product(where, group, cuts, event):
    return pl.pallas_call(
        wide_kernel,
        out_shape=jax.ShapeDtypeStruct((D, cuts[0].shape[1]), BF),
        in_specs=[pl.BlockSpec(memory_space=pltpu.SMEM)] + [in_vmem()] * 5 + [anywhere()],
        out_specs=in_vmem(),
        compiler_params=pltpu.CompilerParams(vmem_limit_bytes=VMEM_GRANT),
        cost_estimate=pl.CostEstimate(flops=5 * 10**9, bytes_accessed=10**7, transcendentals=0),
        name="wide_product",
    )(where, group, *cuts, event)


def turn_kernel(small, attn, *refs):
    parts, out, grads = refs[:4], refs[-2], refs[-1]
    low = small.shape[0]
    for i, part in enumerate(parts):
        grads[64 * i : 64 * (i + 1)] = part[...]
    unit = (
        lax.broadcasted_iota(jnp.int32, (low, 256), 0)
        == lax.broadcasted_iota(jnp.int32, (low, 256), 1)
    ).astype(BF)
    out[:, :512] = dot_rows(grads[...], attn[...]).astype(BF)
    out[:, 512:] = dot_rows(small[...], unit).astype(BF)


def token_kernel(where, group, gains, *refs):
    cuts, (kept, sent) = refs[:4], refs[4:]
    x, y, z = where[0], where[1], where[2]
    unit = (
        lax.broadcasted_iota(jnp.int32, (16, 64), 0) == lax.broadcasted_iota(jnp.int32, (16, 64), 1)
    ).astype(BF)
    for i, far_y in enumerate(Y_FIRST):
        for far_z in range(2):
            at = pl.multiple_of(((y ^ far_y) * 2 + (z ^ far_z)) * 256, 256)
            total = group_sum(x, group, [cut[...] for cut in cuts], at, 256)
            more = dot_rows(gains[:, pl.ds(at, 256)], unit)
            total = jnp.concatenate([total, more], axis=1).astype(BF)
            (kept, sent)[i // 2][i % 2, far_z] = total


def token_product(where, group, gains, cuts):
    shape = (2, 2, 256, cuts[0].shape[1] + 64)
    return pl.pallas_call(
        token_kernel,
        out_shape=(jax.ShapeDtypeStruct(shape, BF),) * 2,
        in_specs=[pl.BlockSpec(memory_space=pltpu.SMEM)] + [in_vmem()] * 6,
        out_specs=(in_vmem(),) * 2,
        compiler_params=pltpu.CompilerParams(vmem_limit_bytes=VMEM_GRANT),
        cost_estimate=pl.CostEstimate(flops=10**9, bytes_accessed=6 * 10**6, transcendentals=0),
        name="token_product",
    )(where, group, gains, *cuts)


def payload_kernel(where, wide, tokens, turn, *outs):
    for k, out in enumerate(outs):
        at = pl.ds(pl.multiple_of((where[0] ^ k) * 64, 64), 64)
        out[:, :1024] = wide[at]
        out[:, 1024:1280] = tokens[at]
        out[:, 1280:] = turn[at]


def share_kernel(where, *refs):
    shares, down_kept, down_came = refs[:4], refs[4], refs[5]
    gate, up, query, key, value, attn, left, right, join_g, join_p, gains, down = refs[6:]
    x = where[0]

    def turned(rows):
        rows = jnp.concatenate([rows, jnp.zeros_like(rows)], axis=0)
        return jnp.transpose(rows)[:, :64]

    for k, share in enumerate(shares):
        gate[:, pl.ds(pl.multiple_of((x ^ k) * 512, 512), 512)] = share[:, :512].astype(F32)
        up[:, pl.ds(pl.multiple_of((x ^ k) * 512, 512), 512)] = share[:, 512:1024].astype(F32)
        query[:, pl.ds(pl.multiple_of((x ^ k) * 128, 128), 128)] = share[:, 1024:1152].astype(F32)
    quarters = [share[:, 1152:1216].astype(F32) for share in shares]
    placed = []
    for q in range(4):
        choice = quarters[3]
        for k in range(3):
            choice = jnp.where((x ^ k) == q, quarters[k], choice)
        placed.append(choice)
    key[:, :64], key[:, 64:] = placed[0], placed[1]
    value[:, :64], value[:, 64:] = placed[2], placed[3]
    total = shares[0][:, 1216:].astype(F32)
    for share in shares[1:]:
        total = total + share[:, 1216:].astype(F32)
    gains[...] = total[:, :16]
    attn[...] = total[:, 64:576]
    small = total[:, 576:736]
    join_g[...] = small[:, 32:96]
    lines = turned(jnp.concatenate([small, jnp.zeros((64, 96), F32)], axis=1))
    left[...] = lines[:16]
    right[...] = lines[16:32]
    join_p[...] = lines[96:160]
    down[...] = down_kept[...].astype(F32) + down_came[...].astype(F32)


def down_kernel(where, group, *refs):
    cuts, out, total = refs[:4], refs[5], refs[6]
    x, y = where[0], where[1]
    units = group.shape[2]
    for first in range(0, units, 512):
        value = None
        for k, cut in enumerate(cuts):
            term = dot_rows(cut[...], group[y ^ k, :, first : first + 512])
            value = term if value is None else value + term
        total[...] = value
        for i, far_x in enumerate(Y_FIRST):
            for z in range(2):
                at = pl.multiple_of((z * 4 + (x ^ far_x)) * 64, 64)
                out[z, i, :, first : first + 512] = total[pl.ds(at, 64)].astype(BF)


def down_product(where, group, cuts, event):
    return pl.pallas_call(
        down_kernel,
        out_shape=jax.ShapeDtypeStruct((2, 4, 64, group.shape[2]), BF),
        in_specs=[pl.BlockSpec(memory_space=pltpu.SMEM)] + [in_vmem()] * 5 + [anywhere()],
        out_specs=in_vmem(),
        scratch_shapes=[pltpu.VMEM((512, 512), F32)],
        compiler_params=pltpu.CompilerParams(vmem_limit_bytes=VMEM_GRANT),
        cost_estimate=pl.CostEstimate(flops=3 * 10**9, bytes_accessed=10**7, transcendentals=0),
        name="down_product",
    )(where, group, *cuts, event)


def local(
    stream,
    layer_input,
    out_grad,
    doc_lengths,
    stretch_slots,
    gain_input,
    gain_query,
    gain_key,
    w_query,
    w_key,
    w_value,
    w_attn_out,
    gain_attn,
    laurel_left,
    laurel_right,
    gain_laurel,
    gain_pre_ff,
    w_gate,
    w_up,
    w_down,
    gain_post_ff,
    join_gate,
    join_proj,
    gain_join,
):
    wt = lax.axis_index("wt")
    core, zlo = wt & 1, wt >> 1
    ctx = lax.axis_index("ctx")
    at_x, at_z, at_y = ctx & 3, (ctx >> 2) & 1, ctx >> 3
    first_core = core == 0
    half = HEAD // 2

    def starts(k):
        return ((core ^ (k & 1)) * 2 + (zlo ^ (k >> 1))) * 64

    def natural(blocks):
        stacked = jnp.stack(blocks)
        return jnp.concatenate(
            [pick(stacked, wt ^ ((b & 1) * 2 + (b >> 1)), 0) for b in range(4)], axis=0
        )

    stream_own = lax.dynamic_slice_in_dim(stream, starts(0), 64, 0)
    grad_top = lax.dynamic_slice_in_dim(out_grad, starts(0), 64, 0)
    where = jnp.stack([at_x, at_y, at_z])
    spots = (jnp.stack([starts(0), starts(2), starts(1), starts(3), core, at_x]),)
    g_in, g_attn, g_laurel, g_pre, g_post, g_join = (
        gain[None, :]
        for gain in (gain_input, gain_attn, gain_laurel, gain_pre_ff, gain_post_ff, gain_join)
    )

    doc_ends = jnp.cumsum(doc_lengths)
    tiles = [lax.dynamic_index_in_dim(stretch_slots, 2 * ctx + (core ^ t), 0) for t in range(2)]
    hi = jnp.concatenate(tiles)
    lo = jnp.max(
        jnp.where(doc_ends[None, :] <= hi[:, None] * STRETCH, doc_ends[None, :], 0), axis=1
    )
    lo = lo // STRETCH
    row = (jnp.arange(STRETCH, dtype=jnp.int32) + 64 * zlo) & (STRETCH - 1)
    positions = (hi[:, None] * STRETCH + row[None, :]).reshape(-1)
    names = jnp.arange(SLOTS, dtype=jnp.int32)
    slot_of = jnp.sum(jnp.where(stretch_slots[None, :] == names[:, None], names[None, :], 0), axis=1)
    relative = (slot_of >> 1) ^ ctx
    rel_x, rel_z, rel_y = relative & 3, (relative >> 2) & 1, relative >> 3
    places = (
        (rel_y ^ (rel_y >> 1)) * 8 + rel_x * 2 + rel_z,
        SLOTS // 2 + (rel_x ^ (rel_x >> 1)) * 8 + rel_y * 2 + rel_z,
    )
    second = (slot_of & 1) == 1
    key_at = core * SLOTS + jnp.where(second, places[1], places[0])
    value_at = (1 - core) * SLOTS + jnp.where(second, places[0], places[1])
    blank = jnp.zeros((PAD_SLOTS - SLOTS,), jnp.int32)
    meta = jnp.concatenate([key_at, blank, value_at, blank, hi, lo, zlo[None], doc_ends]).astype(
        jnp.int32
    )
    exponents = jnp.arange(half, dtype=F32) * (2.0 / HEAD)
    angles = positions.astype(F32)[:, None] * (1.0 / ROPE_BASE**exponents)[None, :]
    cosine, sine = jnp.cos(angles), jnp.sin(angles)

    half_rows, heads_b = ((2 * STRETCH, half), F32), ((2 * STRETCH, 2 * HEAD), BF)
    normed_b, mine, theirs = in_one(
        input_kernel,
        (((2 * STRETCH, D), BF), half_rows, half_rows),
        (stream, w_key, w_value, g_in),
        "input",
        spots=spots,
    )
    kind_b, kind = in_one(
        kind_kernel,
        (((2 * STRETCH, HEAD), BF), ((2 * STRETCH, HEAD), F32)),
        (mine, hop(theirs, "wt", 1), cosine, sine, gain_key[None, :]),
        "kind",
        spots=spots,
    )

    across = hop(kind_b, "ctx", 4)
    groups = []
    for h, one in enumerate((1, 8)):
        rows = slice(h * STRETCH, (h + 1) * STRETCH)
        block = jnp.concatenate([kind_b[rows], across[rows]], axis=0)
        groups.append([block] + [hop(block, "ctx", k * one) for k in (1, 2, 3)])
    quads = in_one(lay_kernel, (((1024, HEAD), BF),) * 2, (*groups[0], *groups[1]), "lay")
    pieces = ring_gather(quads[0], 8, 24) + ring_gather(quads[1], 1, 3)
    pieces += [hop(piece, "wt", 1) for piece in pieces]
    pieces = [piece.reshape(-1, STRETCH, HEAD) for piece in pieces]

    (pack,) = in_one(
        pack_kernel,
        (((176, D), BF),),
        (laurel_left, laurel_right, join_gate, join_proj, layer_input),
        "pack",
        (quads[0],),
    )
    packs = lax.all_gather(pack, "wt", axis=0)

    query_b, query_raw = in_one(
        query_kernel,
        (heads_b, ((2 * STRETCH, 2 * HEAD), F32)),
        (normed_b, w_query, cosine, sine, gain_query[None, :]),
        "query",
        (pieces[0],),
    )

    attn_b, attn_full, lse, kept, sent = attend_forward(meta, query_b, w_attn_out, pieces)

    kept, came = scatter_wt(kept, sent)

    def from_packs(first, last):
        return jnp.concatenate([pick(packs, wt ^ k, 0)[first:last] for k in range(4)], axis=0)

    left_t, right_w = from_packs(0, 16), from_packs(16, 32)
    gate_t, proj_w = from_packs(32, 96), from_packs(96, 160)
    inputs = packs[:, 160:, :1024].reshape(4, 16, 4, 256).transpose(0, 2, 1, 3)
    inputs = lax.dynamic_slice_in_dim(inputs.reshape(4, 64, 256), starts(0), 64, 2)
    inputs = jnp.concatenate([pick(inputs, wt ^ k, 0) for k in range(4)], axis=0).T
    normed_group = gather_group(normed_b, GROUP_X)
    wide_f, wide_b = ((64, D), F32), ((64, D), BF)
    pre_b, resid, attn_sum, laurel_sum, laurel_mid = in_one(
        mid_kernel,
        (wide_b, wide_f, wide_f, wide_f, ((64, 64), F32)),
        (kept, came, stream_own, left_t, right_w, g_in, g_attn, g_laurel, g_pre),
        "mid",
    )

    gate_pre, up_pre, pre_all, act_b, kept, sent = ff_forward(
        gather_wt(pre_b), w_gate, w_up, w_down
    )
    kept, came = scatter_wt(kept, sent)
    pre_group = gather_group(pre_all, GROUP_X)
    act_group = gather_group(act_b, GROUP_Y)

    grad_ff, grad_after, results, gains_join, gates_mine, gates_sent = in_one(
        join_kernel,
        (
            wide_b,
            wide_f,
            ((64, D + 256), BF),
            ((8, D), F32),
            ((2, 128, D), BF),
            ((2, 128, D), BF),
        ),
        (kept, came, resid, grad_top, inputs, gate_t, proj_w, g_post, g_join),
        "join",
        (normed_group,),
    )

    grad_ff_parts = gather_wt(grad_ff)
    wide_cuts, down_cuts = ff_grads(where, grad_ff_parts, gate_pre, up_pre, w_down)
    kept, sent = ff_back(where, wide_cuts, w_gate, w_up)
    wide_cuts = [wide_cuts[0]] + [hop(wide_cuts[k], "ctx", k) for k in (1, 2, 3)]
    kept, came = scatter_wt(kept, sent)

    grad_attn, branch, own_part, gains_resid, small_mine, small_sent = in_one(
        resid_kernel,
        (wide_b, wide_f, wide_f, ((8, D), F32), ((2, 160, D), BF), ((2, 160, D), BF)),
        (
            kept,
            came,
            resid,
            grad_after,
            attn_sum,
            laurel_sum,
            laurel_mid,
            stream_own,
            left_t,
            right_w,
            g_in,
            g_attn,
            g_laurel,
            g_pre,
            gates_mine,
            gates_sent,
        ),
        "resid",
        (pre_group,),
    )
    grad_attn_parts = gather_wt(grad_attn)

    grad_query_rot, grad_pieces = attend_backward(
        meta, query_b, attn_full, lse, w_attn_out, grad_attn_parts, pieces, *wide_cuts[1:]
    )
    wide = wide_product(where, pre_group, wide_cuts, grad_query_rot)
    def blocks(count, kind):
        return ((count, STRETCH, HEAD), kind)

    def hops(values, masks):
        return [hop(value, "ctx", mask) for value, mask in zip(values, masks)]

    own_far, own_rest, sent_far, sent_rest = grad_pieces
    came_rest = hop(sent_rest, "wt", 1)
    far = in_one(
        far_kernel,
        (blocks(4, BF),) * 4,
        (own_far, hop(sent_far, "wt", 1)),
        "far",
        (came_rest, wide),
    )
    wide = scatter_group(wide, GROUP_Y)
    grad_query_b, gain_query_part = in_one(
        query_back_kernel,
        (heads_b, ((1, HEAD), F32)),
        (grad_query_rot, query_raw, cosine, sine, gain_query[None, :]),
        "query_back",
        (far[0],),
    )
    bases = in_one(
        near_kernel,
        (blocks(8, F32),) * 2 + (blocks(8, BF),) * 4,
        (own_rest, came_rest, *hops(far, (8, 24, 1, 3))),
        "near",
    )
    (small_sent,) = hold((small_sent,), bases[2])
    small = small_mine.astype(F32) + hop(small_sent, "wt", 1).astype(F32)
    small_far = small[1].astype(BF)
    small = (small[0] + hop(small_far, "wt", 2).astype(F32)).astype(BF)
    inner = in_one(
        inner_kernel,
        (blocks(2, F32),) * 2 + (blocks(2, BF),) * 6,
        (*bases[:2], *hops(bases[2:], (8, 24, 1, 3))),
        "inner",
        (grad_query_b,),
    )
    last = in_one(
        last_kernel,
        (((STRETCH, HEAD), F32),) * 2 + (blocks(2, BF),),
        (*inner[:2], *hops(inner[2:], (1, 2, 3, 8, 16, 24))),
        "last",
    )
    across = hop(last[2], "ctx", 4)
    down_cuts = [down_cuts[0]] + [
        hop(value, "ctx", 8 * k) for k, value in zip((1, 2, 3), hold(down_cuts[1:], last[2]))
    ]
    down = down_product(where, act_group, down_cuts, last[2])
    down_event = down
    down = scatter_group(down, GROUP_Z).reshape(4, 64, -1)
    (turn,) = in_one(
        turn_kernel,
        (((D, 768), BF),),
        (small, attn_b, *grad_attn_parts),
        "turn",
        (last[2],),
        scratch=(pltpu.VMEM((2 * STRETCH, D), BF),),
    )
    turn_event = turn
    turn = scatter_group(turn, GROUP_Y)
    home, away, gain_key_part = in_one(
        kind_back_kernel,
        (((2 * STRETCH, half), BF), ((2 * STRETCH, half), BF), ((1, HEAD), F32)),
        (*last[:2], across, kind, cosine, sine, gain_key[None, :]),
        "kind_back",
        (turn_event,),
        spots=spots,
    )

    outs = in_one(
        normed_back_kernel,
        (((STRETCH, D), F32), ((STRETCH, D), BF), ((1, D), F32))
        + (((2 * STRETCH, 192), BF),) * 4,
        (home, hop(away, "wt", 1), grad_query_b, w_query, w_key, w_value, stream),
        "normed_back",
        (wide, down_event),
        spots=spots,
    )
    def fold_z(value):
        value = value.reshape(2, 256, -1)
        return fold(pick(value, at_z, 0), pick(value, 1 - at_z, 0), 4)

    wide = fold_z(wide)
    turn = fold_z(turn)
    kept, sent, gain_input_part, token_cuts = outs[0], outs[1], outs[2], outs[3:]
    kept, came = scatter_wt(kept, sent)
    (stream_grad,) = in_one(
        final_kernel, (wide_b,), (kept, came, own_part, branch, stream_own, g_in), "final", (turn,)
    )

    first, near, core_rows, far_rows = gather_wt(stream_grad)
    stream_grad_all = natural([first, core_rows, near, far_rows]).astype(F32)
    heads = jnp.concatenate(
        [gain_query_part.reshape(32, 8), gain_key_part.reshape(32, 8), jnp.zeros((32, 48), F32)],
        axis=1,
    ).reshape(1, -1)
    line = jnp.arange(8)[:, None]
    late_gains = jnp.where(line == 0, heads, 0.0) + jnp.where(
        line == 1, gain_input_part, 0.0
    )
    late_gains = jnp.concatenate(
        [late_gains + jnp.roll(gains_join, 2, axis=0), gains_resid], axis=0
    )

    late_gains = late_gains + hop(late_gains, "wt", 1)
    late_gains = late_gains + hop(late_gains, "wt", 2)
    token_cuts = [token_cuts[0]] + [hop(token_cuts[k], "ctx", k) for k in (1, 2, 3)]
    (results,) = hold((results,), turn)
    results = lax.all_gather(results, "wt", axis=0)
    layer_out_all = jnp.concatenate([results[i, :, :D] for i in (0, 2, 1, 3)]).astype(F32)
    grad_input_all = jnp.concatenate(
        [
            lax.dynamic_slice_in_dim(results[i], D + 64 * (wt ^ i), 64, 1)
            for i in (0, 2, 1, 3)
        ]
    ).astype(F32)

    (down,) = hold((down,), token_cuts[1])
    down = fold(down[:2], down[2:], 1)
    tokens = fold(*token_product(where, normed_group, late_gains.astype(BF), token_cuts), 8)
    tokens = fold(tokens[0], tokens[1], 24)
    tokens = fold(tokens[0], tokens[1], 4)
    shares = in_one(
        payload_kernel,
        (((64, 2048), BF),) * 4,
        (wide, tokens, turn),
        "payload",
        spots=(where,),
    )
    shares = [shares[0]] + [hop(shares[k], "ctx", k) for k in (1, 2, 3)]
    (
        grad_w_gate,
        grad_w_up,
        grad_w_query,
        grad_w_key,
        grad_w_value,
        grad_w_attn_out,
        grad_left,
        grad_right,
        grad_gate,
        grad_proj,
        gains,
        grad_w_down,
    ) = in_one(
        share_kernel,
        tuple(
            (shape, F32)
            for shape in (
                (64, D),
                (64, D),
                (64, 512),
                (64, half),
                (64, half),
                (64, 512),
                (16, 64),
                (16, 64),
                (64, 64),
                (64, 64),
                (64, 16),
                (64, D),
            )
        ),
        (*shares, down[0], hop(down[1], "ctx", 3)),
        "share",
        spots=(where,),
    )

    return (
        layer_out_all,
        stream_grad_all,
        grad_input_all,
        gains[:, 1] + gains[:, 11],
        gains[:8, 0],
        gains[8:16, 0],
        grad_w_query,
        grad_w_key,
        grad_w_value,
        grad_w_attn_out.T,
        gains[:, 8],
        grad_left.T,
        grad_right,
        gains[:, 9],
        gains[:, 10],
        grad_w_gate,
        grad_w_up,
        grad_w_down.T,
        gains[:, 2],
        grad_gate,
        grad_proj,
        gains[:, 3],
    )


def solution(mesh):
    rows, cols, tops = P("ctx", "wt"), P("wt", "ctx"), P("ctx")
    down, across = P(None, "wt"), P("wt", None)
    return jax.shard_map(
        local,
        mesh=mesh,
        in_specs=(
            P("ctx", None),
            P("ctx", "wt"),
            P("ctx", None),
            P(),
            P(),
            P(),
            P(),
            P(),
            down,
            down,
            down,
            across,
            P(),
            down,
            across,
            P(),
            P(),
            down,
            down,
            across,
            P(),
            down,
            across,
            P(),
        ),
        out_specs=(
            P("ctx", None),
            P("ctx", None),
            rows,
            tops,
            tops,
            tops,
            rows,
            rows,
            rows,
            cols,
            tops,
            rows,
            cols,
            tops,
            tops,
            rows,
            rows,
            cols,
            tops,
            rows,
            cols,
            tops,
        ),
        check_vma=False,
    )
```
